32 devices in a mesh: job: 2 (over y), blk: 4 (over z), cell: 2 (over x), col: 2 (over core).
Axes of the slice: x: 2, y: 2, z: 4, core: 2. Of those that a mesh axis runs over, the one named last changes fastest.
Arguments:
- p_blocks: bfloat16 [64, 4, 2, 128, 128], P(('job', 'blk', 'cell')), parts along dimension 0, may hold values from -0.1875 to 0.1875
- p_cols: int32 [64, 4, 2], P(('job', 'blk', 'cell')), parts along dimension 0, may hold values from 0 to 7
- l_blocks: bfloat16 [64, 4, 2, 128, 128], P(('job', 'blk', 'cell')), parts along dimension 0, may hold values from -0.1875 to 0.1875
- l_cols: int32 [64, 4, 2], P(('job', 'blk', 'cell')), parts along dimension 0, may hold values from 0 to 7
- charges: bfloat16 [24, 2, 8192], P('col', None, ('job', 'blk', 'cell')), parts along dimension 2, may hold values from -6 to 6
- currents: bfloat16 [24, 2, 8192], P('col', None, ('job', 'blk', 'cell')), parts along dimension 2, may hold values from -6 to 6
- omegas: float32 [24], P('col'), may hold values from 0.5 to 4
- resist: float32 [8192], P(('job', 'blk', 'cell')), parts along dimension 0, may hold values from 0.05 to 2
- branch_ends: int32 [2, 8192], P(None, ('job', 'blk', 'cell')), parts along dimension 1, may hold values from 0 to 1023
Outputs:
- cell_rows: float32 [24, 2, 8192], P('col', None, ('job', 'blk', 'cell')), parts along dimension 2
- panel_rows: float32 [24, 2, 8192], P('col', None, ('job', 'blk', 'cell')), parts along dimension 2
The draws below stay inside these ranges and needn't reach their ends.
There are 2 independent parts, one for each index of `job`. The reference program is written for one: setup_inputs(seed, part) draws one part's arguments, and reference() takes and returns one part's arrays. A program takes and returns all parts, laid end to end along the dimension named above; an argument that names none is the same for every part. Nothing has to cross between parts.
Inputs may be any that keep to these rules, and one draw needn't show every extreme that they name: `p_cols`: block columns are numbered within the region of 8 blocks that the slot's region index names; repeats may occur. `l_cols`: as for p_cols. `branch_ends`: panel numbers within the cell's own region of 1024 panels; a cell may leave and enter the same panel.
All inputs are finite; a program needn't handle non-finite values.
Results may differ from the reference program's by a relative error of at most 0.0059.
Values may be sent and summed in bfloat16 or wider, within the bound.
No kernel may reach another device: no remote copies, remote signals or barrier semaphores. Data moves between devices by JAX's collectives and lax.ppermute only.
A program may use at most 64 MiB of HBM per device.

```python
import math
import jax
import jax.numpy as jnp
from jax import lax

FREQS = 24
BS = 128
KP = 2
KL = 2
REG_BLOCKS = 8
REGION = 1024
NBLOCKS = 32
PANELS = 4096
CELLS = 4096
N_BLK = 4


def place_ends(values, own_key, smallest, largest):
    place = [jax.random.randint(jax.random.fold_in(own_key, axis), (), 0, length) for axis, length in enumerate(values.shape)]
    widest = values.shape.index(max(values.shape))
    beside = place[:widest] + [(place[widest] + 1) % values.shape[widest]] + place[widest + 1:]
    return values.at[tuple(place)].set(smallest).at[tuple(beside)].set(largest)


def levels(own_key, dims, split, low, largest):
    gain = 1.0
    for position, shards_of in split:
        draws = jax.random.uniform(jax.random.fold_in(jax.random.fold_in(own_key, 6), position), (shards_of,), jnp.float32, low / len(split), largest / len(split))
        gain = gain * jnp.repeat(jnp.exp(draws), dims[position] // shards_of).reshape((-1,) + (1,) * (len(dims) - 1 - position))
    return gain


def normal_values(stream_key, shape, deviation, bound, pieces=(), kind=jnp.bfloat16):
    level = levels(stream_key, shape, pieces, -0.22, 0.18) if pieces else 1.0
    array = jax.random.normal(stream_key, shape, jnp.float32) * deviation * level
    return jnp.minimum(jnp.maximum(array, -bound), bound).astype(kind)


def setup_inputs(seed: int = 0, part: int = 0) -> dict:
    seeds = jax.random.split(jax.random.key(seed), 10)
    own_keys = jax.random.split(jax.random.fold_in(seeds[9], part), 10)
    return {
        "p_blocks": normal_values(own_keys[0], (NBLOCKS, N_BLK, KP, BS, BS), (N_BLK * KP * BS) ** -0.5, 0.1875, ((0, 8),)),
        "p_cols": place_ends(jax.random.randint(own_keys[1], (NBLOCKS, N_BLK, KP), 0, REG_BLOCKS), jax.random.fold_in(own_keys[1], 1), 0, REG_BLOCKS - 1).astype(jnp.int32),
        "l_blocks": normal_values(own_keys[2], (NBLOCKS, N_BLK, KL, BS, BS), (N_BLK * KL * BS) ** -0.5, 0.1875, ((0, 8),)),
        "l_cols": place_ends(jax.random.randint(own_keys[3], (NBLOCKS, N_BLK, KL), 0, REG_BLOCKS), jax.random.fold_in(own_keys[3], 1), 0, REG_BLOCKS - 1).astype(jnp.int32),
        "charges": normal_values(own_keys[4], (FREQS, 2, PANELS), 1.0, 6.0, ((0, 2), (2, 8))),
        "currents": normal_values(own_keys[5], (FREQS, 2, CELLS), 1.0, 6.0, ((0, 2), (2, 8))),
        "omegas": jnp.clip(jnp.exp(math.log(4.0) - 2.0794415 * jax.random.uniform(seeds[6], (FREQS,), jnp.float32) ** levels(seeds[6], (FREQS,), ((0, 2),), -0.2, 0.2)), 0.5, 4.0),
        "resist": jnp.clip(jnp.exp(math.log(2.0) - 3.6888794 * jax.random.uniform(own_keys[7], (CELLS,), jnp.float32) ** levels(own_keys[7], (CELLS,), ((0, 8),), -0.2, 0.2)), 0.05, 2.0),
        "branch_ends": place_ends(jax.random.randint(own_keys[8], (2, CELLS), 0, REGION), jax.random.fold_in(own_keys[8], 1), 0, REGION - 1).astype(jnp.int32),
    }


def block_product(slabs, columns, vectors, reg_blocks):
    shifts = jnp.arange(N_BLK, dtype=jnp.int32)[:, None] * reg_blocks

    def one_row(pair):
        slab, index_set = pair
        picked_cols = (index_set.astype(jnp.int32) + shifts).astype(jnp.int32)
        picked = vectors[:, picked_cols].astype(jnp.float32)
        return jnp.einsum('skab,fskb->fa', slab.astype(jnp.float32), picked)

    result = lax.map(one_row, (slabs, columns))
    return jnp.transpose(result, (1, 0, 2)).reshape(result.shape[1], -1)


def reference(p_blocks, p_cols, l_blocks, l_cols, charges, currents, omegas, resist, branch_ends):
    col_rows = 2 * FREQS
    charge_mat = charges.reshape(col_rows, -1, BS)
    current_mat = currents.reshape(col_rows, -1, BS)
    potential = block_product(p_blocks, p_cols, charge_mat, REG_BLOCKS).astype(jnp.bfloat16)
    flux = block_product(l_blocks, l_cols, current_mat, REG_BLOCKS).reshape(FREQS, 2, -1)
    base = (jnp.arange(CELLS, dtype=jnp.int32) // REGION) * REGION
    source = (branch_ends[0] + base).astype(jnp.int32)
    target = (branch_ends[1] + base).astype(jnp.int32)
    drop = potential[:, source].astype(jnp.float32) - potential[:, target].astype(jnp.float32)
    drop = drop.reshape(FREQS, 2, -1)
    current_f = currents.astype(jnp.float32)
    scale = omegas[:, None]
    cell_re = resist * current_f[:, 0] - scale * flux[:, 1] + drop[:, 0]
    cell_im = resist * current_f[:, 1] + scale * flux[:, 0] + drop[:, 1]
    cell_rows = jnp.stack([cell_re, cell_im], axis=1)
    flat_cur = current_f.reshape(col_rows, -1).T
    outflow = jax.ops.segment_sum(flat_cur, source, PANELS) - jax.ops.segment_sum(flat_cur, target, PANELS)
    outflow = outflow.T.reshape(FREQS, 2, -1)
    charge_f = charges.astype(jnp.float32)
    panel_re = outflow[:, 0] - scale * charge_f[:, 1]
    panel_im = outflow[:, 1] + scale * charge_f[:, 0]
    panel_rows = jnp.stack([panel_re, panel_im], axis=1)
    return (cell_rows, panel_rows)
```

```python
import functools

import jax
import jax.numpy as jnp
from jax import lax
from jax.experimental import pallas as pl
from jax.experimental.pallas import tpu as pltpu
from jax.sharding import PartitionSpec as P

NT = (((1,), (1,)), ((), ()))
NN = (((1,), (0,)), ((), ()))
VMEM = pl.BlockSpec(memory_space=pltpu.VMEM)
SMEM = pl.BlockSpec(memory_space=pltpu.SMEM)


def halves(count):
    steps = []
    while count > 1:
        count //= 2
        steps.append(count)
    return steps


def swapped(array, axis, distance):
    return lax.ppermute(array, axis, [(i, i ^ distance) for i in range(lax.axis_size(axis))])


def block_kernel(offsets, cols_ref, place_ref, held_ref, slab_ref, out_ref):
    row_blocks, _, slots = slab_ref.shape[:3]
    own_region, own_cell = place_ref[0], place_ref[1]
    for row in range(row_blocks):
        total = jnp.zeros(out_ref.shape[1:], jnp.float32)
        for piece, offset in enumerate(offsets):
            region = own_region ^ offset
            for slot in range(slots):
                column = cols_ref[row, region, slot]
                side = lax.div(column, row_blocks) ^ own_cell
                block = held_ref[side, piece, lax.rem(column, row_blocks)]
                total += lax.dot_general(
                    block, slab_ref[row, region, slot], NT, preferred_element_type=jnp.float32
                )
        out_ref[row] = total.astype(out_ref.dtype)


def block_product(slab, cols, place, held, offsets, dtype):
    row_blocks, block_size = slab.shape[0], slab.shape[-1]
    rows = held.shape[-2]
    return pl.pallas_call(
        functools.partial(block_kernel, offsets),
        out_shape=jax.ShapeDtypeStruct((row_blocks, rows, block_size), dtype),
        in_specs=[SMEM, SMEM, VMEM, VMEM],
        out_specs=VMEM,
        compiler_params=pltpu.CompilerParams(vmem_limit_bytes=32 * 1024 * 1024),
        cost_estimate=pl.CostEstimate(
            flops=2 * rows * slab.size, bytes_accessed=2 * slab.size + 2 * held.size, transcendentals=0
        ),
    )(cols, place, held, slab)


def incidence_kernel(ends_ref, current_ref, matrix_ref, out_ref):
    blocks, _, block_size = out_ref.shape
    cells = ends_ref.shape[1]
    leaves, enters = ends_ref[0:1, :], ends_ref[1:2, :]
    current = current_ref[...]
    for block in range(blocks):
        panel = lax.broadcasted_iota(jnp.int32, (block_size, cells), 0) + block * block_size
        entry = (leaves == panel).astype(jnp.float32) - (enters == panel).astype(jnp.float32)
        entry = entry.astype(jnp.bfloat16)
        matrix_ref[block] = entry
        out_ref[block] = lax.dot_general(current, entry, NT, preferred_element_type=jnp.float32)


def incidence(ends, current, panels, block_size):
    cells = ends.shape[1]
    blocks = panels // block_size
    return pl.pallas_call(
        incidence_kernel,
        out_shape=(
            jax.ShapeDtypeStruct((blocks, block_size, cells), jnp.bfloat16),
            jax.ShapeDtypeStruct((blocks, current.shape[0], block_size), jnp.float32),
        ),
        in_specs=[VMEM, VMEM],
        out_specs=(VMEM, VMEM),
        compiler_params=pltpu.CompilerParams(vmem_limit_bytes=32 * 1024 * 1024),
        cost_estimate=pl.CostEstimate(
            flops=4 * panels * cells * current.shape[0], bytes_accessed=2 * panels * cells, transcendentals=0
        ),
    )(ends, current)


def drop_kernel(potential_ref, matrix_ref, base_ref, out_ref):
    total = base_ref[...]
    for block in range(matrix_ref.shape[0]):
        total += lax.dot_general(
            potential_ref[block], matrix_ref[block], NN, preferred_element_type=jnp.float32
        )
    out_ref[...] = total


def with_drop(potential, matrix, base):
    return pl.pallas_call(
        drop_kernel,
        out_shape=jax.ShapeDtypeStruct(base.shape, jnp.float32),
        in_specs=[VMEM, VMEM, VMEM],
        out_specs=VMEM,
        compiler_params=pltpu.CompilerParams(vmem_limit_bytes=32 * 1024 * 1024),
        cost_estimate=pl.CostEstimate(
            flops=2 * base.shape[0] * matrix.size, bytes_accessed=2 * matrix.size, transcendentals=0
        ),
    )(potential, matrix, base)


def turned(array):
    return jnp.stack([-array[:, 1], array[:, 0]], axis=1)


def per_device(p_blocks, p_cols, l_blocks, l_cols, charges, currents, omegas, resist, branch_ends):
    freq_count, _, share = charges.shape
    block_size = p_blocks.shape[-1]
    row_blocks = p_blocks.shape[0]
    rows = 2 * freq_count
    regions, cells = lax.axis_size("blk"), lax.axis_size("cell")
    region, cell = lax.axis_index("blk"), lax.axis_index("cell")
    place = jnp.stack([region, cell]).astype(jnp.int32)

    def blocked(array):
        return array.reshape(rows, row_blocks, block_size).transpose(1, 0, 2)

    def flat(array):
        return array.transpose(1, 0, 2).reshape(rows, share)

    held = jnp.stack([blocked(charges), blocked(turned(currents))])[:, None]
    offsets = [0]
    for step in halves(regions):
        held = jnp.concatenate([held, swapped(held, "blk", step)], axis=1)
        offsets = offsets + [o ^ step for o in offsets]

    local = ((branch_ends // share) ^ cell) * share + branch_ends % share
    matrix, outflow = incidence(local, currents.reshape(rows, share), cells * share, block_size)
    outflow = outflow.reshape(cells, row_blocks, rows, block_size)

    charge_all, current_all = held[0][None], held[1][None]
    for step in reversed(halves(cells)):
        charge_all = jnp.concatenate([charge_all, swapped(charge_all, "cell", step)], axis=0)
    potential = block_product(p_blocks, p_cols, place, charge_all, offsets, jnp.bfloat16)
    for step in reversed(halves(cells)):
        away = [o for o in range(cells) if o & step and not o & (step - 1)]
        kept = [o - step for o in away]
        sums = jnp.stack([outflow[o] for o in away]).astype(jnp.bfloat16)
        flat_current = current_all.reshape(-1, rows, block_size)
        message = jnp.concatenate([flat_current, sums.reshape(-1, rows, block_size)], axis=0)
        message = swapped(message, "cell", step)
        got = message[: flat_current.shape[0]].reshape(current_all.shape)
        more = message[flat_current.shape[0] :].reshape(sums.shape).astype(jnp.float32)
        current_all = jnp.concatenate([current_all, got], axis=0)
        for position, o in enumerate(kept):
            outflow = outflow.at[o].add(more[position])
    potential_all = potential[None]
    for step in reversed(halves(cells)):
        potential_all = jnp.concatenate([potential_all, swapped(potential_all, "cell", step)], axis=0)
    flux_turned = block_product(l_blocks, l_cols, place, current_all, offsets, jnp.float32)

    scale = jnp.repeat(omegas, 2)[:, None]
    base = resist * currents.reshape(rows, share).astype(jnp.float32) + scale * flat(flux_turned)
    cell_rows = with_drop(potential_all.reshape(-1, rows, block_size), matrix, base)
    panel_rows = flat(outflow[0]) + scale * turned(charges).reshape(rows, share).astype(jnp.float32)
    return (cell_rows.reshape(freq_count, 2, share), panel_rows.reshape(freq_count, 2, share))


def solution(mesh):
    placed = (
        P(("job", "blk", "cell"), None, None, None, None),
        P(("job", "blk", "cell"), None, None),
        P(("job", "blk", "cell"), None, None, None, None),
        P(("job", "blk", "cell"), None, None),
        P("col", None, ("job", "blk", "cell")),
        P("col", None, ("job", "blk", "cell")),
        P("col"),
        P(("job", "blk", "cell")),
        P(None, ("job", "blk", "cell")),
    )
    return jax.shard_map(
        per_device,
        mesh=mesh,
        in_specs=placed,
        out_specs=(P("col", None, ("job", "blk", "cell")), P("col", None, ("job", "blk", "cell"))),
        check_vma=False,
    )
```

```python
import functools

import jax
import jax.numpy as jnp
from jax import lax
from jax.experimental import pallas as pl
from jax.experimental.pallas import tpu as pltpu
from jax.sharding import PartitionSpec as P

NT = (((1,), (1,)), ((), ()))
NN = (((1,), (0,)), ((), ()))
VMEM = pl.BlockSpec(memory_space=pltpu.VMEM)
SMEM = pl.BlockSpec(memory_space=pltpu.SMEM)
ANY = pl.BlockSpec(memory_space=pl.ANY)
HBM = pl.BlockSpec(memory_space=pltpu.HBM)
JOIN = 10_000_000
SEND = 1_000
FIRST = 1_000
NEXT = 3_000_000
LAST = 8_000_000


def halves(count):
    steps = []
    while count > 1:
        count //= 2
        steps.append(count)
    return steps


def swapped(array, axis, distance):
    return lax.ppermute(array, axis, [(i, i ^ distance) for i in range(lax.axis_size(axis))])


def block_kernel(offsets, cols_ref, place_ref, held_ref, slab_ref, out_ref):
    row_blocks, _, slots = slab_ref.shape[:3]
    own_region, own_cell = place_ref[0], place_ref[1]
    for row in range(row_blocks):
        total = jnp.zeros(out_ref.shape[1:], jnp.float32)
        for piece, offset in enumerate(offsets):
            region = own_region ^ offset
            for slot in range(slots):
                column = cols_ref[row, region, slot]
                side = lax.div(column, row_blocks) ^ own_cell
                block = held_ref[side, piece, lax.rem(column, row_blocks)]
                total += lax.dot_general(
                    block, slab_ref[row, region, slot], NT, preferred_element_type=jnp.float32
                )
        out_ref[row] = total.astype(out_ref.dtype)


def block_product(slab, cols, place, held, offsets, dtype):
    row_blocks, block_size = slab.shape[0], slab.shape[-1]
    rows = held.shape[-2]
    return pl.pallas_call(
        functools.partial(block_kernel, offsets),
        out_shape=jax.ShapeDtypeStruct((row_blocks, rows, block_size), dtype),
        in_specs=[SMEM, SMEM, VMEM, VMEM],
        out_specs=VMEM,
        compiler_params=pltpu.CompilerParams(vmem_limit_bytes=32 * 1024 * 1024),
        cost_estimate=pl.CostEstimate(
            flops=2 * rows * slab.size, bytes_accessed=2 * slab.size + 2 * held.size, transcendentals=0
        ),
    )(cols, place, held, slab)


def incidence_kernel(ends_ref, current_ref, matrix_ref, out_ref):
    blocks, _, block_size = out_ref.shape
    cells = ends_ref.shape[1]
    leaves, enters = ends_ref[0:1, :], ends_ref[1:2, :]
    current = current_ref[...]
    for block in range(blocks):
        panel = lax.broadcasted_iota(jnp.int32, (block_size, cells), 0) + block * block_size
        entry = (leaves == panel).astype(jnp.float32) - (enters == panel).astype(jnp.float32)
        entry = entry.astype(jnp.bfloat16)
        matrix_ref[block] = entry
        out_ref[block] = lax.dot_general(current, entry, NT, preferred_element_type=jnp.float32)


def incidence(ends, current, panels, block_size):
    cells = ends.shape[1]
    blocks = panels // block_size
    return pl.pallas_call(
        incidence_kernel,
        out_shape=(
            jax.ShapeDtypeStruct((blocks, block_size, cells), jnp.bfloat16),
            jax.ShapeDtypeStruct((blocks, current.shape[0], block_size), jnp.float32),
        ),
        in_specs=[VMEM, VMEM],
        out_specs=(VMEM, VMEM),
        compiler_params=pltpu.CompilerParams(vmem_limit_bytes=32 * 1024 * 1024),
        cost_estimate=pl.CostEstimate(
            flops=4 * panels * cells * current.shape[0], bytes_accessed=2 * panels * cells, transcendentals=0
        ),
    )(ends, current)


def drop_kernel(potential_ref, matrix_ref, base_ref, out_ref):
    total = base_ref[...]
    for block in range(matrix_ref.shape[0]):
        total += lax.dot_general(
            potential_ref[block], matrix_ref[block], NN, preferred_element_type=jnp.float32
        )
    out_ref[...] = total


def with_drop(potential, matrix, base):
    return pl.pallas_call(
        drop_kernel,
        out_shape=jax.ShapeDtypeStruct(base.shape, jnp.float32),
        in_specs=[VMEM, VMEM, VMEM],
        out_specs=VMEM,
        compiler_params=pltpu.CompilerParams(vmem_limit_bytes=32 * 1024 * 1024),
        cost_estimate=pl.CostEstimate(
            flops=2 * base.shape[0] * matrix.size, bytes_accessed=2 * matrix.size, transcendentals=0
        ),
    )(potential, matrix, base)


def turned(array):
    return jnp.stack([-array[:, 1], array[:, 0]], axis=1)


def general_step(p_blocks, p_cols, l_blocks, l_cols, charges, currents, omegas, resist, branch_ends):
    freq_count, _, share = charges.shape
    block_size = p_blocks.shape[-1]
    row_blocks = p_blocks.shape[0]
    rows = 2 * freq_count
    regions, cells = lax.axis_size("blk"), lax.axis_size("cell")
    region, cell = lax.axis_index("blk"), lax.axis_index("cell")
    place = jnp.stack([region, cell]).astype(jnp.int32)

    def blocked(array):
        return array.reshape(rows, row_blocks, block_size).transpose(1, 0, 2)

    def flat(array):
        return array.transpose(1, 0, 2).reshape(rows, share)

    held = jnp.stack([blocked(charges), blocked(turned(currents))])[:, None]
    offsets = [0]
    for step in halves(regions):
        held = jnp.concatenate([held, swapped(held, "blk", step)], axis=1)
        offsets = offsets + [o ^ step for o in offsets]

    local = ((branch_ends // share) ^ cell) * share + branch_ends % share
    matrix, outflow = incidence(local, currents.reshape(rows, share), cells * share, block_size)
    outflow = outflow.reshape(cells, row_blocks, rows, block_size)

    charge_all, current_all = held[0][None], held[1][None]
    for step in reversed(halves(cells)):
        charge_all = jnp.concatenate([charge_all, swapped(charge_all, "cell", step)], axis=0)
    potential = block_product(p_blocks, p_cols, place, charge_all, offsets, jnp.bfloat16)
    for step in reversed(halves(cells)):
        away = [o for o in range(cells) if o & step and not o & (step - 1)]
        kept = [o - step for o in away]
        sums = jnp.stack([outflow[o] for o in away]).astype(jnp.bfloat16)
        flat_current = current_all.reshape(-1, rows, block_size)
        message = jnp.concatenate([flat_current, sums.reshape(-1, rows, block_size)], axis=0)
        message = swapped(message, "cell", step)
        got = message[: flat_current.shape[0]].reshape(current_all.shape)
        more = message[flat_current.shape[0] :].reshape(sums.shape).astype(jnp.float32)
        current_all = jnp.concatenate([current_all, got], axis=0)
        for position, o in enumerate(kept):
            outflow = outflow.at[o].add(more[position])
    potential_all = potential[None]
    for step in reversed(halves(cells)):
        potential_all = jnp.concatenate([potential_all, swapped(potential_all, "cell", step)], axis=0)
    flux_turned = block_product(l_blocks, l_cols, place, current_all, offsets, jnp.float32)

    scale = jnp.repeat(omegas, 2)[:, None]
    base = resist * currents.reshape(rows, share).astype(jnp.float32) + scale * flat(flux_turned)
    cell_rows = with_drop(potential_all.reshape(-1, rows, block_size), matrix, base)
    panel_rows = flat(outflow[0]) + scale * turned(charges).reshape(rows, share).astype(jnp.float32)
    return (cell_rows.reshape(freq_count, 2, share), panel_rows.reshape(freq_count, 2, share))


def back(regions, shift):
    return lax.rem(lax.axis_index("blk") + regions - shift, regions)


def turned_rows(array):
    rows = array.shape[0]
    odd = lax.broadcasted_iota(jnp.int32, array.shape, 0) & 1
    return jnp.where(odd == 0, -pltpu.roll(array, rows - 1, 0), pltpu.roll(array, 1, 0))


def row_scale(omega_ref, rows):
    shape = (rows, omega_ref.shape[1])
    same = lax.broadcasted_iota(jnp.int32, shape, 0) >> 1 == lax.broadcasted_iota(jnp.int32, shape, 1)
    return jnp.sum(jnp.where(same, omega_ref[...], 0.0), axis=1, keepdims=True)


def lanes(blocks):
    return jnp.concatenate(blocks, axis=1)


def pair_dot(held_ref, positions, slabs):
    return lax.dot_general(
        lanes([held_ref[position] for position in positions]), lanes(slabs), NT, preferred_element_type=jnp.float32
    )


def region_terms(shift, table_ref, held_ref, p_ref, l_ref, region, row):
    slots = range(p_ref.shape[2])
    return tuple(
        pair_dot(
            held_ref.at[kind],
            [table_ref[kind, shift, row, slot, 0] for slot in slots],
            [slab_ref[row, region, slot] for slot in slots],
        )
        for kind, slab_ref in enumerate((p_ref, l_ref))
    )


def first_kernel(
    regions, held_ref, p_ref, l_ref, p_cols_ref, l_cols_ref, ends_ref,
    table_ref, potential_ref, flux_ref, matrix_ref, outflow_ref, early_ref, numbers_ref,
):
    row_blocks, rows, block_size = potential_ref.shape
    slots = p_ref.shape[2]
    cell = lax.axis_index("cell")
    shape = table_ref.shape[2:]
    lane = lax.broadcasted_iota(jnp.int32, shape, 2)
    numbers = jnp.zeros(shape, jnp.float32)
    for kind, cols_ref in enumerate((p_cols_ref, l_cols_ref)):
        columns = cols_ref[...].astype(jnp.float32)
        place = lax.broadcasted_iota(jnp.int32, columns.shape, 2)
        for shift in range(regions):
            column = jnp.sum(jnp.where(place == back(regions, shift), columns, 0.0), axis=2, keepdims=True)
            column = jnp.broadcast_to(column, shape)
            other = jnp.where(column < row_blocks, column + row_blocks, column - row_blocks)
            table_ref[kind, shift] = jnp.where(cell == 0, column, other).astype(jnp.int32)
            if kind == 0:
                numbers = jnp.where(lane == shift, jnp.where(cell == 0, other, column), numbers)
    numbers_ref[...] = jnp.zeros_like(numbers_ref)
    for row in range(row_blocks):
        numbers_ref[row * slots : (row + 1) * slots, :] = numbers[row]
    early_ref[2 * row_blocks] = numbers_ref[...].astype(jnp.bfloat16)
    for row in range(row_blocks):
        potential, flux = region_terms(0, table_ref, held_ref, p_ref, l_ref, back(regions, 0), row)
        potential_ref[row], flux_ref[row] = potential, flux
        early_ref[row] = potential.astype(jnp.bfloat16)
    leaves, enters = ends_ref[0:1, :], ends_ref[1:2, :]
    current = lanes([held_ref[1, block] for block in range(row_blocks)])
    for block in range(2 * row_blocks):
        side, at = divmod(block, row_blocks)
        base = ((cell ^ side) * row_blocks + at) * block_size
        panel = lax.broadcasted_iota(jnp.int32, (block_size, ends_ref.shape[1]), 0) + base
        entry = (leaves == panel).astype(jnp.float32) - (enters == panel).astype(jnp.float32)
        entry = entry.astype(jnp.bfloat16)
        matrix_ref[block] = entry
        sums = lax.dot_general(current, entry, NT, preferred_element_type=jnp.float32)
        if side == 0:
            outflow_ref[at] = sums
        else:
            early_ref[block] = sums.astype(jnp.bfloat16)


def next_kernel(regions, shift, table_ref, held_ref, p_ref, l_ref, p_in_ref, f_in_ref, *refs):
    potential_ref, flux_ref = refs[-2:]
    region = back(regions, shift)
    for row in range(potential_ref.shape[0]):
        potential, flux = region_terms(shift, table_ref, held_ref, p_ref, l_ref, region, row)
        potential_ref[row], flux_ref[row] = p_in_ref[row] + potential, f_in_ref[row] + flux


def send_kernel(regions, p_ref, after_ref, out_ref, sems):
    del after_ref
    half = out_ref.shape[1]
    start = lax.axis_index("col") * half
    copies = [
        pltpu.make_async_copy(
            p_ref.at[pl.ds(start, half), back(regions, shift)], out_ref.at[shift - 1], sems.at[shift - 1]
        )
        for shift in range(1, regions)
    ]
    for copy in copies:
        copy.start()
    for copy in copies:
        copy.wait()


def join_kernel(own_ref, other_ref, out_ref):
    blocks = own_ref.shape[1]
    for kind in range(own_ref.shape[0]):
        out_ref[kind, :blocks] = own_ref[kind]
        out_ref[kind, blocks:] = other_ref[kind]


def store_rows(out_ref, columns, array):
    for freq in range(out_ref.shape[0]):
        out_ref[freq, :, columns] = array[2 * freq : 2 * freq + 2]


def last_kernel(regions, mine_ref, theirs_ref, *refs):
    piece_refs = refs[: regions - 1]
    (table_ref, p_ref, l_ref, p_in_ref, f_in_ref, early_ref, matrix_ref, held_ref, outflow_ref, omega_ref,
     resist_ref, cell_ref, panel_ref, other_ref, numbers_ref) = refs[regions - 1 :]
    row_blocks, rows, block_size = p_in_ref.shape
    half = row_blocks // 2
    slots = range(mine_ref.shape[2])
    core = lax.axis_index("col")
    numbers_ref[...] = early_ref[2 * row_blocks].astype(jnp.float32).astype(jnp.int32)
    potentials, fluxes = [], []
    for row in range(row_blocks):
        potential, flux = p_in_ref[row], f_in_ref[row]
        if regions > 1:
            shift = regions - 1
            terms = region_terms(shift, table_ref, piece_refs[-1], p_ref, l_ref, back(regions, shift), row)
            potential, flux = potential + terms[0], flux + terms[1]
        potentials.append(potential.astype(jnp.bfloat16))
        fluxes.append(flux)
    for part, slab_ref in enumerate((mine_ref, theirs_ref)):
        for position in range(half):
            row = (core ^ part) * half + position
            total = early_ref[row].astype(jnp.float32)
            for shift in range(1, regions):
                total += pair_dot(
                    piece_refs[shift - 1].at[0],
                    [numbers_ref[row * len(slots) + slot, shift] for slot in slots],
                    [slab_ref[shift - 1, position, slot] for slot in slots],
                )
            other_ref[row] = total.astype(jnp.bfloat16)
    matrix = matrix_ref[...].reshape(2, row_blocks * block_size, -1)
    drop = lax.dot_general(lanes(potentials), matrix[0], NN, preferred_element_type=jnp.float32)
    others = lanes([other_ref[row] for row in range(row_blocks)])
    drop += lax.dot_general(others, matrix[1], NN, preferred_element_type=jnp.float32)
    scale = row_scale(omega_ref, rows)
    for row in range(row_blocks):
        columns = slice(row * block_size, (row + 1) * block_size)
        current = held_ref[1, row].astype(jnp.float32)
        flux = scale * turned_rows(fluxes[row])
        store_rows(cell_ref, columns, resist_ref[:, columns] * current + flux + drop[:, columns])
        outflow = outflow_ref[row] + early_ref[row_blocks + row].astype(jnp.float32)
        charge = scale * turned_rows(held_ref[0, row].astype(jnp.float32))
        store_rows(panel_ref, columns, outflow + charge)


def kernel_call(body, out_shape, memories, cost, scratch=(), size=4_000_000):
    many = isinstance(out_shape, tuple)
    return pl.pallas_call(
        body,
        out_shape=out_shape,
        in_specs=[{"h": HBM, "v": VMEM, "a": ANY}[m] for m in memories],
        out_specs=tuple(VMEM for _ in out_shape) if many else VMEM,
        scratch_shapes=scratch,
        compiler_params=pltpu.CompilerParams(vmem_limit_bytes=16 * 1024 * 1024),
        cost_estimate=pl.CostEstimate(flops=cost * 1000, bytes_accessed=size, transcendentals=0),
    )


def paired_step(p_blocks, p_cols, l_blocks, l_cols, charges, currents, omegas, resist, branch_ends):
    freq_count, _, share = charges.shape
    block_size = p_blocks.shape[-1]
    row_blocks = p_blocks.shape[0]
    rows = 2 * freq_count
    regions = lax.axis_size("blk")

    def blocked(array):
        return array.reshape(rows, row_blocks, block_size).transpose(1, 0, 2)

    message = jnp.stack([blocked(charges), blocked(currents)])
    got = swapped(message, "cell", 1)
    held = kernel_call(
        join_kernel, jax.ShapeDtypeStruct((2, 2 * row_blocks, rows, block_size), jnp.bfloat16), "vv", JOIN
    )(message, got)

    half_shape = jax.ShapeDtypeStruct((regions - 1, row_blocks // 2) + p_blocks.shape[2:], jnp.bfloat16)
    sent = kernel_call(
        functools.partial(send_kernel, regions), half_shape, "ha", SEND, [pltpu.SemaphoreType.DMA((regions - 1,))]
    )(p_blocks, message)
    mine = swapped(sent, "cell", 1)
    theirs = swapped(mine, "col", 1)

    pieces = [
        lax.ppermute(held, "blk", [(i, (i + shift) % regions) for i in range(regions)])
        for shift in range(1, regions)
    ]

    slots = p_cols.shape[2]
    totals = jax.ShapeDtypeStruct((row_blocks, rows, block_size), jnp.float32)
    table, potential, flux, matrix, outflow, early = kernel_call(
        functools.partial(first_kernel, regions),
        (
            jax.ShapeDtypeStruct((2, regions, row_blocks, slots, block_size), jnp.int32),
            totals,
            totals,
            jax.ShapeDtypeStruct((2 * row_blocks, block_size, share), jnp.bfloat16),
            totals,
            jax.ShapeDtypeStruct((2 * row_blocks + 1, rows, block_size), jnp.bfloat16),
        ),
        "vvvvvv",
        FIRST,
        [pltpu.VMEM((rows, block_size), jnp.float32)],
    )(held, p_blocks, l_blocks, p_cols.transpose(0, 2, 1), l_cols.transpose(0, 2, 1), branch_ends)
    early = swapped(early, "cell", 1)
    for shift in range(1, regions - 1):
        potential, flux = kernel_call(
            functools.partial(next_kernel, regions, shift), (totals, totals), "vvvvvvv", NEXT
        )(table, pieces[shift - 1], p_blocks, l_blocks, potential, flux, matrix)

    result = jax.ShapeDtypeStruct(charges.shape, jnp.float32)
    return kernel_call(
        functools.partial(last_kernel, regions),
        (result, result),
        "v" * (12 + regions),
        LAST,
        [pltpu.VMEM((row_blocks, rows, block_size), jnp.bfloat16), pltpu.VMEM((rows, block_size), jnp.int32)],
    )(
        mine, theirs, *pieces, table, p_blocks, l_blocks, potential, flux, early, matrix, held, outflow,
        omegas[None], resist[None],
    )


def per_device(*args):
    row_blocks, regions = args[0].shape[:2]
    paired = lax.axis_size("cell") == 2 and lax.axis_size("col") == 2
    paired = paired and row_blocks % 2 == 0 and row_blocks * args[0].shape[2] <= 2 * args[4].shape[0]
    return (paired_step if paired else general_step)(*args)


def solution(mesh):
    placed = (
        P(("job", "blk", "cell"), None, None, None, None),
        P(("job", "blk", "cell"), None, None),
        P(("job", "blk", "cell"), None, None, None, None),
        P(("job", "blk", "cell"), None, None),
        P("col", None, ("job", "blk", "cell")),
        P("col", None, ("job", "blk", "cell")),
        P("col"),
        P(("job", "blk", "cell")),
        P(None, ("job", "blk", "cell")),
    )
    return jax.shard_map(
        per_device,
        mesh=mesh,
        in_specs=placed,
        out_specs=(P("col", None, ("job", "blk", "cell")), P("col", None, ("job", "blk", "cell"))),
        check_vma=False,
    )
```

```python
import functools

import jax
import jax.numpy as jnp
from jax import lax
from jax.experimental import pallas as pl
from jax.experimental.pallas import tpu as pltpu
from jax.sharding import PartitionSpec as P

NT = (((1,), (1,)), ((), ()))
NN = (((1,), (0,)), ((), ()))
VMEM = pl.BlockSpec(memory_space=pltpu.VMEM)
SMEM = pl.BlockSpec(memory_space=pltpu.SMEM)
ANY = pl.BlockSpec(memory_space=pl.ANY)
HBM = pl.BlockSpec(memory_space=pltpu.HBM)
MAIN = 6_000_000
STACK = 5_000_000
JOIN = 10_000_000
SEND = 1_000
FIRST = 1_000
NEXT = 3_000_000
LAST = 8_000_000


def halves(count):
    steps = []
    while count > 1:
        count //= 2
        steps.append(count)
    return steps


def swapped(array, axis, distance):
    return lax.ppermute(array, axis, [(i, i ^ distance) for i in range(lax.axis_size(axis))])


def block_kernel(offsets, cols_ref, place_ref, held_ref, slab_ref, out_ref):
    row_blocks, _, slots = slab_ref.shape[:3]
    own_region, own_cell = place_ref[0], place_ref[1]
    for row in range(row_blocks):
        total = jnp.zeros(out_ref.shape[1:], jnp.float32)
        for piece, offset in enumerate(offsets):
            region = own_region ^ offset
            for slot in range(slots):
                column = cols_ref[row, region, slot]
                side = lax.div(column, row_blocks) ^ own_cell
                block = held_ref[side, piece, lax.rem(column, row_blocks)]
                total += lax.dot_general(
                    block, slab_ref[row, region, slot], NT, preferred_element_type=jnp.float32
                )
        out_ref[row] = total.astype(out_ref.dtype)


def block_product(slab, cols, place, held, offsets, dtype):
    row_blocks, block_size = slab.shape[0], slab.shape[-1]
    rows = held.shape[-2]
    return pl.pallas_call(
        functools.partial(block_kernel, offsets),
        out_shape=jax.ShapeDtypeStruct((row_blocks, rows, block_size), dtype),
        in_specs=[SMEM, SMEM, VMEM, VMEM],
        out_specs=VMEM,
        compiler_params=pltpu.CompilerParams(vmem_limit_bytes=32 * 1024 * 1024),
        cost_estimate=pl.CostEstimate(
            flops=2 * rows * slab.size, bytes_accessed=2 * slab.size + 2 * held.size, transcendentals=0
        ),
    )(cols, place, held, slab)


def incidence_kernel(ends_ref, current_ref, matrix_ref, out_ref):
    blocks, _, block_size = out_ref.shape
    cells = ends_ref.shape[1]
    leaves, enters = ends_ref[0:1, :], ends_ref[1:2, :]
    current = current_ref[...]
    for block in range(blocks):
        panel = lax.broadcasted_iota(jnp.int32, (block_size, cells), 0) + block * block_size
        entry = (leaves == panel).astype(jnp.float32) - (enters == panel).astype(jnp.float32)
        entry = entry.astype(jnp.bfloat16)
        matrix_ref[block] = entry
        out_ref[block] = lax.dot_general(current, entry, NT, preferred_element_type=jnp.float32)


def incidence(ends, current, panels, block_size):
    cells = ends.shape[1]
    blocks = panels // block_size
    return pl.pallas_call(
        incidence_kernel,
        out_shape=(
            jax.ShapeDtypeStruct((blocks, block_size, cells), jnp.bfloat16),
            jax.ShapeDtypeStruct((blocks, current.shape[0], block_size), jnp.float32),
        ),
        in_specs=[VMEM, VMEM],
        out_specs=(VMEM, VMEM),
        compiler_params=pltpu.CompilerParams(vmem_limit_bytes=32 * 1024 * 1024),
        cost_estimate=pl.CostEstimate(
            flops=4 * panels * cells * current.shape[0], bytes_accessed=2 * panels * cells, transcendentals=0
        ),
    )(ends, current)


def drop_kernel(potential_ref, matrix_ref, base_ref, out_ref):
    total = base_ref[...]
    for block in range(matrix_ref.shape[0]):
        total += lax.dot_general(
            potential_ref[block], matrix_ref[block], NN, preferred_element_type=jnp.float32
        )
    out_ref[...] = total


def with_drop(potential, matrix, base):
    return pl.pallas_call(
        drop_kernel,
        out_shape=jax.ShapeDtypeStruct(base.shape, jnp.float32),
        in_specs=[VMEM, VMEM, VMEM],
        out_specs=VMEM,
        compiler_params=pltpu.CompilerParams(vmem_limit_bytes=32 * 1024 * 1024),
        cost_estimate=pl.CostEstimate(
            flops=2 * base.shape[0] * matrix.size, bytes_accessed=2 * matrix.size, transcendentals=0
        ),
    )(potential, matrix, base)


def turned(array):
    return jnp.stack([-array[:, 1], array[:, 0]], axis=1)


def general_step(p_blocks, p_cols, l_blocks, l_cols, charges, currents, omegas, resist, branch_ends):
    freq_count, _, share = charges.shape
    block_size = p_blocks.shape[-1]
    row_blocks = p_blocks.shape[0]
    rows = 2 * freq_count
    regions, cells = lax.axis_size("blk"), lax.axis_size("cell")
    region, cell = lax.axis_index("blk"), lax.axis_index("cell")
    place = jnp.stack([region, cell]).astype(jnp.int32)

    def blocked(array):
        return array.reshape(rows, row_blocks, block_size).transpose(1, 0, 2)

    def flat(array):
        return array.transpose(1, 0, 2).reshape(rows, share)

    held = jnp.stack([blocked(charges), blocked(turned(currents))])[:, None]
    offsets = [0]
    for step in halves(regions):
        held = jnp.concatenate([held, swapped(held, "blk", step)], axis=1)
        offsets = offsets + [o ^ step for o in offsets]

    local = ((branch_ends // share) ^ cell) * share + branch_ends % share
    matrix, outflow = incidence(local, currents.reshape(rows, share), cells * share, block_size)
    outflow = outflow.reshape(cells, row_blocks, rows, block_size)

    charge_all, current_all = held[0][None], held[1][None]
    for step in reversed(halves(cells)):
        charge_all = jnp.concatenate([charge_all, swapped(charge_all, "cell", step)], axis=0)
    potential = block_product(p_blocks, p_cols, place, charge_all, offsets, jnp.bfloat16)
    for step in reversed(halves(cells)):
        away = [o for o in range(cells) if o & step and not o & (step - 1)]
        kept = [o - step for o in away]
        sums = jnp.stack([outflow[o] for o in away]).astype(jnp.bfloat16)
        flat_current = current_all.reshape(-1, rows, block_size)
        message = jnp.concatenate([flat_current, sums.reshape(-1, rows, block_size)], axis=0)
        message = swapped(message, "cell", step)
        got = message[: flat_current.shape[0]].reshape(current_all.shape)
        more = message[flat_current.shape[0] :].reshape(sums.shape).astype(jnp.float32)
        current_all = jnp.concatenate([current_all, got], axis=0)
        for position, o in enumerate(kept):
            outflow = outflow.at[o].add(more[position])
    potential_all = potential[None]
    for step in reversed(halves(cells)):
        potential_all = jnp.concatenate([potential_all, swapped(potential_all, "cell", step)], axis=0)
    flux_turned = block_product(l_blocks, l_cols, place, current_all, offsets, jnp.float32)

    scale = jnp.repeat(omegas, 2)[:, None]
    base = resist * currents.reshape(rows, share).astype(jnp.float32) + scale * flat(flux_turned)
    cell_rows = with_drop(potential_all.reshape(-1, rows, block_size), matrix, base)
    panel_rows = flat(outflow[0]) + scale * turned(charges).reshape(rows, share).astype(jnp.float32)
    return (cell_rows.reshape(freq_count, 2, share), panel_rows.reshape(freq_count, 2, share))


def back(regions, shift):
    return lax.rem(lax.axis_index("blk") + regions - shift, regions)


def shift_order(regions):
    order = list(range(1, regions))
    return [2, 1, 3]


def turned_rows(array):
    rows = array.shape[0]
    odd = lax.broadcasted_iota(jnp.int32, array.shape, 0) & 1
    return jnp.where(odd == 0, -pltpu.roll(array, rows - 1, 0), pltpu.roll(array, 1, 0))


def row_scale(omega_ref, rows):
    shape = (rows, omega_ref.shape[1])
    same = lax.broadcasted_iota(jnp.int32, shape, 0) >> 1 == lax.broadcasted_iota(jnp.int32, shape, 1)
    return jnp.sum(jnp.where(same, omega_ref[...], 0.0), axis=1, keepdims=True)


def lanes(blocks):
    return jnp.concatenate(blocks, axis=1)


def pair_dot(held_ref, positions, slabs):
    return lax.dot_general(
        lanes([held_ref[position] for position in positions]), lanes(slabs), NT, preferred_element_type=jnp.float32
    )


def region_terms(shift, table_ref, held_ref, p_ref, l_ref, region, row):
    slots = range(p_ref.shape[2])
    return tuple(
        pair_dot(
            held_ref.at[kind],
            [table_ref[kind, shift, row, slot, 0] for slot in slots],
            [slab_ref[row, region, slot] for slot in slots],
        )
        for kind, slab_ref in enumerate((p_ref, l_ref))
    )


def outflow_kernel(message_ref, ends_ref, matrix_ref, outflow_ref, away_ref):
    row_blocks, _, block_size = outflow_ref.shape
    leaves, enters = ends_ref[0:1, :], ends_ref[1:2, :]
    current = lanes([message_ref[1, block] for block in range(row_blocks)])
    for block in range(2 * row_blocks):
        side, at = divmod(block, row_blocks)
        base = ((lax.axis_index("cell") ^ side) * row_blocks + at) * block_size
        panel = lax.broadcasted_iota(jnp.int32, (block_size, ends_ref.shape[1]), 0) + base
        entry = (leaves == panel).astype(jnp.float32) - (enters == panel).astype(jnp.float32)
        entry = entry.astype(jnp.bfloat16)
        matrix_ref[block] = entry
        sums = lax.dot_general(current, entry, NT, preferred_element_type=jnp.float32)
        if side == 0:
            outflow_ref[at] = sums
        else:
            away_ref[at] = sums.astype(jnp.bfloat16)


def first_kernel(
    regions, held_ref, p_ref, l_ref, p_cols_ref, l_cols_ref, omega_ref, resist_ref, away_ref,
    factor_ref, table_ref, potential_ref, flux_ref, early_ref, numbers_ref,
):
    row_blocks, rows, block_size = potential_ref.shape
    slots = p_ref.shape[2]
    cell = lax.axis_index("cell")
    shape = table_ref.shape[2:]
    lane = lax.broadcasted_iota(jnp.int32, shape, 2)
    numbers = jnp.zeros(shape, jnp.float32)
    for kind, cols_ref in enumerate((p_cols_ref, l_cols_ref)):
        columns = cols_ref[...].astype(jnp.float32)
        place = lax.broadcasted_iota(jnp.int32, columns.shape, 2)
        for shift in range(regions):
            column = jnp.sum(jnp.where(place == back(regions, shift), columns, 0.0), axis=2, keepdims=True)
            column = jnp.broadcast_to(column, shape)
            other = jnp.where(column < row_blocks, column + row_blocks, column - row_blocks)
            table_ref[kind, shift] = jnp.where(cell == 0, column, other).astype(jnp.int32)
            if kind == 0:
                numbers = jnp.where(lane == shift, jnp.where(cell == 0, other, column), numbers)
    numbers_ref[...] = jnp.zeros_like(numbers_ref)
    for row in range(row_blocks):
        numbers_ref[row * slots : (row + 1) * slots, :] = numbers[row]
    early_ref[2 * row_blocks] = numbers_ref[...].astype(jnp.bfloat16)
    early_ref[row_blocks : 2 * row_blocks] = away_ref[...]
    for row in range(row_blocks):
        potential, flux = region_terms(0, table_ref, held_ref, p_ref, l_ref, back(regions, 0), row)
        potential_ref[row], flux_ref[row] = potential, flux
        early_ref[row] = potential.astype(jnp.bfloat16)
    factor_ref[0] = jnp.broadcast_to(row_scale(omega_ref, rows), (rows, block_size))
    for row in range(row_blocks):
        columns = slice(row * block_size, (row + 1) * block_size)
        factor_ref[1 + row] = jnp.broadcast_to(resist_ref[:, columns], (rows, block_size))


def next_kernel(regions, shift, table_ref, held_ref, p_ref, l_ref, p_in_ref, f_in_ref, *refs):
    potential_ref, flux_ref = refs[-2:]
    region = back(regions, shift)
    for row in range(potential_ref.shape[0]):
        potential, flux = region_terms(shift, table_ref, held_ref, p_ref, l_ref, region, row)
        potential_ref[row], flux_ref[row] = p_in_ref[row] + potential, f_in_ref[row] + flux


def stack_kernel(charge_ref, current_ref, out_ref):
    out_ref[0] = charge_ref[...]
    out_ref[1] = current_ref[...]


def send_kernel(regions, p_ref, after_ref, out_ref):
    del after_ref
    half = out_ref.shape[1]
    for at, shift in enumerate(shift_order(regions)):
        for row in range(half):
            out_ref[at, row] = p_ref[lax.axis_index("col") * half + row, back(regions, shift)]


def join_kernel(own_ref, other_ref, out_ref):
    blocks = own_ref.shape[1]
    for kind in range(own_ref.shape[0]):
        out_ref[kind, :blocks] = own_ref[kind]
        out_ref[kind, blocks:] = other_ref[kind]


def store_rows(out_ref, columns, array):
    for freq in range(out_ref.shape[0]):
        out_ref[freq, :, columns] = array[2 * freq : 2 * freq + 2]


def other_rows(order, part, slab_ref, numbers_ref, early_ref, piece_refs, other_ref):
    half, slots = slab_ref.shape[1:3]
    for position in range(half):
        row = (lax.axis_index("col") ^ part) * half + position
        total = early_ref[row].astype(jnp.float32)
        for at, shift in enumerate(order):
            total += pair_dot(
                piece_refs[at].at[0],
                [numbers_ref[row * slots + slot, shift] for slot in range(slots)],
                [slab_ref[at, position, slot] for slot in range(slots)],
            )
        other_ref[row] = total.astype(jnp.bfloat16)


def other_drop(part, half, other_ref, matrix_ref):
    start = (lax.axis_index("col") ^ part) * half
    rows = lanes([other_ref[start + position] for position in range(half)])
    matrix = matrix_ref[pl.ds(2 * half + start, half)].reshape(rows.shape[1], -1)
    return lax.dot_general(rows, matrix, NN, preferred_element_type=jnp.float32)


def main_kernel(regions, *refs):
    order = shift_order(regions)
    piece_refs = refs[: regions - 1]
    (mine_ref, table_ref, p_ref, l_ref, p_in_ref, f_in_ref, early_ref, matrix_ref, held_ref, factor_ref,
     out_ref, numbers_ref, other_ref) = refs[regions - 1 :]
    row_blocks, _, block_size = p_in_ref.shape
    numbers_ref[...] = early_ref[2 * row_blocks].astype(jnp.float32).astype(jnp.int32)
    potentials, fluxes = [], []
    for row in range(row_blocks):
        potential, flux = p_in_ref[row], f_in_ref[row]
        for shift, piece_ref in list(zip(order, piece_refs))[1:]:
            terms = region_terms(shift, table_ref, piece_ref, p_ref, l_ref, back(regions, shift), row)
            potential, flux = potential + terms[0], flux + terms[1]
        potentials.append(potential.astype(jnp.bfloat16))
        fluxes.append(flux)
    other_rows(order, 0, mine_ref, numbers_ref, early_ref, piece_refs, other_ref)
    matrix = matrix_ref[:row_blocks].reshape(row_blocks * block_size, -1)
    drop = lax.dot_general(lanes(potentials), matrix, NN, preferred_element_type=jnp.float32)
    drop += other_drop(0, row_blocks // 2, other_ref, matrix_ref)
    for row in range(row_blocks):
        columns = slice(row * block_size, (row + 1) * block_size)
        current = held_ref[1, row].astype(jnp.float32)
        flux = factor_ref[0] * turned_rows(fluxes[row])
        out_ref[:, columns] = factor_ref[1 + row] * current + flux + drop[:, columns]


def last_kernel(regions, *refs):
    piece_refs = refs[: regions - 1]
    (theirs_ref, numbers_ref, begun_ref, early_ref, matrix_ref, held_ref, outflow_ref, factor_ref,
     cell_ref, panel_ref, other_ref) = refs[regions - 1 :]
    row_blocks, _, block_size = outflow_ref.shape
    other_rows(shift_order(regions), 1, theirs_ref, numbers_ref, early_ref, piece_refs, other_ref)
    total = begun_ref[...] + other_drop(1, row_blocks // 2, other_ref, matrix_ref)
    for row in range(row_blocks):
        columns = slice(row * block_size, (row + 1) * block_size)
        store_rows(cell_ref, columns, total[:, columns])
        outflow = outflow_ref[row] + early_ref[row_blocks + row].astype(jnp.float32)
        charge = factor_ref[0] * turned_rows(held_ref[0, row].astype(jnp.float32))
        store_rows(panel_ref, columns, outflow + charge)


def kernel_call(body, out_shape, memories, cost, scratch=(), size=4_000_000):
    many = isinstance(out_shape, tuple)
    return pl.pallas_call(
        body,
        out_shape=out_shape,
        in_specs=[{"h": HBM, "v": VMEM, "a": ANY}[m] for m in memories],
        out_specs=tuple(VMEM for _ in out_shape) if many else VMEM,
        scratch_shapes=scratch,
        compiler_params=pltpu.CompilerParams(vmem_limit_bytes=16 * 1024 * 1024),
        cost_estimate=pl.CostEstimate(flops=cost * 1000, bytes_accessed=size, transcendentals=0),
    )


def paired_step(p_blocks, p_cols, l_blocks, l_cols, charges, currents, omegas, resist, branch_ends):
    freq_count, _, share = charges.shape
    block_size = p_blocks.shape[-1]
    row_blocks = p_blocks.shape[0]
    rows = 2 * freq_count
    regions = lax.axis_size("blk")
    order = shift_order(regions)

    def blocked(array):
        return array.reshape(rows, row_blocks, block_size).transpose(1, 0, 2)

    message = kernel_call(
        stack_kernel, jax.ShapeDtypeStruct((2, row_blocks, rows, block_size), jnp.bfloat16), "vv", STACK
    )(blocked(charges), blocked(currents))
    held = kernel_call(
        join_kernel, jax.ShapeDtypeStruct((2, 2 * row_blocks, rows, block_size), jnp.bfloat16), "vv", JOIN
    )(message, swapped(message, "cell", 1))

    totals = jax.ShapeDtypeStruct((row_blocks, rows, block_size), jnp.float32)
    matrix, outflow, away = kernel_call(
        outflow_kernel,
        (
            jax.ShapeDtypeStruct((2 * row_blocks, block_size, share), jnp.bfloat16),
            totals,
            jax.ShapeDtypeStruct((row_blocks, rows, block_size), jnp.bfloat16),
        ),
        "vv",
        SEND,
    )(message, branch_ends)
    half_shape = jax.ShapeDtypeStruct((regions - 1, row_blocks // 2) + p_blocks.shape[2:], jnp.bfloat16)
    sent = kernel_call(functools.partial(send_kernel, regions), half_shape, "va", SEND)(p_blocks, outflow)
    mine = swapped(sent, "cell", 1)
    theirs = swapped(mine, "col", 1)

    pieces = [
        lax.ppermute(held, "blk", [(i, (i + shift) % regions) for i in range(regions)])
        for shift in order
    ]

    slots = p_cols.shape[2]
    factors, table, potential, flux, early = kernel_call(
        functools.partial(first_kernel, regions),
        (
            jax.ShapeDtypeStruct((1 + row_blocks, rows, block_size), jnp.float32),
            jax.ShapeDtypeStruct((2, regions, row_blocks, slots, block_size), jnp.int32),
            totals,
            totals,
            jax.ShapeDtypeStruct((2 * row_blocks + 1, rows, block_size), jnp.bfloat16),
        ),
        "vvvvvvvv",
        FIRST,
        [pltpu.VMEM((rows, block_size), jnp.float32)],
    )(held, p_blocks, l_blocks, p_cols.transpose(0, 2, 1), l_cols.transpose(0, 2, 1), omegas[None], resist[None], away)
    early = swapped(early, "cell", 1)
    for shift, piece in list(zip(order, pieces))[:1]:
        potential, flux = kernel_call(
            functools.partial(next_kernel, regions, shift), (totals, totals), "vvvvvvv", NEXT
        )(table, piece, p_blocks, l_blocks, potential, flux, matrix)

    numbers_shape = jax.ShapeDtypeStruct((rows, block_size), jnp.int32)
    other_scratch = pltpu.VMEM((row_blocks, rows, block_size), jnp.bfloat16)
    begun, numbers = kernel_call(
        functools.partial(main_kernel, regions),
        (jax.ShapeDtypeStruct((rows, share), jnp.float32), numbers_shape),
        "v" * (9 + regions),
        MAIN,
        [other_scratch],
    )(*pieces, mine, table, p_blocks, l_blocks, potential, flux, early, matrix, held, factors)
    result = jax.ShapeDtypeStruct(charges.shape, jnp.float32)
    return kernel_call(
        functools.partial(last_kernel, regions), (result, result), "v" * (7 + regions), LAST, [other_scratch]
    )(*pieces, theirs, numbers, begun, early, matrix, held, outflow, factors)


def per_device(*args):
    row_blocks, regions = args[0].shape[:2]
    paired = lax.axis_size("cell") == 2 and lax.axis_size("col") == 2
    paired = paired and row_blocks % 2 == 0 and row_blocks * args[0].shape[2] <= 2 * args[4].shape[0]
    return (paired_step if paired else general_step)(*args)


def solution(mesh):
    placed = (
        P(("job", "blk", "cell"), None, None, None, None),
        P(("job", "blk", "cell"), None, None),
        P(("job", "blk", "cell"), None, None, None, None),
        P(("job", "blk", "cell"), None, None),
        P("col", None, ("job", "blk", "cell")),
        P("col", None, ("job", "blk", "cell")),
        P("col"),
        P(("job", "blk", "cell")),
        P(None, ("job", "blk", "cell")),
    )
    return jax.shard_map(
        per_device,
        mesh=mesh,
        in_specs=placed,
        out_specs=(P("col", None, ("job", "blk", "cell")), P("col", None, ("job", "blk", "cell"))),
        check_vma=False,
    )
```

```python
import functools

import jax
import jax.numpy as jnp
from jax import lax
from jax.experimental import pallas as pl
from jax.experimental.pallas import tpu as pltpu
from jax.sharding import PartitionSpec as P

NT = (((1,), (1,)), ((), ()))
NN = (((1,), (0,)), ((), ()))
VMEM = pl.BlockSpec(memory_space=pltpu.VMEM)
SMEM = pl.BlockSpec(memory_space=pltpu.SMEM)
ANY = pl.BlockSpec(memory_space=pl.ANY)
HBM = pl.BlockSpec(memory_space=pltpu.HBM)
MAIN = 3_000_000
STACK = 5_000_000
JOIN = 10_000_000
SEND = 1_000
FIRST = 1_000
NEXT = 3_000_000
LAST = 8_000_000


def halves(count):
    steps = []
    while count > 1:
        count //= 2
        steps.append(count)
    return steps


def swapped(array, axis, distance):
    return lax.ppermute(array, axis, [(i, i ^ distance) for i in range(lax.axis_size(axis))])


def block_kernel(offsets, cols_ref, place_ref, held_ref, slab_ref, out_ref):
    row_blocks, _, slots = slab_ref.shape[:3]
    own_region, own_cell = place_ref[0], place_ref[1]
    for row in range(row_blocks):
        total = jnp.zeros(out_ref.shape[1:], jnp.float32)
        for piece, offset in enumerate(offsets):
            region = own_region ^ offset
            for slot in range(slots):
                column = cols_ref[row, region, slot]
                side = lax.div(column, row_blocks) ^ own_cell
                block = held_ref[side, piece, lax.rem(column, row_blocks)]
                total += lax.dot_general(
                    block, slab_ref[row, region, slot], NT, preferred_element_type=jnp.float32
                )
        out_ref[row] = total.astype(out_ref.dtype)


def block_product(slab, cols, place, held, offsets, dtype):
    row_blocks, block_size = slab.shape[0], slab.shape[-1]
    rows = held.shape[-2]
    return pl.pallas_call(
        functools.partial(block_kernel, offsets),
        out_shape=jax.ShapeDtypeStruct((row_blocks, rows, block_size), dtype),
        in_specs=[SMEM, SMEM, VMEM, VMEM],
        out_specs=VMEM,
        compiler_params=pltpu.CompilerParams(vmem_limit_bytes=32 * 1024 * 1024),
        cost_estimate=pl.CostEstimate(
            flops=2 * rows * slab.size, bytes_accessed=2 * slab.size + 2 * held.size, transcendentals=0
        ),
    )(cols, place, held, slab)


def incidence_kernel(ends_ref, current_ref, matrix_ref, out_ref):
    blocks, _, block_size = out_ref.shape
    cells = ends_ref.shape[1]
    leaves, enters = ends_ref[0:1, :], ends_ref[1:2, :]
    current = current_ref[...]
    for block in range(blocks):
        panel = lax.broadcasted_iota(jnp.int32, (block_size, cells), 0) + block * block_size
        entry = (leaves == panel).astype(jnp.float32) - (enters == panel).astype(jnp.float32)
        entry = entry.astype(jnp.bfloat16)
        matrix_ref[block] = entry
        out_ref[block] = lax.dot_general(current, entry, NT, preferred_element_type=jnp.float32)


def incidence(ends, current, panels, block_size):
    cells = ends.shape[1]
    blocks = panels // block_size
    return pl.pallas_call(
        incidence_kernel,
        out_shape=(
            jax.ShapeDtypeStruct((blocks, block_size, cells), jnp.bfloat16),
            jax.ShapeDtypeStruct((blocks, current.shape[0], block_size), jnp.float32),
        ),
        in_specs=[VMEM, VMEM],
        out_specs=(VMEM, VMEM),
        compiler_params=pltpu.CompilerParams(vmem_limit_bytes=32 * 1024 * 1024),
        cost_estimate=pl.CostEstimate(
            flops=4 * panels * cells * current.shape[0], bytes_accessed=2 * panels * cells, transcendentals=0
        ),
    )(ends, current)


def drop_kernel(potential_ref, matrix_ref, base_ref, out_ref):
    total = base_ref[...]
    for block in range(matrix_ref.shape[0]):
        total += lax.dot_general(
            potential_ref[block], matrix_ref[block], NN, preferred_element_type=jnp.float32
        )
    out_ref[...] = total


def with_drop(potential, matrix, base):
    return pl.pallas_call(
        drop_kernel,
        out_shape=jax.ShapeDtypeStruct(base.shape, jnp.float32),
        in_specs=[VMEM, VMEM, VMEM],
        out_specs=VMEM,
        compiler_params=pltpu.CompilerParams(vmem_limit_bytes=32 * 1024 * 1024),
        cost_estimate=pl.CostEstimate(
            flops=2 * base.shape[0] * matrix.size, bytes_accessed=2 * matrix.size, transcendentals=0
        ),
    )(potential, matrix, base)


def turned(array):
    return jnp.stack([-array[:, 1], array[:, 0]], axis=1)


def general_step(p_blocks, p_cols, l_blocks, l_cols, charges, currents, omegas, resist, branch_ends):
    freq_count, _, share = charges.shape
    block_size = p_blocks.shape[-1]
    row_blocks = p_blocks.shape[0]
    rows = 2 * freq_count
    regions, cells = lax.axis_size("blk"), lax.axis_size("cell")
    region, cell = lax.axis_index("blk"), lax.axis_index("cell")
    place = jnp.stack([region, cell]).astype(jnp.int32)

    def blocked(array):
        return array.reshape(rows, row_blocks, block_size).transpose(1, 0, 2)

    def flat(array):
        return array.transpose(1, 0, 2).reshape(rows, share)

    held = jnp.stack([blocked(charges), blocked(turned(currents))])[:, None]
    offsets = [0]
    for step in halves(regions):
        held = jnp.concatenate([held, swapped(held, "blk", step)], axis=1)
        offsets = offsets + [o ^ step for o in offsets]

    local = ((branch_ends // share) ^ cell) * share + branch_ends % share
    matrix, outflow = incidence(local, currents.reshape(rows, share), cells * share, block_size)
    outflow = outflow.reshape(cells, row_blocks, rows, block_size)

    charge_all, current_all = held[0][None], held[1][None]
    for step in reversed(halves(cells)):
        charge_all = jnp.concatenate([charge_all, swapped(charge_all, "cell", step)], axis=0)
    potential = block_product(p_blocks, p_cols, place, charge_all, offsets, jnp.bfloat16)
    for step in reversed(halves(cells)):
        away = [o for o in range(cells) if o & step and not o & (step - 1)]
        kept = [o - step for o in away]
        sums = jnp.stack([outflow[o] for o in away]).astype(jnp.bfloat16)
        flat_current = current_all.reshape(-1, rows, block_size)
        message = jnp.concatenate([flat_current, sums.reshape(-1, rows, block_size)], axis=0)
        message = swapped(message, "cell", step)
        got = message[: flat_current.shape[0]].reshape(current_all.shape)
        more = message[flat_current.shape[0] :].reshape(sums.shape).astype(jnp.float32)
        current_all = jnp.concatenate([current_all, got], axis=0)
        for position, o in enumerate(kept):
            outflow = outflow.at[o].add(more[position])
    potential_all = potential[None]
    for step in reversed(halves(cells)):
        potential_all = jnp.concatenate([potential_all, swapped(potential_all, "cell", step)], axis=0)
    flux_turned = block_product(l_blocks, l_cols, place, current_all, offsets, jnp.float32)

    scale = jnp.repeat(omegas, 2)[:, None]
    base = resist * currents.reshape(rows, share).astype(jnp.float32) + scale * flat(flux_turned)
    cell_rows = with_drop(potential_all.reshape(-1, rows, block_size), matrix, base)
    panel_rows = flat(outflow[0]) + scale * turned(charges).reshape(rows, share).astype(jnp.float32)
    return (cell_rows.reshape(freq_count, 2, share), panel_rows.reshape(freq_count, 2, share))


def back(regions, move):
    own = lax.axis_index("blk")
    if move == 0:
        return own
    targets = region_moves(regions)[move - 1]
    return sum(jnp.where(own == target, source, 0) for source, target in enumerate(targets))


def region_moves(regions):
    if regions == 4:
        return [[2, 3, 0, 1], [1, 0, 3, 2], [3, 2, 1, 0]]
    return [[(place + shift) % regions for place in range(regions)] for shift in range(1, regions)]


def shift_order(regions):
    return list(range(1, regions))


def turned_rows(array):
    rows = array.shape[0]
    odd = lax.broadcasted_iota(jnp.int32, array.shape, 0) & 1
    return jnp.where(odd == 0, -pltpu.roll(array, rows - 1, 0), pltpu.roll(array, 1, 0))


def row_scale(omega_ref, rows):
    shape = (rows, omega_ref.shape[1])
    same = lax.broadcasted_iota(jnp.int32, shape, 0) >> 1 == lax.broadcasted_iota(jnp.int32, shape, 1)
    return jnp.sum(jnp.where(same, omega_ref[...], 0.0), axis=1, keepdims=True)


def lanes(blocks):
    return jnp.concatenate(blocks, axis=1)


def pair_dot(held_ref, positions, slabs):
    return lax.dot_general(
        lanes([held_ref[position] for position in positions]), lanes(slabs), NT, preferred_element_type=jnp.float32
    )


def region_terms(shift, table_ref, held_ref, p_ref, l_ref, region, row):
    slots = range(p_ref.shape[2])
    return tuple(
        pair_dot(
            held_ref.at[kind],
            [table_ref[kind, shift, row, slot, 0] for slot in slots],
            [slab_ref[row, region, slot] for slot in slots],
        )
        for kind, slab_ref in enumerate((p_ref, l_ref))
    )


def outflow_kernel(message_ref, ends_ref, matrix_ref, outflow_ref, away_ref):
    row_blocks, _, block_size = outflow_ref.shape
    leaves, enters = ends_ref[0:1, :], ends_ref[1:2, :]
    current = lanes([message_ref[1, block] for block in range(row_blocks)])
    for block in range(2 * row_blocks):
        side, at = divmod(block, row_blocks)
        base = ((lax.axis_index("cell") ^ side) * row_blocks + at) * block_size
        panel = lax.broadcasted_iota(jnp.int32, (block_size, ends_ref.shape[1]), 0) + base
        entry = (leaves == panel).astype(jnp.float32) - (enters == panel).astype(jnp.float32)
        entry = entry.astype(jnp.bfloat16)
        matrix_ref[block] = entry
        sums = lax.dot_general(current, entry, NT, preferred_element_type=jnp.float32)
        if side == 0:
            outflow_ref[at] = sums
        else:
            away_ref[at] = sums.astype(jnp.bfloat16)


def first_kernel(
    regions, held_ref, p_ref, l_ref, p_cols_ref, l_cols_ref, omega_ref, resist_ref, away_ref,
    factor_ref, table_ref, potential_ref, flux_ref, early_ref, numbers_ref,
):
    row_blocks, rows, block_size = potential_ref.shape
    slots = p_ref.shape[2]
    cell = lax.axis_index("cell")
    shape = table_ref.shape[2:]
    lane = lax.broadcasted_iota(jnp.int32, shape, 2)
    numbers = jnp.zeros(shape, jnp.float32)
    for kind, cols_ref in enumerate((p_cols_ref, l_cols_ref)):
        columns = cols_ref[...].astype(jnp.float32)
        place = lax.broadcasted_iota(jnp.int32, columns.shape, 2)
        for shift in range(regions):
            column = jnp.sum(jnp.where(place == back(regions, shift), columns, 0.0), axis=2, keepdims=True)
            column = jnp.broadcast_to(column, shape)
            other = jnp.where(column < row_blocks, column + row_blocks, column - row_blocks)
            table_ref[kind, shift] = jnp.where(cell == 0, column, other).astype(jnp.int32)
            if kind == 0:
                numbers = jnp.where(lane == shift, jnp.where(cell == 0, other, column), numbers)
    numbers_ref[...] = jnp.zeros_like(numbers_ref)
    for row in range(row_blocks):
        numbers_ref[row * slots : (row + 1) * slots, :] = numbers[row]
    early_ref[2 * row_blocks] = numbers_ref[...].astype(jnp.bfloat16)
    early_ref[row_blocks : 2 * row_blocks] = away_ref[...]
    for row in range(row_blocks):
        potential, flux = region_terms(0, table_ref, held_ref, p_ref, l_ref, back(regions, 0), row)
        potential_ref[row], flux_ref[row] = potential, flux
        early_ref[row] = potential.astype(jnp.bfloat16)
    factor_ref[0] = jnp.broadcast_to(row_scale(omega_ref, rows), (rows, block_size))
    for row in range(row_blocks):
        columns = slice(row * block_size, (row + 1) * block_size)
        factor_ref[1 + row] = jnp.broadcast_to(resist_ref[:, columns], (rows, block_size))


def next_kernel(regions, shift, table_ref, held_ref, p_ref, l_ref, p_in_ref, f_in_ref, *refs):
    potential_ref, flux_ref = refs[-2:]
    region = back(regions, shift)
    for row in range(potential_ref.shape[0]):
        potential, flux = region_terms(shift, table_ref, held_ref, p_ref, l_ref, region, row)
        potential_ref[row], flux_ref[row] = p_in_ref[row] + potential, f_in_ref[row] + flux


def stack_kernel(charge_ref, current_ref, out_ref):
    out_ref[0] = charge_ref[...]
    out_ref[1] = current_ref[...]


def send_kernel(regions, p_ref, after_ref, out_ref):
    del after_ref
    half = out_ref.shape[1]
    for at, shift in enumerate(shift_order(regions)):
        for row in range(half):
            out_ref[at, row] = p_ref[lax.axis_index("col") * half + row, back(regions, shift)]


def join_kernel(own_ref, other_ref, out_ref):
    blocks = own_ref.shape[1]
    for kind in range(own_ref.shape[0]):
        out_ref[kind, :blocks] = own_ref[kind]
        out_ref[kind, blocks:] = other_ref[kind]


def store_rows(out_ref, columns, array):
    for freq in range(out_ref.shape[0]):
        out_ref[freq, :, columns] = array[2 * freq : 2 * freq + 2]


def other_rows(order, part, slab_ref, numbers_ref, early_ref, piece_refs, other_ref):
    half, slots = slab_ref.shape[1:3]
    for position in range(half):
        row = (lax.axis_index("col") ^ part) * half + position
        total = early_ref[row].astype(jnp.float32)
        for at, shift in enumerate(order):
            total += pair_dot(
                piece_refs[at].at[0],
                [numbers_ref[row * slots + slot, shift] for slot in range(slots)],
                [slab_ref[at, position, slot] for slot in range(slots)],
            )
        other_ref[row] = total.astype(jnp.bfloat16)


def other_drop(part, half, other_ref, matrix_ref):
    start = (lax.axis_index("col") ^ part) * half
    rows = lanes([other_ref[start + position] for position in range(half)])
    matrix = matrix_ref[pl.ds(2 * half + start, half)].reshape(rows.shape[1], -1)
    return lax.dot_general(rows, matrix, NN, preferred_element_type=jnp.float32)


def main_kernel(regions, *refs):
    order = shift_order(regions)
    piece_refs = refs[: regions - 1]
    (mine_ref, table_ref, p_ref, l_ref, p_in_ref, f_in_ref, early_ref, matrix_ref, held_ref, factor_ref,
     out_ref, numbers_ref, other_ref) = refs[regions - 1 :]
    row_blocks, _, block_size = p_in_ref.shape
    numbers_ref[...] = early_ref[2 * row_blocks].astype(jnp.float32).astype(jnp.int32)
    potentials, fluxes = [], []
    for row in range(row_blocks):
        potential, flux = p_in_ref[row], f_in_ref[row]
        for shift, piece_ref in list(zip(order, piece_refs))[1:]:
            terms = region_terms(shift, table_ref, piece_ref, p_ref, l_ref, back(regions, shift), row)
            potential, flux = potential + terms[0], flux + terms[1]
        potentials.append(potential.astype(jnp.bfloat16))
        fluxes.append(flux)
    other_rows(order, 0, mine_ref, numbers_ref, early_ref, piece_refs, other_ref)
    matrix = matrix_ref[:row_blocks].reshape(row_blocks * block_size, -1)
    drop = lax.dot_general(lanes(potentials), matrix, NN, preferred_element_type=jnp.float32)
    drop += other_drop(0, row_blocks // 2, other_ref, matrix_ref)
    for row in range(row_blocks):
        columns = slice(row * block_size, (row + 1) * block_size)
        current = held_ref[1, row].astype(jnp.float32)
        flux = factor_ref[0] * turned_rows(fluxes[row])
        out_ref[:, columns] = factor_ref[1 + row] * current + flux + drop[:, columns]


def last_kernel(regions, *refs):
    piece_refs = refs[: regions - 1]
    (theirs_ref, numbers_ref, begun_ref, early_ref, matrix_ref, held_ref, outflow_ref, factor_ref,
     cell_ref, panel_ref, other_ref) = refs[regions - 1 :]
    row_blocks, _, block_size = outflow_ref.shape
    other_rows(shift_order(regions), 1, theirs_ref, numbers_ref, early_ref, piece_refs, other_ref)
    total = begun_ref[...] + other_drop(1, row_blocks // 2, other_ref, matrix_ref)
    for row in range(row_blocks):
        columns = slice(row * block_size, (row + 1) * block_size)
        store_rows(cell_ref, columns, total[:, columns])
        outflow = outflow_ref[row] + early_ref[row_blocks + row].astype(jnp.float32)
        charge = factor_ref[0] * turned_rows(held_ref[0, row].astype(jnp.float32))
        store_rows(panel_ref, columns, outflow + charge)


def kernel_call(body, out_shape, memories, cost, scratch=(), size=4_000_000):
    many = isinstance(out_shape, tuple)
    return pl.pallas_call(
        body,
        out_shape=out_shape,
        in_specs=[{"h": HBM, "v": VMEM, "a": ANY}[m] for m in memories],
        out_specs=tuple(VMEM for _ in out_shape) if many else VMEM,
        scratch_shapes=scratch,
        compiler_params=pltpu.CompilerParams(vmem_limit_bytes=16 * 1024 * 1024),
        cost_estimate=pl.CostEstimate(flops=cost * 1000, bytes_accessed=size, transcendentals=0),
    )


def paired_step(p_blocks, p_cols, l_blocks, l_cols, charges, currents, omegas, resist, branch_ends):
    freq_count, _, share = charges.shape
    block_size = p_blocks.shape[-1]
    row_blocks = p_blocks.shape[0]
    rows = 2 * freq_count
    regions = lax.axis_size("blk")
    order = shift_order(regions)

    def blocked(array):
        return array.reshape(rows, row_blocks, block_size).transpose(1, 0, 2)

    message = kernel_call(
        stack_kernel, jax.ShapeDtypeStruct((2, row_blocks, rows, block_size), jnp.bfloat16), "vv", STACK
    )(blocked(charges), blocked(currents))
    held = kernel_call(
        join_kernel, jax.ShapeDtypeStruct((2, 2 * row_blocks, rows, block_size), jnp.bfloat16), "vv", JOIN
    )(message, swapped(message, "cell", 1))

    totals = jax.ShapeDtypeStruct((row_blocks, rows, block_size), jnp.float32)
    matrix, outflow, away = kernel_call(
        outflow_kernel,
        (
            jax.ShapeDtypeStruct((2 * row_blocks, block_size, share), jnp.bfloat16),
            totals,
            jax.ShapeDtypeStruct((row_blocks, rows, block_size), jnp.bfloat16),
        ),
        "vv",
        SEND,
    )(message, branch_ends)
    half_shape = jax.ShapeDtypeStruct((regions - 1, row_blocks // 2) + p_blocks.shape[2:], jnp.bfloat16)
    sent = kernel_call(functools.partial(send_kernel, regions), half_shape, "va", SEND)(p_blocks, outflow)
    mine = swapped(sent, "cell", 1)
    theirs = swapped(mine, "col", 1)

    pieces = [
        lax.ppermute(held, "blk", list(enumerate(targets))) for targets in region_moves(regions)
    ]

    slots = p_cols.shape[2]
    factors, table, potential, flux, early = kernel_call(
        functools.partial(first_kernel, regions),
        (
            jax.ShapeDtypeStruct((1 + row_blocks, rows, block_size), jnp.float32),
            jax.ShapeDtypeStruct((2, regions, row_blocks, slots, block_size), jnp.int32),
            totals,
            totals,
            jax.ShapeDtypeStruct((2 * row_blocks + 1, rows, block_size), jnp.bfloat16),
        ),
        "vvvvvvvv",
        FIRST,
        [pltpu.VMEM((rows, block_size), jnp.float32)],
    )(held, p_blocks, l_blocks, p_cols.transpose(0, 2, 1), l_cols.transpose(0, 2, 1), omegas[None], resist[None], away)
    early = swapped(early, "cell", 1)
    for shift, piece in list(zip(order, pieces))[:1]:
        potential, flux = kernel_call(
            functools.partial(next_kernel, regions, shift), (totals, totals), "vvvvvvv", NEXT
        )(table, piece, p_blocks, l_blocks, potential, flux, matrix)

    numbers_shape = jax.ShapeDtypeStruct((rows, block_size), jnp.int32)
    other_scratch = pltpu.VMEM((row_blocks, rows, block_size), jnp.bfloat16)
    begun, numbers = kernel_call(
        functools.partial(main_kernel, regions),
        (jax.ShapeDtypeStruct((rows, share), jnp.float32), numbers_shape),
        "v" * (9 + regions),
        MAIN,
        [other_scratch],
    )(*pieces, mine, table, p_blocks, l_blocks, potential, flux, early, matrix, held, factors)
    result = jax.ShapeDtypeStruct(charges.shape, jnp.float32)
    return kernel_call(
        functools.partial(last_kernel, regions), (result, result), "v" * (7 + regions), LAST, [other_scratch]
    )(*pieces, theirs, numbers, begun, early, matrix, held, outflow, factors)


def per_device(*args):
    row_blocks, regions = args[0].shape[:2]
    paired = lax.axis_size("cell") == 2 and lax.axis_size("col") == 2
    paired = paired and row_blocks % 2 == 0 and row_blocks * args[0].shape[2] <= 2 * args[4].shape[0]
    return (paired_step if paired else general_step)(*args)


def solution(mesh):
    placed = (
        P(("job", "blk", "cell"), None, None, None, None),
        P(("job", "blk", "cell"), None, None),
        P(("job", "blk", "cell"), None, None, None, None),
        P(("job", "blk", "cell"), None, None),
        P("col", None, ("job", "blk", "cell")),
        P("col", None, ("job", "blk", "cell")),
        P("col"),
        P(("job", "blk", "cell")),
        P(None, ("job", "blk", "cell")),
    )
    return jax.shard_map(
        per_device,
        mesh=mesh,
        in_specs=placed,
        out_specs=(P("col", None, ("job", "blk", "cell")), P("col", None, ("job", "blk", "cell"))),
        check_vma=False,
    )
```

```python
import functools

import jax
import jax.numpy as jnp
from jax import lax
from jax.experimental import pallas as pl
from jax.experimental.pallas import tpu as pltpu
from jax.sharding import PartitionSpec as P

NT = (((1,), (1,)), ((), ()))
NN = (((1,), (0,)), ((), ()))
VMEM = pl.BlockSpec(memory_space=pltpu.VMEM)
SMEM = pl.BlockSpec(memory_space=pltpu.SMEM)
ANY = pl.BlockSpec(memory_space=pl.ANY)
STACK = 5_000_000
JOIN = 10_000_000
SMALL = 1_000
NEXT = 3_000_000
MAIN = 3_000_000
LAST = 8_000_000


def halves(count):
    steps = []
    while count > 1:
        count //= 2
        steps.append(count)
    return steps


def swapped(array, axis, distance):
    return lax.ppermute(array, axis, [(i, i ^ distance) for i in range(lax.axis_size(axis))])


def block_kernel(offsets, cols_ref, place_ref, held_ref, slab_ref, out_ref):
    row_blocks, _, slots = slab_ref.shape[:3]
    own_region, own_cell = place_ref[0], place_ref[1]
    for row in range(row_blocks):
        total = jnp.zeros(out_ref.shape[1:], jnp.float32)
        for piece, offset in enumerate(offsets):
            region = own_region ^ offset
            for slot in range(slots):
                column = cols_ref[row, region, slot]
                side = lax.div(column, row_blocks) ^ own_cell
                block = held_ref[side, piece, lax.rem(column, row_blocks)]
                total += lax.dot_general(
                    block, slab_ref[row, region, slot], NT, preferred_element_type=jnp.float32
                )
        out_ref[row] = total.astype(out_ref.dtype)


def block_product(slab, cols, place, held, offsets, dtype):
    row_blocks, block_size = slab.shape[0], slab.shape[-1]
    rows = held.shape[-2]
    return pl.pallas_call(
        functools.partial(block_kernel, offsets),
        out_shape=jax.ShapeDtypeStruct((row_blocks, rows, block_size), dtype),
        in_specs=[SMEM, SMEM, VMEM, VMEM],
        out_specs=VMEM,
        compiler_params=pltpu.CompilerParams(vmem_limit_bytes=32 * 1024 * 1024),
        cost_estimate=pl.CostEstimate(
            flops=2 * rows * slab.size, bytes_accessed=2 * slab.size + 2 * held.size, transcendentals=0
        ),
    )(cols, place, held, slab)


def incidence_kernel(ends_ref, current_ref, matrix_ref, out_ref):
    blocks, _, block_size = out_ref.shape
    cells = ends_ref.shape[1]
    leaves, enters = ends_ref[0:1, :], ends_ref[1:2, :]
    current = current_ref[...]
    for block in range(blocks):
        panel = lax.broadcasted_iota(jnp.int32, (block_size, cells), 0) + block * block_size
        entry = (leaves == panel).astype(jnp.float32) - (enters == panel).astype(jnp.float32)
        entry = entry.astype(jnp.bfloat16)
        matrix_ref[block] = entry
        out_ref[block] = lax.dot_general(current, entry, NT, preferred_element_type=jnp.float32)


def incidence(ends, current, panels, block_size):
    cells = ends.shape[1]
    blocks = panels // block_size
    return pl.pallas_call(
        incidence_kernel,
        out_shape=(
            jax.ShapeDtypeStruct((blocks, block_size, cells), jnp.bfloat16),
            jax.ShapeDtypeStruct((blocks, current.shape[0], block_size), jnp.float32),
        ),
        in_specs=[VMEM, VMEM],
        out_specs=(VMEM, VMEM),
        compiler_params=pltpu.CompilerParams(vmem_limit_bytes=32 * 1024 * 1024),
        cost_estimate=pl.CostEstimate(
            flops=4 * panels * cells * current.shape[0], bytes_accessed=2 * panels * cells, transcendentals=0
        ),
    )(ends, current)


def drop_kernel(potential_ref, matrix_ref, base_ref, out_ref):
    total = base_ref[...]
    for block in range(matrix_ref.shape[0]):
        total += lax.dot_general(
            potential_ref[block], matrix_ref[block], NN, preferred_element_type=jnp.float32
        )
    out_ref[...] = total


def with_drop(potential, matrix, base):
    return pl.pallas_call(
        drop_kernel,
        out_shape=jax.ShapeDtypeStruct(base.shape, jnp.float32),
        in_specs=[VMEM, VMEM, VMEM],
        out_specs=VMEM,
        compiler_params=pltpu.CompilerParams(vmem_limit_bytes=32 * 1024 * 1024),
        cost_estimate=pl.CostEstimate(
            flops=2 * base.shape[0] * matrix.size, bytes_accessed=2 * matrix.size, transcendentals=0
        ),
    )(potential, matrix, base)


def turned(array):
    return jnp.stack([-array[:, 1], array[:, 0]], axis=1)


def general_step(p_blocks, p_cols, l_blocks, l_cols, charges, currents, omegas, resist, branch_ends):
    freq_count, _, share = charges.shape
    block_size = p_blocks.shape[-1]
    row_blocks = p_blocks.shape[0]
    rows = 2 * freq_count
    regions, cells = lax.axis_size("blk"), lax.axis_size("cell")
    region, cell = lax.axis_index("blk"), lax.axis_index("cell")
    place = jnp.stack([region, cell]).astype(jnp.int32)

    def blocked(array):
        return array.reshape(rows, row_blocks, block_size).transpose(1, 0, 2)

    def flat(array):
        return array.transpose(1, 0, 2).reshape(rows, share)

    held = jnp.stack([blocked(charges), blocked(turned(currents))])[:, None]
    offsets = [0]
    for step in halves(regions):
        held = jnp.concatenate([held, swapped(held, "blk", step)], axis=1)
        offsets = offsets + [o ^ step for o in offsets]

    local = ((branch_ends // share) ^ cell) * share + branch_ends % share
    matrix, outflow = incidence(local, currents.reshape(rows, share), cells * share, block_size)
    outflow = outflow.reshape(cells, row_blocks, rows, block_size)

    charge_all, current_all = held[0][None], held[1][None]
    for step in reversed(halves(cells)):
        charge_all = jnp.concatenate([charge_all, swapped(charge_all, "cell", step)], axis=0)
    potential = block_product(p_blocks, p_cols, place, charge_all, offsets, jnp.bfloat16)
    for step in reversed(halves(cells)):
        away = [o for o in range(cells) if o & step and not o & (step - 1)]
        kept = [o - step for o in away]
        sums = jnp.stack([outflow[o] for o in away]).astype(jnp.bfloat16)
        flat_current = current_all.reshape(-1, rows, block_size)
        message = jnp.concatenate([flat_current, sums.reshape(-1, rows, block_size)], axis=0)
        message = swapped(message, "cell", step)
        got = message[: flat_current.shape[0]].reshape(current_all.shape)
        more = message[flat_current.shape[0] :].reshape(sums.shape).astype(jnp.float32)
        current_all = jnp.concatenate([current_all, got], axis=0)
        for position, o in enumerate(kept):
            outflow = outflow.at[o].add(more[position])
    potential_all = potential[None]
    for step in reversed(halves(cells)):
        potential_all = jnp.concatenate([potential_all, swapped(potential_all, "cell", step)], axis=0)
    flux_turned = block_product(l_blocks, l_cols, place, current_all, offsets, jnp.float32)

    scale = jnp.repeat(omegas, 2)[:, None]
    base = resist * currents.reshape(rows, share).astype(jnp.float32) + scale * flat(flux_turned)
    cell_rows = with_drop(potential_all.reshape(-1, rows, block_size), matrix, base)
    panel_rows = flat(outflow[0]) + scale * turned(charges).reshape(rows, share).astype(jnp.float32)
    return (cell_rows.reshape(freq_count, 2, share), panel_rows.reshape(freq_count, 2, share))


def back(regions, move):
    own = lax.axis_index("blk")
    if move == 0:
        return own
    targets = region_moves(regions)[move - 1]
    return sum(jnp.where(own == target, source, 0) for source, target in enumerate(targets))


def region_moves(regions):
    if regions == 4:
        return [[3, 2, 0, 1], [1, 0, 3, 2], [2, 3, 1, 0]]
    return [[(place + shift) % regions for place in range(regions)] for shift in range(1, regions)]


def turned_rows(array):
    rows = array.shape[0]
    odd = lax.broadcasted_iota(jnp.int32, array.shape, 0) & 1
    return jnp.where(odd == 0, -pltpu.roll(array, rows - 1, 0), pltpu.roll(array, 1, 0))


def row_scale(omega_ref, rows):
    shape = (rows, omega_ref.shape[1])
    same = lax.broadcasted_iota(jnp.int32, shape, 0) >> 1 == lax.broadcasted_iota(jnp.int32, shape, 1)
    return jnp.sum(jnp.where(same, omega_ref[...], 0.0), axis=1, keepdims=True)


def lanes(blocks):
    return jnp.concatenate(blocks, axis=1)


def pair_dot(held_ref, positions, slabs):
    return lax.dot_general(
        lanes([held_ref[position] for position in positions]), lanes(slabs), NT, preferred_element_type=jnp.float32
    )


def region_terms(regions, move, table_ref, held_ref, p_ref, l_ref, row):
    region = back(regions, move)
    slots = range(p_ref.shape[2])
    return tuple(
        pair_dot(
            held_ref.at[kind],
            [table_ref[kind, move, row, slot, 0] for slot in slots],
            [slab_ref[row, region, slot] for slot in slots],
        )
        for kind, slab_ref in enumerate((p_ref, l_ref))
    )


def outflow_terms(side, ends_ref, current_ref, matrix_ref, store):
    row_blocks, block_size = matrix_ref.shape[:2]
    leaves, enters = ends_ref[0:1, :], ends_ref[1:2, :]
    current = lanes([current_ref[1, block] for block in range(row_blocks)])
    for block in range(row_blocks):
        base = ((lax.axis_index("cell") ^ side) * row_blocks + block) * block_size
        panel = lax.broadcasted_iota(jnp.int32, (block_size, ends_ref.shape[1]), 0) + base
        entry = (leaves == panel).astype(jnp.float32) - (enters == panel).astype(jnp.float32)
        entry = entry.astype(jnp.bfloat16)
        matrix_ref[block] = entry
        store(block, lax.dot_general(current, entry, NT, preferred_element_type=jnp.float32))


def outflow_kernel(message_ref, ends_ref, matrix_ref, outflow_ref):
    def store(block, sums):
        outflow_ref[block] = sums

    outflow_terms(0, ends_ref, message_ref, matrix_ref, store)


def first_kernel(
    regions, held_ref, p_ref, l_ref, p_cols_ref, l_cols_ref, omega_ref, resist_ref, ends_ref,
    factor_ref, table_ref, potential_ref, flux_ref, early_ref, matrix_ref, numbers_ref,
):
    row_blocks, rows, block_size = potential_ref.shape
    slots = p_ref.shape[2]
    cell = lax.axis_index("cell")
    shape = table_ref.shape[2:]
    lane = lax.broadcasted_iota(jnp.int32, shape, 2)
    numbers = jnp.zeros(shape, jnp.float32)
    for kind, cols_ref in enumerate((p_cols_ref, l_cols_ref)):
        columns = cols_ref[...].astype(jnp.float32)
        place = lax.broadcasted_iota(jnp.int32, columns.shape, 2)
        for move in range(regions):
            column = jnp.sum(jnp.where(place == back(regions, move), columns, 0.0), axis=2, keepdims=True)
            column = jnp.broadcast_to(column, shape)
            other = jnp.where(column < row_blocks, column + row_blocks, column - row_blocks)
            table_ref[kind, move] = jnp.where(cell == 0, column, other).astype(jnp.int32)
            if kind == 0:
                numbers = jnp.where(lane == move, jnp.where(cell == 0, other, column), numbers)
    numbers_ref[...] = jnp.zeros_like(numbers_ref)
    for row in range(row_blocks):
        numbers_ref[row * slots : (row + 1) * slots, :] = numbers[row]
    early_ref[2 * row_blocks] = numbers_ref[...].astype(jnp.bfloat16)

    def store(block, sums):
        early_ref[row_blocks + block] = sums.astype(jnp.bfloat16)

    outflow_terms(1, ends_ref, held_ref, matrix_ref, store)
    for row in range(row_blocks):
        potential, flux = region_terms(regions, 0, table_ref, held_ref, p_ref, l_ref, row)
        potential_ref[row], flux_ref[row] = potential, flux
        early_ref[row] = potential.astype(jnp.bfloat16)
    factor_ref[0] = jnp.broadcast_to(row_scale(omega_ref, rows), (rows, block_size))
    for row in range(row_blocks):
        columns = slice(row * block_size, (row + 1) * block_size)
        factor_ref[1 + row] = jnp.broadcast_to(resist_ref[:, columns], (rows, block_size))


def next_kernel(
    regions, move, table_ref, held_ref, p_ref, l_ref, p_in_ref, f_in_ref, matrix_ref, potential_ref, flux_ref
):
    del matrix_ref
    for row in range(potential_ref.shape[0]):
        potential, flux = region_terms(regions, move, table_ref, held_ref, p_ref, l_ref, row)
        potential_ref[row], flux_ref[row] = p_in_ref[row] + potential, f_in_ref[row] + flux


def stack_kernel(charge_ref, current_ref, out_ref):
    out_ref[0] = charge_ref[...]
    out_ref[1] = current_ref[...]


def send_kernel(regions, p_ref, after_ref, out_ref):
    del after_ref
    half = out_ref.shape[1]
    for move in range(1, regions):
        for row in range(half):
            out_ref[move - 1, row] = p_ref[lax.axis_index("col") * half + row, back(regions, move)]


def join_kernel(own_ref, other_ref, out_ref):
    blocks = own_ref.shape[1]
    for kind in range(own_ref.shape[0]):
        out_ref[kind, :blocks] = own_ref[kind]
        out_ref[kind, blocks:] = other_ref[kind]


def store_rows(out_ref, columns, array):
    for freq in range(out_ref.shape[0]):
        out_ref[freq, :, columns] = array[2 * freq : 2 * freq + 2]


def other_rows(part, slab_ref, numbers_ref, early_ref, piece_refs, other_ref):
    half, slots = slab_ref.shape[1:3]
    for position in range(half):
        row = (lax.axis_index("col") ^ part) * half + position
        total = early_ref[row].astype(jnp.float32)
        for at, piece_ref in enumerate(piece_refs):
            total += pair_dot(
                piece_ref.at[0],
                [numbers_ref[row * slots + slot, at + 1] for slot in range(slots)],
                [slab_ref[at, position, slot] for slot in range(slots)],
            )
        other_ref[row] = total.astype(jnp.bfloat16)


def other_drop(part, half, other_ref, matrix_ref):
    start = (lax.axis_index("col") ^ part) * half
    rows = lanes([other_ref[start + position] for position in range(half)])
    matrix = matrix_ref[pl.ds(start, half)].reshape(rows.shape[1], -1)
    return lax.dot_general(rows, matrix, NN, preferred_element_type=jnp.float32)


def main_kernel(regions, *refs):
    piece_refs = refs[: regions - 1]
    (mine_ref, table_ref, p_ref, l_ref, p_in_ref, f_in_ref, early_ref, matrix_ref, other_matrix_ref, held_ref,
     factor_ref, out_ref, numbers_ref, other_ref) = refs[regions - 1 :]
    row_blocks, _, block_size = p_in_ref.shape
    numbers_ref[...] = early_ref[2 * row_blocks].astype(jnp.float32).astype(jnp.int32)
    potentials, fluxes = [], []
    for row in range(row_blocks):
        potential, flux = region_terms(regions, regions - 1, table_ref, piece_refs[-1], p_ref, l_ref, row)
        potentials.append((p_in_ref[row] + potential).astype(jnp.bfloat16))
        fluxes.append(f_in_ref[row] + flux)
    other_rows(0, mine_ref, numbers_ref, early_ref, piece_refs, other_ref)
    matrix = matrix_ref[...].reshape(row_blocks * block_size, -1)
    drop = lax.dot_general(lanes(potentials), matrix, NN, preferred_element_type=jnp.float32)
    drop += other_drop(0, row_blocks // 2, other_ref, other_matrix_ref)
    for row in range(row_blocks):
        columns = slice(row * block_size, (row + 1) * block_size)
        current = held_ref[1, row].astype(jnp.float32)
        flux = factor_ref[0] * turned_rows(fluxes[row])
        out_ref[:, columns] = factor_ref[1 + row] * current + flux + drop[:, columns]


def last_kernel(regions, *refs):
    piece_refs = refs[: regions - 1]
    (theirs_ref, numbers_ref, begun_ref, early_ref, matrix_ref, held_ref, outflow_ref, factor_ref,
     cell_ref, panel_ref, other_ref) = refs[regions - 1 :]
    row_blocks, _, block_size = outflow_ref.shape
    other_rows(1, theirs_ref, numbers_ref, early_ref, piece_refs, other_ref)
    total = begun_ref[...] + other_drop(1, row_blocks // 2, other_ref, matrix_ref)
    for row in range(row_blocks):
        columns = slice(row * block_size, (row + 1) * block_size)
        store_rows(cell_ref, columns, total[:, columns])
        outflow = outflow_ref[row] + early_ref[row_blocks + row].astype(jnp.float32)
        charge = factor_ref[0] * turned_rows(held_ref[0, row].astype(jnp.float32))
        store_rows(panel_ref, columns, outflow + charge)


def kernel_call(body, out_shape, memories, weight, scratch=()):
    many = isinstance(out_shape, tuple)
    return pl.pallas_call(
        body,
        out_shape=out_shape,
        in_specs=[{"v": VMEM, "a": ANY}[m] for m in memories],
        out_specs=tuple(VMEM for _ in out_shape) if many else VMEM,
        scratch_shapes=scratch,
        compiler_params=pltpu.CompilerParams(vmem_limit_bytes=16 * 1024 * 1024),
        cost_estimate=pl.CostEstimate(flops=weight * 1000, bytes_accessed=4_000_000, transcendentals=0),
    )


def paired_step(p_blocks, p_cols, l_blocks, l_cols, charges, currents, omegas, resist, branch_ends):
    freq_count, _, share = charges.shape
    block_size = p_blocks.shape[-1]
    row_blocks = p_blocks.shape[0]
    rows = 2 * freq_count
    regions = lax.axis_size("blk")

    def blocked(array):
        return array.reshape(rows, row_blocks, block_size).transpose(1, 0, 2)

    message = kernel_call(
        stack_kernel, jax.ShapeDtypeStruct((2, row_blocks, rows, block_size), jnp.bfloat16), "vv", STACK
    )(blocked(charges), blocked(currents))
    held = kernel_call(
        join_kernel, jax.ShapeDtypeStruct((2, 2 * row_blocks, rows, block_size), jnp.bfloat16), "vv", JOIN
    )(message, swapped(message, "cell", 1))

    totals = jax.ShapeDtypeStruct((row_blocks, rows, block_size), jnp.float32)
    matrix_shape = jax.ShapeDtypeStruct((row_blocks, block_size, share), jnp.bfloat16)
    matrix, outflow = kernel_call(outflow_kernel, (matrix_shape, totals), "vv", SMALL)(message, branch_ends)
    half_shape = jax.ShapeDtypeStruct((regions - 1, row_blocks // 2) + p_blocks.shape[2:], jnp.bfloat16)
    sent = kernel_call(functools.partial(send_kernel, regions), half_shape, "va", SMALL)(p_blocks, outflow)
    mine = swapped(sent, "cell", 1)
    theirs = swapped(mine, "col", 1)

    pieces = [lax.ppermute(held, "blk", list(enumerate(targets))) for targets in region_moves(regions)]

    slots = p_cols.shape[2]
    factors, table, potential, flux, early, other_matrix = kernel_call(
        functools.partial(first_kernel, regions),
        (
            jax.ShapeDtypeStruct((1 + row_blocks, rows, block_size), jnp.float32),
            jax.ShapeDtypeStruct((2, regions, row_blocks, slots, block_size), jnp.int32),
            totals,
            totals,
            jax.ShapeDtypeStruct((2 * row_blocks + 1, rows, block_size), jnp.bfloat16),
            matrix_shape,
        ),
        "vvvvvvvv",
        SMALL,
        [pltpu.VMEM((rows, block_size), jnp.float32)],
    )(
        held, p_blocks, l_blocks, p_cols.transpose(0, 2, 1), l_cols.transpose(0, 2, 1), omegas[None], resist[None],
        branch_ends,
    )
    early = swapped(early, "cell", 1)
    for move, piece in enumerate(pieces[:-1], 1):
        potential, flux = kernel_call(
            functools.partial(next_kernel, regions, move), (totals, totals), "vvvvvvv", NEXT
        )(table, piece, p_blocks, l_blocks, potential, flux, matrix)

    numbers_shape = jax.ShapeDtypeStruct((rows, block_size), jnp.int32)
    other_scratch = pltpu.VMEM((row_blocks, rows, block_size), jnp.bfloat16)
    begun, numbers = kernel_call(
        functools.partial(main_kernel, regions),
        (jax.ShapeDtypeStruct((rows, share), jnp.float32), numbers_shape),
        "v" * (10 + regions),
        MAIN,
        [other_scratch],
    )(*pieces, mine, table, p_blocks, l_blocks, potential, flux, early, matrix, other_matrix, held, factors)
    result = jax.ShapeDtypeStruct(charges.shape, jnp.float32)
    return kernel_call(
        functools.partial(last_kernel, regions), (result, result), "v" * (7 + regions), LAST, [other_scratch]
    )(*pieces, theirs, numbers, begun, early, other_matrix, held, outflow, factors)


def per_device(*args):
    row_blocks, regions = args[0].shape[:2]
    paired = lax.axis_size("cell") == 2 and lax.axis_size("col") == 2
    paired = paired and row_blocks % 2 == 0 and row_blocks * args[0].shape[2] <= 2 * args[4].shape[0]
    return (paired_step if paired else general_step)(*args)


def solution(mesh):
    placed = (
        P(("job", "blk", "cell"), None, None, None, None),
        P(("job", "blk", "cell"), None, None),
        P(("job", "blk", "cell"), None, None, None, None),
        P(("job", "blk", "cell"), None, None),
        P("col", None, ("job", "blk", "cell")),
        P("col", None, ("job", "blk", "cell")),
        P("col"),
        P(("job", "blk", "cell")),
        P(None, ("job", "blk", "cell")),
    )
    return jax.shard_map(
        per_device,
        mesh=mesh,
        in_specs=placed,
        out_specs=(P("col", None, ("job", "blk", "cell")), P("col", None, ("job", "blk", "cell"))),
        check_vma=False,
    )
```

```python
import functools

import jax
import jax.numpy as jnp
from jax import lax
from jax.experimental import pallas as pl
from jax.experimental.pallas import tpu as pltpu
from jax.sharding import PartitionSpec as P

NT = (((1,), (1,)), ((), ()))
NN = (((1,), (0,)), ((), ()))
VMEM = pl.BlockSpec(memory_space=pltpu.VMEM)
SMEM = pl.BlockSpec(memory_space=pltpu.SMEM)
ANY = pl.BlockSpec(memory_space=pl.ANY)
STACK = 5_000_000
JOIN = 10_000_000
SMALL = 1_000
NEXT = 3_000_000
MAIN = 1000000
LAST = 8_000_000


def halves(count):
    steps = []
    while count > 1:
        count //= 2
        steps.append(count)
    return steps


def swapped(array, axis, distance):
    return lax.ppermute(array, axis, [(i, i ^ distance) for i in range(lax.axis_size(axis))])


def block_kernel(offsets, cols_ref, place_ref, held_ref, slab_ref, out_ref):
    row_blocks, _, slots = slab_ref.shape[:3]
    own_region, own_cell = place_ref[0], place_ref[1]
    for row in range(row_blocks):
        total = jnp.zeros(out_ref.shape[1:], jnp.float32)
        for piece, offset in enumerate(offsets):
            region = own_region ^ offset
            for slot in range(slots):
                column = cols_ref[row, region, slot]
                side = lax.div(column, row_blocks) ^ own_cell
                block = held_ref[side, piece, lax.rem(column, row_blocks)]
                total += lax.dot_general(
                    block, slab_ref[row, region, slot], NT, preferred_element_type=jnp.float32
                )
        out_ref[row] = total.astype(out_ref.dtype)


def block_product(slab, cols, place, held, offsets, dtype):
    row_blocks, block_size = slab.shape[0], slab.shape[-1]
    rows = held.shape[-2]
    return pl.pallas_call(
        functools.partial(block_kernel, offsets),
        out_shape=jax.ShapeDtypeStruct((row_blocks, rows, block_size), dtype),
        in_specs=[SMEM, SMEM, VMEM, VMEM],
        out_specs=VMEM,
        compiler_params=pltpu.CompilerParams(vmem_limit_bytes=32 * 1024 * 1024),
        cost_estimate=pl.CostEstimate(
            flops=2 * rows * slab.size, bytes_accessed=2 * slab.size + 2 * held.size, transcendentals=0
        ),
    )(cols, place, held, slab)


def incidence_kernel(ends_ref, current_ref, matrix_ref, out_ref):
    blocks, _, block_size = out_ref.shape
    cells = ends_ref.shape[1]
    leaves, enters = ends_ref[0:1, :], ends_ref[1:2, :]
    current = current_ref[...]
    for block in range(blocks):
        panel = lax.broadcasted_iota(jnp.int32, (block_size, cells), 0) + block * block_size
        entry = (leaves == panel).astype(jnp.float32) - (enters == panel).astype(jnp.float32)
        entry = entry.astype(jnp.bfloat16)
        matrix_ref[block] = entry
        out_ref[block] = lax.dot_general(current, entry, NT, preferred_element_type=jnp.float32)


def incidence(ends, current, panels, block_size):
    cells = ends.shape[1]
    blocks = panels // block_size
    return pl.pallas_call(
        incidence_kernel,
        out_shape=(
            jax.ShapeDtypeStruct((blocks, block_size, cells), jnp.bfloat16),
            jax.ShapeDtypeStruct((blocks, current.shape[0], block_size), jnp.float32),
        ),
        in_specs=[VMEM, VMEM],
        out_specs=(VMEM, VMEM),
        compiler_params=pltpu.CompilerParams(vmem_limit_bytes=32 * 1024 * 1024),
        cost_estimate=pl.CostEstimate(
            flops=4 * panels * cells * current.shape[0], bytes_accessed=2 * panels * cells, transcendentals=0
        ),
    )(ends, current)


def drop_kernel(potential_ref, matrix_ref, base_ref, out_ref):
    total = base_ref[...]
    for block in range(matrix_ref.shape[0]):
        total += lax.dot_general(
            potential_ref[block], matrix_ref[block], NN, preferred_element_type=jnp.float32
        )
    out_ref[...] = total


def with_drop(potential, matrix, base):
    return pl.pallas_call(
        drop_kernel,
        out_shape=jax.ShapeDtypeStruct(base.shape, jnp.float32),
        in_specs=[VMEM, VMEM, VMEM],
        out_specs=VMEM,
        compiler_params=pltpu.CompilerParams(vmem_limit_bytes=32 * 1024 * 1024),
        cost_estimate=pl.CostEstimate(
            flops=2 * base.shape[0] * matrix.size, bytes_accessed=2 * matrix.size, transcendentals=0
        ),
    )(potential, matrix, base)


def turned(array):
    return jnp.stack([-array[:, 1], array[:, 0]], axis=1)


def general_step(p_blocks, p_cols, l_blocks, l_cols, charges, currents, omegas, resist, branch_ends):
    freq_count, _, share = charges.shape
    block_size = p_blocks.shape[-1]
    row_blocks = p_blocks.shape[0]
    rows = 2 * freq_count
    regions, cells = lax.axis_size("blk"), lax.axis_size("cell")
    region, cell = lax.axis_index("blk"), lax.axis_index("cell")
    place = jnp.stack([region, cell]).astype(jnp.int32)

    def blocked(array):
        return array.reshape(rows, row_blocks, block_size).transpose(1, 0, 2)

    def flat(array):
        return array.transpose(1, 0, 2).reshape(rows, share)

    held = jnp.stack([blocked(charges), blocked(turned(currents))])[:, None]
    offsets = [0]
    for step in halves(regions):
        held = jnp.concatenate([held, swapped(held, "blk", step)], axis=1)
        offsets = offsets + [o ^ step for o in offsets]

    local = ((branch_ends // share) ^ cell) * share + branch_ends % share
    matrix, outflow = incidence(local, currents.reshape(rows, share), cells * share, block_size)
    outflow = outflow.reshape(cells, row_blocks, rows, block_size)

    charge_all, current_all = held[0][None], held[1][None]
    for step in reversed(halves(cells)):
        charge_all = jnp.concatenate([charge_all, swapped(charge_all, "cell", step)], axis=0)
    potential = block_product(p_blocks, p_cols, place, charge_all, offsets, jnp.bfloat16)
    for step in reversed(halves(cells)):
        away = [o for o in range(cells) if o & step and not o & (step - 1)]
        kept = [o - step for o in away]
        sums = jnp.stack([outflow[o] for o in away]).astype(jnp.bfloat16)
        flat_current = current_all.reshape(-1, rows, block_size)
        message = jnp.concatenate([flat_current, sums.reshape(-1, rows, block_size)], axis=0)
        message = swapped(message, "cell", step)
        got = message[: flat_current.shape[0]].reshape(current_all.shape)
        more = message[flat_current.shape[0] :].reshape(sums.shape).astype(jnp.float32)
        current_all = jnp.concatenate([current_all, got], axis=0)
        for position, o in enumerate(kept):
            outflow = outflow.at[o].add(more[position])
    potential_all = potential[None]
    for step in reversed(halves(cells)):
        potential_all = jnp.concatenate([potential_all, swapped(potential_all, "cell", step)], axis=0)
    flux_turned = block_product(l_blocks, l_cols, place, current_all, offsets, jnp.float32)

    scale = jnp.repeat(omegas, 2)[:, None]
    base = resist * currents.reshape(rows, share).astype(jnp.float32) + scale * flat(flux_turned)
    cell_rows = with_drop(potential_all.reshape(-1, rows, block_size), matrix, base)
    panel_rows = flat(outflow[0]) + scale * turned(charges).reshape(rows, share).astype(jnp.float32)
    return (cell_rows.reshape(freq_count, 2, share), panel_rows.reshape(freq_count, 2, share))


def back(regions, move):
    own = lax.axis_index("blk")
    if move == 0:
        return own
    targets = region_moves(regions)[move - 1]
    return sum(jnp.where(own == target, source, 0) for source, target in enumerate(targets))


def region_moves(regions):
    if regions == 4:
        return [[2, 3, 0, 1], [3, 2, 1, 0], [1, 0, 3, 2]]
    return [[(place + shift) % regions for place in range(regions)] for shift in range(1, regions)]


def turned_rows(array):
    rows = array.shape[0]
    odd = lax.broadcasted_iota(jnp.int32, array.shape, 0) & 1
    return jnp.where(odd == 0, -pltpu.roll(array, rows - 1, 0), pltpu.roll(array, 1, 0))


def row_scale(omega_ref, rows):
    shape = (rows, omega_ref.shape[1])
    same = lax.broadcasted_iota(jnp.int32, shape, 0) >> 1 == lax.broadcasted_iota(jnp.int32, shape, 1)
    return jnp.sum(jnp.where(same, omega_ref[...], 0.0), axis=1, keepdims=True)


def lanes(blocks):
    return jnp.concatenate(blocks, axis=1)


def pair_dot(held_ref, positions, slabs):
    return lax.dot_general(
        lanes([held_ref[position] for position in positions]), lanes(slabs), NT, preferred_element_type=jnp.float32
    )


def region_terms(regions, move, table_ref, held_ref, p_ref, l_ref, row):
    region = back(regions, move)
    slots = range(p_ref.shape[2])
    return tuple(
        pair_dot(
            held_ref.at[kind],
            [table_ref[kind, move, row, slot, 0] for slot in slots],
            [slab_ref[row, region, slot] for slot in slots],
        )
        for kind, slab_ref in enumerate((p_ref, l_ref))
    )


def outflow_terms(side, ends_ref, current_ref, matrix_ref, store):
    row_blocks, block_size = matrix_ref.shape[:2]
    leaves, enters = ends_ref[0:1, :], ends_ref[1:2, :]
    current = lanes([current_ref[1, block] for block in range(row_blocks)])
    for block in range(row_blocks):
        base = ((lax.axis_index("cell") ^ side) * row_blocks + block) * block_size
        panel = lax.broadcasted_iota(jnp.int32, (block_size, ends_ref.shape[1]), 0) + base
        entry = (leaves == panel).astype(jnp.float32) - (enters == panel).astype(jnp.float32)
        entry = entry.astype(jnp.bfloat16)
        matrix_ref[block] = entry
        store(block, lax.dot_general(current, entry, NT, preferred_element_type=jnp.float32))


def outflow_kernel(message_ref, ends_ref, matrix_ref, outflow_ref):
    def store(block, sums):
        outflow_ref[block] = sums

    outflow_terms(0, ends_ref, message_ref, matrix_ref, store)


def first_kernel(
    regions, held_ref, p_ref, l_ref, p_cols_ref, l_cols_ref, omega_ref, resist_ref, ends_ref,
    factor_ref, table_ref, potential_ref, flux_ref, early_ref, matrix_ref, numbers_ref,
):
    row_blocks, rows, block_size = potential_ref.shape
    slots = p_ref.shape[2]
    cell = lax.axis_index("cell")
    shape = table_ref.shape[2:]
    lane = lax.broadcasted_iota(jnp.int32, shape, 2)
    numbers = jnp.zeros(shape, jnp.float32)
    for kind, cols_ref in enumerate((p_cols_ref, l_cols_ref)):
        columns = cols_ref[...].astype(jnp.float32)
        place = lax.broadcasted_iota(jnp.int32, columns.shape, 2)
        for move in range(regions):
            column = jnp.sum(jnp.where(place == back(regions, move), columns, 0.0), axis=2, keepdims=True)
            column = jnp.broadcast_to(column, shape)
            other = jnp.where(column < row_blocks, column + row_blocks, column - row_blocks)
            table_ref[kind, move] = jnp.where(cell == 0, column, other).astype(jnp.int32)
            if kind == 0:
                numbers = jnp.where(lane == move, jnp.where(cell == 0, other, column), numbers)
    numbers_ref[...] = jnp.zeros_like(numbers_ref)
    for row in range(row_blocks):
        numbers_ref[row * slots : (row + 1) * slots, :] = numbers[row]
    early_ref[2 * row_blocks] = numbers_ref[...].astype(jnp.bfloat16)

    def store(block, sums):
        early_ref[row_blocks + block] = sums.astype(jnp.bfloat16)

    outflow_terms(1, ends_ref, held_ref, matrix_ref, store)
    for row in range(row_blocks):
        potential, flux = region_terms(regions, 0, table_ref, held_ref, p_ref, l_ref, row)
        potential_ref[row], flux_ref[row] = potential, flux
        early_ref[row] = potential.astype(jnp.bfloat16)
    factor_ref[0] = jnp.broadcast_to(row_scale(omega_ref, rows), (rows, block_size))
    for row in range(row_blocks):
        columns = slice(row * block_size, (row + 1) * block_size)
        factor_ref[1 + row] = jnp.broadcast_to(resist_ref[:, columns], (rows, block_size))


def next_kernel(
    regions, move, table_ref, held_ref, p_ref, l_ref, p_in_ref, f_in_ref, matrix_ref, potential_ref, flux_ref
):
    del matrix_ref
    for row in range(potential_ref.shape[0]):
        potential, flux = region_terms(regions, move, table_ref, held_ref, p_ref, l_ref, row)
        potential_ref[row], flux_ref[row] = p_in_ref[row] + potential, f_in_ref[row] + flux


def stack_kernel(charge_ref, current_ref, out_ref):
    out_ref[0] = charge_ref[...]
    out_ref[1] = current_ref[...]


def send_kernel(regions, p_ref, after_ref, out_ref):
    del after_ref
    half = out_ref.shape[1]
    for move in range(1, regions):
        for row in range(half):
            out_ref[move - 1, row] = p_ref[lax.axis_index("col") * half + row, back(regions, move)]


def join_kernel(own_ref, other_ref, out_ref):
    blocks = own_ref.shape[1]
    for kind in range(own_ref.shape[0]):
        out_ref[kind, :blocks] = own_ref[kind]
        out_ref[kind, blocks:] = other_ref[kind]


def store_rows(out_ref, columns, array):
    for freq in range(out_ref.shape[0]):
        out_ref[freq, :, columns] = array[2 * freq : 2 * freq + 2]


def other_rows(part, slab_ref, numbers_ref, early_ref, piece_refs, other_ref):
    half, slots = slab_ref.shape[1:3]
    for position in range(half):
        row = (lax.axis_index("col") ^ part) * half + position
        total = early_ref[row].astype(jnp.float32)
        for at, piece_ref in enumerate(piece_refs):
            total += pair_dot(
                piece_ref.at[0],
                [numbers_ref[row * slots + slot, at + 1] for slot in range(slots)],
                [slab_ref[at, position, slot] for slot in range(slots)],
            )
        other_ref[row] = total.astype(jnp.bfloat16)


def other_drop(part, half, other_ref, matrix_ref):
    start = (lax.axis_index("col") ^ part) * half
    rows = lanes([other_ref[start + position] for position in range(half)])
    matrix = matrix_ref[pl.ds(start, half)].reshape(rows.shape[1], -1)
    return lax.dot_general(rows, matrix, NN, preferred_element_type=jnp.float32)


def main_kernel(regions, *refs):
    piece_refs = refs[: regions - 1]
    (mine_ref, table_ref, p_ref, l_ref, p_in_ref, f_in_ref, early_ref, matrix_ref, other_matrix_ref, held_ref,
     factor_ref, out_ref, numbers_ref, other_ref) = refs[regions - 1 :]
    row_blocks, _, block_size = p_in_ref.shape
    numbers_ref[...] = early_ref[2 * row_blocks].astype(jnp.float32).astype(jnp.int32)
    potentials, fluxes = [], []
    for row in range(row_blocks):
        potential, flux = region_terms(regions, regions - 1, table_ref, piece_refs[-1], p_ref, l_ref, row)
        potentials.append((p_in_ref[row] + potential).astype(jnp.bfloat16))
        fluxes.append(f_in_ref[row] + flux)
    other_rows(0, mine_ref, numbers_ref, early_ref, piece_refs, other_ref)
    matrix = matrix_ref[...].reshape(row_blocks * block_size, -1)
    drop = lax.dot_general(lanes(potentials), matrix, NN, preferred_element_type=jnp.float32)
    drop += other_drop(0, row_blocks // 2, other_ref, other_matrix_ref)
    for row in range(row_blocks):
        columns = slice(row * block_size, (row + 1) * block_size)
        current = held_ref[1, row].astype(jnp.float32)
        flux = factor_ref[0] * turned_rows(fluxes[row])
        out_ref[:, columns] = factor_ref[1 + row] * current + flux + drop[:, columns]


def last_kernel(regions, *refs):
    piece_refs = refs[: regions - 1]
    (theirs_ref, numbers_ref, begun_ref, early_ref, matrix_ref, held_ref, outflow_ref, factor_ref,
     cell_ref, panel_ref, other_ref) = refs[regions - 1 :]
    row_blocks, _, block_size = outflow_ref.shape
    other_rows(1, theirs_ref, numbers_ref, early_ref, piece_refs, other_ref)
    total = begun_ref[...] + other_drop(1, row_blocks // 2, other_ref, matrix_ref)
    for row in range(row_blocks):
        columns = slice(row * block_size, (row + 1) * block_size)
        store_rows(cell_ref, columns, total[:, columns])
        outflow = outflow_ref[row] + early_ref[row_blocks + row].astype(jnp.float32)
        charge = factor_ref[0] * turned_rows(held_ref[0, row].astype(jnp.float32))
        store_rows(panel_ref, columns, outflow + charge)


def kernel_call(body, out_shape, memories, weight, scratch=()):
    many = isinstance(out_shape, tuple)
    return pl.pallas_call(
        body,
        out_shape=out_shape,
        in_specs=[{"v": VMEM, "a": ANY}[m] for m in memories],
        out_specs=tuple(VMEM for _ in out_shape) if many else VMEM,
        scratch_shapes=scratch,
        compiler_params=pltpu.CompilerParams(vmem_limit_bytes=16 * 1024 * 1024),
        cost_estimate=pl.CostEstimate(flops=weight * 1000, bytes_accessed=4_000_000, transcendentals=0),
    )


def paired_step(p_blocks, p_cols, l_blocks, l_cols, charges, currents, omegas, resist, branch_ends):
    freq_count, _, share = charges.shape
    block_size = p_blocks.shape[-1]
    row_blocks = p_blocks.shape[0]
    rows = 2 * freq_count
    regions = lax.axis_size("blk")

    def blocked(array):
        return array.reshape(rows, row_blocks, block_size).transpose(1, 0, 2)

    message = kernel_call(
        stack_kernel, jax.ShapeDtypeStruct((2, row_blocks, rows, block_size), jnp.bfloat16), "vv", STACK
    )(blocked(charges), blocked(currents))
    held = kernel_call(
        join_kernel, jax.ShapeDtypeStruct((2, 2 * row_blocks, rows, block_size), jnp.bfloat16), "vv", JOIN
    )(message, swapped(message, "cell", 1))

    totals = jax.ShapeDtypeStruct((row_blocks, rows, block_size), jnp.float32)
    matrix_shape = jax.ShapeDtypeStruct((row_blocks, block_size, share), jnp.bfloat16)
    matrix, outflow = kernel_call(outflow_kernel, (matrix_shape, totals), "vv", SMALL)(message, branch_ends)
    half_shape = jax.ShapeDtypeStruct((regions - 1, row_blocks // 2) + p_blocks.shape[2:], jnp.bfloat16)
    sent = kernel_call(functools.partial(send_kernel, regions), half_shape, "va", SMALL)(p_blocks, outflow)
    mine = swapped(sent, "cell", 1)
    theirs = swapped(mine, "col", 1)

    pieces = [lax.ppermute(held, "blk", list(enumerate(targets))) for targets in region_moves(regions)]

    slots = p_cols.shape[2]
    factors, table, potential, flux, early, other_matrix = kernel_call(
        functools.partial(first_kernel, regions),
        (
            jax.ShapeDtypeStruct((1 + row_blocks, rows, block_size), jnp.float32),
            jax.ShapeDtypeStruct((2, regions, row_blocks, slots, block_size), jnp.int32),
            totals,
            totals,
            jax.ShapeDtypeStruct((2 * row_blocks + 1, rows, block_size), jnp.bfloat16),
            matrix_shape,
        ),
        "vvvvvvvv",
        SMALL,
        [pltpu.VMEM((rows, block_size), jnp.float32)],
    )(
        held, p_blocks, l_blocks, p_cols.transpose(0, 2, 1), l_cols.transpose(0, 2, 1), omegas[None], resist[None],
        branch_ends,
    )
    early = swapped(early, "cell", 1)
    for move, piece in enumerate(pieces[:-1], 1):
        potential, flux = kernel_call(
            functools.partial(next_kernel, regions, move), (totals, totals), "vvvvvvv", NEXT
        )(table, piece, p_blocks, l_blocks, potential, flux, matrix)

    numbers_shape = jax.ShapeDtypeStruct((rows, block_size), jnp.int32)
    other_scratch = pltpu.VMEM((row_blocks, rows, block_size), jnp.bfloat16)
    begun, numbers = kernel_call(
        functools.partial(main_kernel, regions),
        (jax.ShapeDtypeStruct((rows, share), jnp.float32), numbers_shape),
        "v" * (10 + regions),
        MAIN,
        [other_scratch],
    )(*pieces, mine, table, p_blocks, l_blocks, potential, flux, early, matrix, other_matrix, held, factors)
    result = jax.ShapeDtypeStruct(charges.shape, jnp.float32)
    return kernel_call(
        functools.partial(last_kernel, regions), (result, result), "v" * (7 + regions), LAST, [other_scratch]
    )(*pieces, theirs, numbers, begun, early, other_matrix, held, outflow, factors)


def per_device(*args):
    row_blocks, regions = args[0].shape[:2]
    paired = lax.axis_size("cell") == 2 and lax.axis_size("col") == 2
    paired = paired and row_blocks % 2 == 0 and row_blocks * args[0].shape[2] <= 2 * args[4].shape[0]
    return (paired_step if paired else general_step)(*args)


def solution(mesh):
    placed = (
        P(("job", "blk", "cell"), None, None, None, None),
        P(("job", "blk", "cell"), None, None),
        P(("job", "blk", "cell"), None, None, None, None),
        P(("job", "blk", "cell"), None, None),
        P("col", None, ("job", "blk", "cell")),
        P("col", None, ("job", "blk", "cell")),
        P("col"),
        P(("job", "blk", "cell")),
        P(None, ("job", "blk", "cell")),
    )
    return jax.shard_map(
        per_device,
        mesh=mesh,
        in_specs=placed,
        out_specs=(P("col", None, ("job", "blk", "cell")), P("col", None, ("job", "blk", "cell"))),
        check_vma=False,
    )
```

```python
import functools

import jax
import jax.numpy as jnp
from jax import lax
from jax.experimental import pallas as pl
from jax.experimental.pallas import tpu as pltpu
from jax.sharding import PartitionSpec as P

NT = (((1,), (1,)), ((), ()))
NN = (((1,), (0,)), ((), ()))
VMEM = pl.BlockSpec(memory_space=pltpu.VMEM)
SMEM = pl.BlockSpec(memory_space=pltpu.SMEM)
ANY = pl.BlockSpec(memory_space=pl.ANY)
STACK = 5_000_000
JOIN = 10_000_000
SMALL = 1_000
NEXT = 3_000_000
MAIN = 1000000
LAST = 8_000_000


def halves(count):
    steps = []
    while count > 1:
        count //= 2
        steps.append(count)
    return steps


def swapped(array, axis, distance):
    return lax.ppermute(array, axis, [(i, i ^ distance) for i in range(lax.axis_size(axis))])


def block_kernel(offsets, cols_ref, place_ref, held_ref, slab_ref, out_ref):
    row_blocks, _, slots = slab_ref.shape[:3]
    own_region, own_cell = place_ref[0], place_ref[1]
    for row in range(row_blocks):
        total = jnp.zeros(out_ref.shape[1:], jnp.float32)
        for piece, offset in enumerate(offsets):
            region = own_region ^ offset
            for slot in range(slots):
                column = cols_ref[row, region, slot]
                side = lax.div(column, row_blocks) ^ own_cell
                block = held_ref[side, piece, lax.rem(column, row_blocks)]
                total += lax.dot_general(
                    block, slab_ref[row, region, slot], NT, preferred_element_type=jnp.float32
                )
        out_ref[row] = total.astype(out_ref.dtype)


def block_product(slab, cols, place, held, offsets, dtype):
    row_blocks, block_size = slab.shape[0], slab.shape[-1]
    rows = held.shape[-2]
    return pl.pallas_call(
        functools.partial(block_kernel, offsets),
        out_shape=jax.ShapeDtypeStruct((row_blocks, rows, block_size), dtype),
        in_specs=[SMEM, SMEM, VMEM, VMEM],
        out_specs=VMEM,
        compiler_params=pltpu.CompilerParams(vmem_limit_bytes=32 * 1024 * 1024),
        cost_estimate=pl.CostEstimate(
            flops=2 * rows * slab.size, bytes_accessed=2 * slab.size + 2 * held.size, transcendentals=0
        ),
    )(cols, place, held, slab)


def incidence_kernel(ends_ref, current_ref, matrix_ref, out_ref):
    blocks, _, block_size = out_ref.shape
    cells = ends_ref.shape[1]
    leaves, enters = ends_ref[0:1, :], ends_ref[1:2, :]
    current = current_ref[...]
    for block in range(blocks):
        panel = lax.broadcasted_iota(jnp.int32, (block_size, cells), 0) + block * block_size
        entry = (leaves == panel).astype(jnp.float32) - (enters == panel).astype(jnp.float32)
        entry = entry.astype(jnp.bfloat16)
        matrix_ref[block] = entry
        out_ref[block] = lax.dot_general(current, entry, NT, preferred_element_type=jnp.float32)


def incidence(ends, current, panels, block_size):
    cells = ends.shape[1]
    blocks = panels // block_size
    return pl.pallas_call(
        incidence_kernel,
        out_shape=(
            jax.ShapeDtypeStruct((blocks, block_size, cells), jnp.bfloat16),
            jax.ShapeDtypeStruct((blocks, current.shape[0], block_size), jnp.float32),
        ),
        in_specs=[VMEM, VMEM],
        out_specs=(VMEM, VMEM),
        compiler_params=pltpu.CompilerParams(vmem_limit_bytes=32 * 1024 * 1024),
        cost_estimate=pl.CostEstimate(
            flops=4 * panels * cells * current.shape[0], bytes_accessed=2 * panels * cells, transcendentals=0
        ),
    )(ends, current)


def drop_kernel(potential_ref, matrix_ref, base_ref, out_ref):
    total = base_ref[...]
    for block in range(matrix_ref.shape[0]):
        total += lax.dot_general(
            potential_ref[block], matrix_ref[block], NN, preferred_element_type=jnp.float32
        )
    out_ref[...] = total


def with_drop(potential, matrix, base):
    return pl.pallas_call(
        drop_kernel,
        out_shape=jax.ShapeDtypeStruct(base.shape, jnp.float32),
        in_specs=[VMEM, VMEM, VMEM],
        out_specs=VMEM,
        compiler_params=pltpu.CompilerParams(vmem_limit_bytes=32 * 1024 * 1024),
        cost_estimate=pl.CostEstimate(
            flops=2 * base.shape[0] * matrix.size, bytes_accessed=2 * matrix.size, transcendentals=0
        ),
    )(potential, matrix, base)


def turned(array):
    return jnp.stack([-array[:, 1], array[:, 0]], axis=1)


def general_step(p_blocks, p_cols, l_blocks, l_cols, charges, currents, omegas, resist, branch_ends):
    freq_count, _, share = charges.shape
    block_size = p_blocks.shape[-1]
    row_blocks = p_blocks.shape[0]
    rows = 2 * freq_count
    regions, cells = lax.axis_size("blk"), lax.axis_size("cell")
    region, cell = lax.axis_index("blk"), lax.axis_index("cell")
    place = jnp.stack([region, cell]).astype(jnp.int32)

    def blocked(array):
        return array.reshape(rows, row_blocks, block_size).transpose(1, 0, 2)

    def flat(array):
        return array.transpose(1, 0, 2).reshape(rows, share)

    held = jnp.stack([blocked(charges), blocked(turned(currents))])[:, None]
    offsets = [0]
    for step in halves(regions):
        held = jnp.concatenate([held, swapped(held, "blk", step)], axis=1)
        offsets = offsets + [o ^ step for o in offsets]

    local = ((branch_ends // share) ^ cell) * share + branch_ends % share
    matrix, outflow = incidence(local, currents.reshape(rows, share), cells * share, block_size)
    outflow = outflow.reshape(cells, row_blocks, rows, block_size)

    charge_all, current_all = held[0][None], held[1][None]
    for step in reversed(halves(cells)):
        charge_all = jnp.concatenate([charge_all, swapped(charge_all, "cell", step)], axis=0)
    potential = block_product(p_blocks, p_cols, place, charge_all, offsets, jnp.bfloat16)
    for step in reversed(halves(cells)):
        away = [o for o in range(cells) if o & step and not o & (step - 1)]
        kept = [o - step for o in away]
        sums = jnp.stack([outflow[o] for o in away]).astype(jnp.bfloat16)
        flat_current = current_all.reshape(-1, rows, block_size)
        message = jnp.concatenate([flat_current, sums.reshape(-1, rows, block_size)], axis=0)
        message = swapped(message, "cell", step)
        got = message[: flat_current.shape[0]].reshape(current_all.shape)
        more = message[flat_current.shape[0] :].reshape(sums.shape).astype(jnp.float32)
        current_all = jnp.concatenate([current_all, got], axis=0)
        for position, o in enumerate(kept):
            outflow = outflow.at[o].add(more[position])
    potential_all = potential[None]
    for step in reversed(halves(cells)):
        potential_all = jnp.concatenate([potential_all, swapped(potential_all, "cell", step)], axis=0)
    flux_turned = block_product(l_blocks, l_cols, place, current_all, offsets, jnp.float32)

    scale = jnp.repeat(omegas, 2)[:, None]
    base = resist * currents.reshape(rows, share).astype(jnp.float32) + scale * flat(flux_turned)
    cell_rows = with_drop(potential_all.reshape(-1, rows, block_size), matrix, base)
    panel_rows = flat(outflow[0]) + scale * turned(charges).reshape(rows, share).astype(jnp.float32)
    return (cell_rows.reshape(freq_count, 2, share), panel_rows.reshape(freq_count, 2, share))


def back(regions, move):
    own = lax.axis_index("blk")
    if move == 0:
        return own
    targets = region_moves(regions)[move - 1]
    return sum(jnp.where(own == target, source, 0) for source, target in enumerate(targets))


def region_moves(regions):
    if regions == 4:
        return [[2, 3, 0, 1], [3, 2, 1, 0], [1, 0, 3, 2]]
    return [[(place + shift) % regions for place in range(regions)] for shift in range(1, regions)]


def turned_rows(array):
    rows = array.shape[0]
    odd = lax.broadcasted_iota(jnp.int32, array.shape, 0) & 1
    return jnp.where(odd == 0, -pltpu.roll(array, rows - 1, 0), pltpu.roll(array, 1, 0))


def row_scale(omega_ref, rows):
    shape = (rows, omega_ref.shape[1])
    same = lax.broadcasted_iota(jnp.int32, shape, 0) >> 1 == lax.broadcasted_iota(jnp.int32, shape, 1)
    return jnp.sum(jnp.where(same, omega_ref[...], 0.0), axis=1, keepdims=True)


def lanes(blocks):
    return jnp.concatenate(blocks, axis=1)


def pair_dot(held_ref, positions, slabs):
    return lax.dot_general(
        lanes([held_ref[position] for position in positions]), lanes(slabs), NT, preferred_element_type=jnp.float32
    )


def region_terms(regions, move, table_ref, held_ref, p_ref, l_ref, row):
    region = back(regions, move)
    slots = range(p_ref.shape[2])
    return tuple(
        pair_dot(
            held_ref.at[kind],
            [table_ref[kind, move, row, slot, 0] for slot in slots],
            [slab_ref[row, region, slot] for slot in slots],
        )
        for kind, slab_ref in enumerate((p_ref, l_ref))
    )


def outflow_terms(side, ends_ref, current_ref, matrix_ref, store):
    row_blocks, block_size = matrix_ref.shape[:2]
    leaves, enters = ends_ref[0:1, :], ends_ref[1:2, :]
    current = lanes([current_ref[1, block] for block in range(row_blocks)])
    for block in range(row_blocks):
        base = ((lax.axis_index("cell") ^ side) * row_blocks + block) * block_size
        panel = lax.broadcasted_iota(jnp.int32, (block_size, ends_ref.shape[1]), 0) + base
        entry = (leaves == panel).astype(jnp.float32) - (enters == panel).astype(jnp.float32)
        entry = entry.astype(jnp.bfloat16)
        matrix_ref[block] = entry
        store(block, lax.dot_general(current, entry, NT, preferred_element_type=jnp.float32))


def outflow_kernel(message_ref, ends_ref, matrix_ref, outflow_ref):
    def store(block, sums):
        outflow_ref[block] = sums

    outflow_terms(0, ends_ref, message_ref, matrix_ref, store)


def first_kernel(
    regions, held_ref, p_ref, l_ref, p_cols_ref, l_cols_ref, omega_ref, resist_ref, ends_ref,
    factor_ref, table_ref, potential_ref, flux_ref, early_ref, matrix_ref, numbers_ref,
):
    row_blocks, rows, block_size = potential_ref.shape
    slots = p_ref.shape[2]
    cell = lax.axis_index("cell")
    shape = table_ref.shape[2:]
    lane = lax.broadcasted_iota(jnp.int32, shape, 2)
    numbers = jnp.zeros(shape, jnp.float32)
    for kind, cols_ref in enumerate((p_cols_ref, l_cols_ref)):
        columns = cols_ref[...].astype(jnp.float32)
        place = lax.broadcasted_iota(jnp.int32, columns.shape, 2)
        for move in range(regions):
            column = jnp.sum(jnp.where(place == back(regions, move), columns, 0.0), axis=2, keepdims=True)
            column = jnp.broadcast_to(column, shape)
            other = jnp.where(column < row_blocks, column + row_blocks, column - row_blocks)
            table_ref[kind, move] = jnp.where(cell == 0, column, other).astype(jnp.int32)
            if kind == 0:
                numbers = jnp.where(lane == move, jnp.where(cell == 0, other, column), numbers)
    numbers_ref[...] = jnp.zeros_like(numbers_ref)
    for row in range(row_blocks):
        numbers_ref[row * slots : (row + 1) * slots, :] = numbers[row]
    early_ref[2 * row_blocks] = numbers_ref[...].astype(jnp.bfloat16)

    def store(block, sums):
        early_ref[row_blocks + block] = sums.astype(jnp.bfloat16)

    outflow_terms(1, ends_ref, held_ref, matrix_ref, store)
    for row in range(row_blocks):
        potential, flux = region_terms(regions, 0, table_ref, held_ref, p_ref, l_ref, row)
        potential_ref[row], flux_ref[row] = potential, flux
        early_ref[row] = potential.astype(jnp.bfloat16)
    factor_ref[0] = jnp.broadcast_to(row_scale(omega_ref, rows), (rows, block_size))
    for row in range(row_blocks):
        columns = slice(row * block_size, (row + 1) * block_size)
        factor_ref[1 + row] = jnp.broadcast_to(resist_ref[:, columns], (rows, block_size))


def next_kernel(
    regions, move, table_ref, held_ref, p_ref, l_ref, p_in_ref, f_in_ref, matrix_ref, potential_ref, flux_ref
):
    del matrix_ref
    for row in range(potential_ref.shape[0]):
        potential, flux = region_terms(regions, move, table_ref, held_ref, p_ref, l_ref, row)
        potential_ref[row], flux_ref[row] = p_in_ref[row] + potential, f_in_ref[row] + flux


def stack_kernel(charge_ref, current_ref, out_ref):
    out_ref[0] = charge_ref[...]
    out_ref[1] = current_ref[...]


def send_kernel(regions, p_ref, after_ref, out_ref):
    del after_ref
    half = out_ref.shape[1]
    for move in range(1, regions):
        for row in range(half):
            out_ref[move - 1, row] = p_ref[lax.axis_index("col") * half + row, back(regions, move)]


def join_kernel(own_ref, other_ref, out_ref):
    blocks = own_ref.shape[1]
    for kind in range(own_ref.shape[0]):
        out_ref[kind, :blocks] = own_ref[kind]
        out_ref[kind, blocks:] = other_ref[kind]


def store_rows(out_ref, columns, array):
    for freq in range(out_ref.shape[0]):
        out_ref[freq, :, columns] = array[2 * freq : 2 * freq + 2]


def other_drop(part, slab_ref, numbers_ref, early_ref, piece_refs, matrix_ref):
    half, slots = slab_ref.shape[1:3]
    start = (lax.axis_index("col") ^ part) * half
    rows = []
    for position in range(half):
        row = start + position
        total = early_ref[row].astype(jnp.float32)
        for at, piece_ref in enumerate(piece_refs):
            total += pair_dot(
                piece_ref.at[0],
                [numbers_ref[row * slots + slot, at + 1] for slot in range(slots)],
                [slab_ref[at, position, slot] for slot in range(slots)],
            )
        rows.append(total.astype(jnp.bfloat16))
    matrix = matrix_ref[pl.ds(start, half)].reshape(half * matrix_ref.shape[1], -1)
    return lax.dot_general(lanes(rows), matrix, NN, preferred_element_type=jnp.float32)


def main_kernel(regions, *refs):
    piece_refs = refs[: regions - 1]
    (mine_ref, table_ref, p_ref, l_ref, p_in_ref, f_in_ref, early_ref, matrix_ref, other_matrix_ref, held_ref,
     factor_ref, out_ref, numbers_ref) = refs[regions - 1 :]
    row_blocks, _, block_size = p_in_ref.shape
    numbers_ref[...] = early_ref[2 * row_blocks].astype(jnp.float32).astype(jnp.int32)
    potentials, fluxes = [], []
    for row in range(row_blocks):
        potential, flux = region_terms(regions, regions - 1, table_ref, piece_refs[-1], p_ref, l_ref, row)
        potentials.append((p_in_ref[row] + potential).astype(jnp.bfloat16))
        fluxes.append(f_in_ref[row] + flux)
    drop = other_drop(0, mine_ref, numbers_ref, early_ref, piece_refs, other_matrix_ref)
    matrix = matrix_ref[...].reshape(row_blocks * block_size, -1)
    drop += lax.dot_general(lanes(potentials), matrix, NN, preferred_element_type=jnp.float32)
    for row in range(row_blocks):
        columns = slice(row * block_size, (row + 1) * block_size)
        current = held_ref[1, row].astype(jnp.float32)
        flux = factor_ref[0] * turned_rows(fluxes[row])
        out_ref[:, columns] = factor_ref[1 + row] * current + flux + drop[:, columns]


def last_kernel(regions, *refs):
    piece_refs = refs[: regions - 1]
    (theirs_ref, numbers_ref, begun_ref, early_ref, matrix_ref, held_ref, outflow_ref, factor_ref,
     cell_ref, panel_ref) = refs[regions - 1 :]
    row_blocks, _, block_size = outflow_ref.shape
    total = begun_ref[...] + other_drop(1, theirs_ref, numbers_ref, early_ref, piece_refs, matrix_ref)
    for row in range(row_blocks):
        columns = slice(row * block_size, (row + 1) * block_size)
        store_rows(cell_ref, columns, total[:, columns])
        outflow = outflow_ref[row] + early_ref[row_blocks + row].astype(jnp.float32)
        charge = factor_ref[0] * turned_rows(held_ref[0, row].astype(jnp.float32))
        store_rows(panel_ref, columns, outflow + charge)


def kernel_call(body, out_shape, memories, weight, scratch=()):
    many = isinstance(out_shape, tuple)
    return pl.pallas_call(
        body,
        out_shape=out_shape,
        in_specs=[{"v": VMEM, "a": ANY}[m] for m in memories],
        out_specs=tuple(VMEM for _ in out_shape) if many else VMEM,
        scratch_shapes=scratch,
        compiler_params=pltpu.CompilerParams(vmem_limit_bytes=16 * 1024 * 1024),
        cost_estimate=pl.CostEstimate(flops=weight * 1000, bytes_accessed=4_000_000, transcendentals=0),
    )


def paired_step(p_blocks, p_cols, l_blocks, l_cols, charges, currents, omegas, resist, branch_ends):
    freq_count, _, share = charges.shape
    block_size = p_blocks.shape[-1]
    row_blocks = p_blocks.shape[0]
    rows = 2 * freq_count
    regions = lax.axis_size("blk")

    def blocked(array):
        return array.reshape(rows, row_blocks, block_size).transpose(1, 0, 2)

    message = kernel_call(
        stack_kernel, jax.ShapeDtypeStruct((2, row_blocks, rows, block_size), jnp.bfloat16), "vv", STACK
    )(blocked(charges), blocked(currents))
    held = kernel_call(
        join_kernel, jax.ShapeDtypeStruct((2, 2 * row_blocks, rows, block_size), jnp.bfloat16), "vv", JOIN
    )(message, swapped(message, "cell", 1))

    totals = jax.ShapeDtypeStruct((row_blocks, rows, block_size), jnp.float32)
    matrix_shape = jax.ShapeDtypeStruct((row_blocks, block_size, share), jnp.bfloat16)
    matrix, outflow = kernel_call(outflow_kernel, (matrix_shape, totals), "vv", SMALL)(message, branch_ends)
    half_shape = jax.ShapeDtypeStruct((regions - 1, row_blocks // 2) + p_blocks.shape[2:], jnp.bfloat16)
    sent = kernel_call(functools.partial(send_kernel, regions), half_shape, "va", SMALL)(p_blocks, outflow)
    mine = swapped(sent, "cell", 1)
    theirs = swapped(mine, "col", 1)

    pieces = [lax.ppermute(held, "blk", list(enumerate(targets))) for targets in region_moves(regions)]

    slots = p_cols.shape[2]
    factors, table, potential, flux, early, other_matrix = kernel_call(
        functools.partial(first_kernel, regions),
        (
            jax.ShapeDtypeStruct((1 + row_blocks, rows, block_size), jnp.float32),
            jax.ShapeDtypeStruct((2, regions, row_blocks, slots, block_size), jnp.int32),
            totals,
            totals,
            jax.ShapeDtypeStruct((2 * row_blocks + 1, rows, block_size), jnp.bfloat16),
            matrix_shape,
        ),
        "vvvvvvvv",
        SMALL,
        [pltpu.VMEM((rows, block_size), jnp.float32)],
    )(
        held, p_blocks, l_blocks, p_cols.transpose(0, 2, 1), l_cols.transpose(0, 2, 1), omegas[None], resist[None],
        branch_ends,
    )
    early = swapped(early, "cell", 1)
    for move, piece in enumerate(pieces[:-1], 1):
        potential, flux = kernel_call(
            functools.partial(next_kernel, regions, move), (totals, totals), "vvvvvvv", NEXT
        )(table, piece, p_blocks, l_blocks, potential, flux, matrix)

    numbers_shape = jax.ShapeDtypeStruct((rows, block_size), jnp.int32)
    begun, numbers = kernel_call(
        functools.partial(main_kernel, regions),
        (jax.ShapeDtypeStruct((rows, share), jnp.float32), numbers_shape),
        "v" * (10 + regions),
        MAIN,
    )(*pieces, mine, table, p_blocks, l_blocks, potential, flux, early, matrix, other_matrix, held, factors)
    result = jax.ShapeDtypeStruct(charges.shape, jnp.float32)
    return kernel_call(
        functools.partial(last_kernel, regions), (result, result), "v" * (7 + regions), LAST
    )(*pieces, theirs, numbers, begun, early, other_matrix, held, outflow, factors)


def per_device(*args):
    row_blocks, regions = args[0].shape[:2]
    paired = lax.axis_size("cell") == 2 and lax.axis_size("col") == 2
    paired = paired and row_blocks % 2 == 0 and row_blocks * args[0].shape[2] <= 2 * args[4].shape[0]
    return (paired_step if paired else general_step)(*args)


def solution(mesh):
    placed = (
        P(("job", "blk", "cell"), None, None, None, None),
        P(("job", "blk", "cell"), None, None),
        P(("job", "blk", "cell"), None, None, None, None),
        P(("job", "blk", "cell"), None, None),
        P("col", None, ("job", "blk", "cell")),
        P("col", None, ("job", "blk", "cell")),
        P("col"),
        P(("job", "blk", "cell")),
        P(None, ("job", "blk", "cell")),
    )
    return jax.shard_map(
        per_device,
        mesh=mesh,
        in_specs=placed,
        out_specs=(P("col", None, ("job", "blk", "cell")), P("col", None, ("job", "blk", "cell"))),
        check_vma=False,
    )
```

```python
import functools

import jax
import jax.numpy as jnp
from jax import lax
from jax.experimental import pallas as pl
from jax.experimental.pallas import tpu as pltpu
from jax.sharding import PartitionSpec as P

NT = (((1,), (1,)), ((), ()))
NN = (((1,), (0,)), ((), ()))
VMEM = pl.BlockSpec(memory_space=pltpu.VMEM)
SMEM = pl.BlockSpec(memory_space=pltpu.SMEM)
ANY = pl.BlockSpec(memory_space=pl.ANY)
STACK = 5_000_000
JOIN = 10_000_000
SMALL = 1_000
NEXT = 3_000_000
MAIN = 1000000
LAST = 8_000_000


def halves(count):
    steps = []
    while count > 1:
        count //= 2
        steps.append(count)
    return steps


def swapped(array, axis, distance):
    return lax.ppermute(array, axis, [(i, i ^ distance) for i in range(lax.axis_size(axis))])


def block_kernel(offsets, cols_ref, place_ref, held_ref, slab_ref, out_ref):
    row_blocks, _, slots = slab_ref.shape[:3]
    own_region, own_cell = place_ref[0], place_ref[1]
    for row in range(row_blocks):
        total = jnp.zeros(out_ref.shape[1:], jnp.float32)
        for piece, offset in enumerate(offsets):
            region = own_region ^ offset
            for slot in range(slots):
                column = cols_ref[row, region, slot]
                side = lax.div(column, row_blocks) ^ own_cell
                block = held_ref[side, piece, lax.rem(column, row_blocks)]
                total += lax.dot_general(
                    block, slab_ref[row, region, slot], NT, preferred_element_type=jnp.float32
                )
        out_ref[row] = total.astype(out_ref.dtype)


def block_product(slab, cols, place, held, offsets, dtype):
    row_blocks, block_size = slab.shape[0], slab.shape[-1]
    rows = held.shape[-2]
    return pl.pallas_call(
        functools.partial(block_kernel, offsets),
        out_shape=jax.ShapeDtypeStruct((row_blocks, rows, block_size), dtype),
        in_specs=[SMEM, SMEM, VMEM, VMEM],
        out_specs=VMEM,
        compiler_params=pltpu.CompilerParams(vmem_limit_bytes=32 * 1024 * 1024),
        cost_estimate=pl.CostEstimate(
            flops=2 * rows * slab.size, bytes_accessed=2 * slab.size + 2 * held.size, transcendentals=0
        ),
    )(cols, place, held, slab)


def incidence_kernel(ends_ref, current_ref, matrix_ref, out_ref):
    blocks, _, block_size = out_ref.shape
    cells = ends_ref.shape[1]
    leaves, enters = ends_ref[0:1, :], ends_ref[1:2, :]
    current = current_ref[...]
    for block in range(blocks):
        panel = lax.broadcasted_iota(jnp.int32, (block_size, cells), 0) + block * block_size
        entry = (leaves == panel).astype(jnp.float32) - (enters == panel).astype(jnp.float32)
        entry = entry.astype(jnp.bfloat16)
        matrix_ref[block] = entry
        out_ref[block] = lax.dot_general(current, entry, NT, preferred_element_type=jnp.float32)


def incidence(ends, current, panels, block_size):
    cells = ends.shape[1]
    blocks = panels // block_size
    return pl.pallas_call(
        incidence_kernel,
        out_shape=(
            jax.ShapeDtypeStruct((blocks, block_size, cells), jnp.bfloat16),
            jax.ShapeDtypeStruct((blocks, current.shape[0], block_size), jnp.float32),
        ),
        in_specs=[VMEM, VMEM],
        out_specs=(VMEM, VMEM),
        compiler_params=pltpu.CompilerParams(vmem_limit_bytes=32 * 1024 * 1024),
        cost_estimate=pl.CostEstimate(
            flops=4 * panels * cells * current.shape[0], bytes_accessed=2 * panels * cells, transcendentals=0
        ),
    )(ends, current)


def drop_kernel(potential_ref, matrix_ref, base_ref, out_ref):
    total = base_ref[...]
    for block in range(matrix_ref.shape[0]):
        total += lax.dot_general(
            potential_ref[block], matrix_ref[block], NN, preferred_element_type=jnp.float32
        )
    out_ref[...] = total


def with_drop(potential, matrix, base):
    return pl.pallas_call(
        drop_kernel,
        out_shape=jax.ShapeDtypeStruct(base.shape, jnp.float32),
        in_specs=[VMEM, VMEM, VMEM],
        out_specs=VMEM,
        compiler_params=pltpu.CompilerParams(vmem_limit_bytes=32 * 1024 * 1024),
        cost_estimate=pl.CostEstimate(
            flops=2 * base.shape[0] * matrix.size, bytes_accessed=2 * matrix.size, transcendentals=0
        ),
    )(potential, matrix, base)


def turned(array):
    return jnp.stack([-array[:, 1], array[:, 0]], axis=1)


def general_step(p_blocks, p_cols, l_blocks, l_cols, charges, currents, omegas, resist, branch_ends):
    freq_count, _, share = charges.shape
    block_size = p_blocks.shape[-1]
    row_blocks = p_blocks.shape[0]
    rows = 2 * freq_count
    regions, cells = lax.axis_size("blk"), lax.axis_size("cell")
    region, cell = lax.axis_index("blk"), lax.axis_index("cell")
    place = jnp.stack([region, cell]).astype(jnp.int32)

    def blocked(array):
        return array.reshape(rows, row_blocks, block_size).transpose(1, 0, 2)

    def flat(array):
        return array.transpose(1, 0, 2).reshape(rows, share)

    held = jnp.stack([blocked(charges), blocked(turned(currents))])[:, None]
    offsets = [0]
    for step in halves(regions):
        held = jnp.concatenate([held, swapped(held, "blk", step)], axis=1)
        offsets = offsets + [o ^ step for o in offsets]

    local = ((branch_ends // share) ^ cell) * share + branch_ends % share
    matrix, outflow = incidence(local, currents.reshape(rows, share), cells * share, block_size)
    outflow = outflow.reshape(cells, row_blocks, rows, block_size)

    charge_all, current_all = held[0][None], held[1][None]
    for step in reversed(halves(cells)):
        charge_all = jnp.concatenate([charge_all, swapped(charge_all, "cell", step)], axis=0)
    potential = block_product(p_blocks, p_cols, place, charge_all, offsets, jnp.bfloat16)
    for step in reversed(halves(cells)):
        away = [o for o in range(cells) if o & step and not o & (step - 1)]
        kept = [o - step for o in away]
        sums = jnp.stack([outflow[o] for o in away]).astype(jnp.bfloat16)
        flat_current = current_all.reshape(-1, rows, block_size)
        message = jnp.concatenate([flat_current, sums.reshape(-1, rows, block_size)], axis=0)
        message = swapped(message, "cell", step)
        got = message[: flat_current.shape[0]].reshape(current_all.shape)
        more = message[flat_current.shape[0] :].reshape(sums.shape).astype(jnp.float32)
        current_all = jnp.concatenate([current_all, got], axis=0)
        for position, o in enumerate(kept):
            outflow = outflow.at[o].add(more[position])
    potential_all = potential[None]
    for step in reversed(halves(cells)):
        potential_all = jnp.concatenate([potential_all, swapped(potential_all, "cell", step)], axis=0)
    flux_turned = block_product(l_blocks, l_cols, place, current_all, offsets, jnp.float32)

    scale = jnp.repeat(omegas, 2)[:, None]
    base = resist * currents.reshape(rows, share).astype(jnp.float32) + scale * flat(flux_turned)
    cell_rows = with_drop(potential_all.reshape(-1, rows, block_size), matrix, base)
    panel_rows = flat(outflow[0]) + scale * turned(charges).reshape(rows, share).astype(jnp.float32)
    return (cell_rows.reshape(freq_count, 2, share), panel_rows.reshape(freq_count, 2, share))


def back(regions, move):
    own = lax.axis_index("blk")
    if move == 0:
        return own
    targets = region_moves(regions)[move - 1]
    return sum(jnp.where(own == target, source, 0) for source, target in enumerate(targets))


def region_moves(regions):
    if regions == 4:
        return [[2, 3, 0, 1], [3, 2, 1, 0], [1, 0, 3, 2]]
    return [[(place + shift) % regions for place in range(regions)] for shift in range(1, regions)]


def turned_rows(array):
    rows = array.shape[0]
    odd = lax.broadcasted_iota(jnp.int32, array.shape, 0) & 1
    return jnp.where(odd == 0, -pltpu.roll(array, rows - 1, 0), pltpu.roll(array, 1, 0))


def row_scale(omega_ref, rows):
    shape = (rows, omega_ref.shape[1])
    same = lax.broadcasted_iota(jnp.int32, shape, 0) >> 1 == lax.broadcasted_iota(jnp.int32, shape, 1)
    return jnp.sum(jnp.where(same, omega_ref[...], 0.0), axis=1, keepdims=True)


def lanes(blocks):
    return jnp.concatenate(blocks, axis=1)


def pair_dot(held_ref, positions, slabs):
    return lax.dot_general(
        lanes([held_ref[position] for position in positions]), lanes(slabs), NT, preferred_element_type=jnp.float32
    )


def region_terms(regions, move, table_ref, held_ref, p_ref, l_ref, row):
    region = back(regions, move)
    slots = range(p_ref.shape[2])
    return tuple(
        pair_dot(
            held_ref.at[kind],
            [table_ref[kind, move, row, slot, 0] for slot in slots],
            [slab_ref[row, region, slot] for slot in slots],
        )
        for kind, slab_ref in enumerate((p_ref, l_ref))
    )


def outflow_terms(side, chosen, ends_ref, current_ref, matrix_ref, store):
    block_size = matrix_ref.shape[1]
    row_blocks = ends_ref.shape[1] // block_size
    leaves, enters = ends_ref[0:1, :], ends_ref[1:2, :]
    current = lanes([current_ref[1, block] for block in range(row_blocks)])
    for block in chosen:
        base = ((lax.axis_index("cell") ^ side) * row_blocks + block) * block_size
        panel = lax.broadcasted_iota(jnp.int32, (block_size, ends_ref.shape[1]), 0) + base
        entry = (leaves == panel).astype(jnp.float32) - (enters == panel).astype(jnp.float32)
        entry = entry.astype(jnp.bfloat16)
        matrix_ref[block] = entry
        store(block, lax.dot_general(current, entry, NT, preferred_element_type=jnp.float32))


def outflow_kernel(message_ref, ends_ref, matrix_ref, outflow_ref):
    def store(block, sums):
        outflow_ref[block] = sums

    outflow_terms(0, range(matrix_ref.shape[0]), ends_ref, message_ref, matrix_ref, store)


def first_kernel(
    regions, held_ref, p_ref, l_ref, p_cols_ref, l_cols_ref, omega_ref, resist_ref, ends_ref, part_ref, sums_ref,
    factor_ref, table_ref, potential_ref, flux_ref, early_ref, matrix_ref, own_matrix_ref, outflow_ref, numbers_ref,
):
    row_blocks, rows, block_size = potential_ref.shape
    slots = p_ref.shape[2]
    cell = lax.axis_index("cell")
    shape = table_ref.shape[2:]
    lane = lax.broadcasted_iota(jnp.int32, shape, 2)
    numbers = jnp.zeros(shape, jnp.float32)
    for kind, cols_ref in enumerate((p_cols_ref, l_cols_ref)):
        columns = cols_ref[...].astype(jnp.float32)
        place = lax.broadcasted_iota(jnp.int32, columns.shape, 2)
        for move in range(regions):
            column = jnp.sum(jnp.where(place == back(regions, move), columns, 0.0), axis=2, keepdims=True)
            column = jnp.broadcast_to(column, shape)
            other = jnp.where(column < row_blocks, column + row_blocks, column - row_blocks)
            table_ref[kind, move] = jnp.where(cell == 0, column, other).astype(jnp.int32)
            if kind == 0:
                numbers = jnp.where(lane == move, jnp.where(cell == 0, other, column), numbers)
    numbers_ref[...] = jnp.zeros_like(numbers_ref)
    for row in range(row_blocks):
        numbers_ref[row * slots : (row + 1) * slots, :] = numbers[row]
    early_ref[2 * row_blocks] = numbers_ref[...].astype(jnp.bfloat16)

    def store(block, sums):
        early_ref[row_blocks + block] = sums.astype(jnp.bfloat16)

    def store_own(block, sums):
        outflow_ref[block] = sums

    done = part_ref.shape[0]
    own_matrix_ref[:done] = part_ref[...]
    outflow_ref[:done] = sums_ref[...]
    outflow_terms(0, range(done, row_blocks), ends_ref, held_ref, own_matrix_ref, store_own)
    outflow_terms(1, range(row_blocks), ends_ref, held_ref, matrix_ref, store)
    for row in range(row_blocks):
        potential, flux = region_terms(regions, 0, table_ref, held_ref, p_ref, l_ref, row)
        potential_ref[row], flux_ref[row] = potential, flux
        early_ref[row] = potential.astype(jnp.bfloat16)
    factor_ref[0] = jnp.broadcast_to(row_scale(omega_ref, rows), (rows, block_size))
    for row in range(row_blocks):
        columns = slice(row * block_size, (row + 1) * block_size)
        factor_ref[1 + row] = jnp.broadcast_to(resist_ref[:, columns], (rows, block_size))


def next_kernel(
    regions, move, table_ref, held_ref, p_ref, l_ref, p_in_ref, f_in_ref, matrix_ref, potential_ref, flux_ref
):
    del matrix_ref
    for row in range(potential_ref.shape[0]):
        potential, flux = region_terms(regions, move, table_ref, held_ref, p_ref, l_ref, row)
        potential_ref[row], flux_ref[row] = p_in_ref[row] + potential, f_in_ref[row] + flux


def stack_kernel(charge_ref, current_ref, out_ref):
    out_ref[0] = charge_ref[...]
    out_ref[1] = current_ref[...]


def send_kernel(regions, p_ref, after_ref, out_ref):
    del after_ref
    half = out_ref.shape[1]
    for move in range(1, regions):
        for row in range(half):
            out_ref[move - 1, row] = p_ref[lax.axis_index("col") * half + row, back(regions, move)]


def join_kernel(own_ref, other_ref, out_ref):
    blocks = own_ref.shape[1]
    for kind in range(own_ref.shape[0]):
        out_ref[kind, :blocks] = own_ref[kind]
        out_ref[kind, blocks:] = other_ref[kind]


def store_rows(out_ref, columns, array):
    for freq in range(out_ref.shape[0]):
        out_ref[freq, :, columns] = array[2 * freq : 2 * freq + 2]


def other_drop(part, slab_ref, numbers_ref, early_ref, piece_refs, matrix_ref):
    half, slots = slab_ref.shape[1:3]
    start = (lax.axis_index("col") ^ part) * half
    rows = []
    for position in range(half):
        row = start + position
        total = early_ref[row].astype(jnp.float32)
        for at, piece_ref in enumerate(piece_refs):
            total += pair_dot(
                piece_ref.at[0],
                [numbers_ref[row * slots + slot, at + 1] for slot in range(slots)],
                [slab_ref[at, position, slot] for slot in range(slots)],
            )
        rows.append(total.astype(jnp.bfloat16))
    matrix = matrix_ref[pl.ds(start, half)].reshape(half * matrix_ref.shape[1], -1)
    return lax.dot_general(lanes(rows), matrix, NN, preferred_element_type=jnp.float32)


def main_kernel(regions, *refs):
    piece_refs = refs[: regions - 1]
    (mine_ref, table_ref, p_ref, l_ref, p_in_ref, f_in_ref, early_ref, matrix_ref, other_matrix_ref, held_ref,
     factor_ref, out_ref, numbers_ref) = refs[regions - 1 :]
    row_blocks, _, block_size = p_in_ref.shape
    numbers_ref[...] = early_ref[2 * row_blocks].astype(jnp.float32).astype(jnp.int32)
    potentials, fluxes = [], []
    for row in range(row_blocks):
        potential, flux = region_terms(regions, regions - 1, table_ref, piece_refs[-1], p_ref, l_ref, row)
        potentials.append((p_in_ref[row] + potential).astype(jnp.bfloat16))
        fluxes.append(f_in_ref[row] + flux)
    drop = other_drop(0, mine_ref, numbers_ref, early_ref, piece_refs, other_matrix_ref)
    matrix = matrix_ref[...].reshape(row_blocks * block_size, -1)
    drop += lax.dot_general(lanes(potentials), matrix, NN, preferred_element_type=jnp.float32)
    for row in range(row_blocks):
        columns = slice(row * block_size, (row + 1) * block_size)
        current = held_ref[1, row].astype(jnp.float32)
        flux = factor_ref[0] * turned_rows(fluxes[row])
        out_ref[:, columns] = factor_ref[1 + row] * current + flux + drop[:, columns]


def last_kernel(regions, *refs):
    piece_refs = refs[: regions - 1]
    (theirs_ref, numbers_ref, begun_ref, early_ref, matrix_ref, held_ref, outflow_ref, factor_ref,
     cell_ref, panel_ref) = refs[regions - 1 :]
    row_blocks, _, block_size = outflow_ref.shape
    total = begun_ref[...] + other_drop(1, theirs_ref, numbers_ref, early_ref, piece_refs, matrix_ref)
    for row in range(row_blocks):
        columns = slice(row * block_size, (row + 1) * block_size)
        store_rows(cell_ref, columns, total[:, columns])
        outflow = outflow_ref[row] + early_ref[row_blocks + row].astype(jnp.float32)
        charge = factor_ref[0] * turned_rows(held_ref[0, row].astype(jnp.float32))
        store_rows(panel_ref, columns, outflow + charge)


def kernel_call(body, out_shape, memories, weight, scratch=()):
    many = isinstance(out_shape, tuple)
    return pl.pallas_call(
        body,
        out_shape=out_shape,
        in_specs=[{"v": VMEM, "a": ANY}[m] for m in memories],
        out_specs=tuple(VMEM for _ in out_shape) if many else VMEM,
        scratch_shapes=scratch,
        compiler_params=pltpu.CompilerParams(vmem_limit_bytes=16 * 1024 * 1024),
        cost_estimate=pl.CostEstimate(flops=weight * 1000, bytes_accessed=4_000_000, transcendentals=0),
    )


def paired_step(p_blocks, p_cols, l_blocks, l_cols, charges, currents, omegas, resist, branch_ends):
    freq_count, _, share = charges.shape
    block_size = p_blocks.shape[-1]
    row_blocks = p_blocks.shape[0]
    rows = 2 * freq_count
    regions = lax.axis_size("blk")

    def blocked(array):
        return array.reshape(rows, row_blocks, block_size).transpose(1, 0, 2)

    message = kernel_call(
        stack_kernel, jax.ShapeDtypeStruct((2, row_blocks, rows, block_size), jnp.bfloat16), "vv", STACK
    )(blocked(charges), blocked(currents))
    held = kernel_call(
        join_kernel, jax.ShapeDtypeStruct((2, 2 * row_blocks, rows, block_size), jnp.bfloat16), "vv", JOIN
    )(message, swapped(message, "cell", 1))

    totals = jax.ShapeDtypeStruct((row_blocks, rows, block_size), jnp.float32)
    matrix_shape = jax.ShapeDtypeStruct((row_blocks, block_size, share), jnp.bfloat16)
    done = row_blocks - 1
    part, sums = kernel_call(
        outflow_kernel,
        (
            jax.ShapeDtypeStruct((done, block_size, share), jnp.bfloat16),
            jax.ShapeDtypeStruct((done, rows, block_size), jnp.float32),
        ),
        "vv",
        SMALL,
    )(message, branch_ends)
    half_shape = jax.ShapeDtypeStruct((regions - 1, row_blocks // 2) + p_blocks.shape[2:], jnp.bfloat16)
    sent = kernel_call(functools.partial(send_kernel, regions), half_shape, "va", SMALL)(p_blocks, sums)
    mine = swapped(sent, "cell", 1)
    theirs = swapped(mine, "col", 1)

    pieces = [lax.ppermute(held, "blk", list(enumerate(targets))) for targets in region_moves(regions)]

    slots = p_cols.shape[2]
    factors, table, potential, flux, early, other_matrix, matrix, outflow = kernel_call(
        functools.partial(first_kernel, regions),
        (
            jax.ShapeDtypeStruct((1 + row_blocks, rows, block_size), jnp.float32),
            jax.ShapeDtypeStruct((2, regions, row_blocks, slots, block_size), jnp.int32),
            totals,
            totals,
            jax.ShapeDtypeStruct((2 * row_blocks + 1, rows, block_size), jnp.bfloat16),
            matrix_shape,
            matrix_shape,
            totals,
        ),
        "vvvvvvvvvv",
        SMALL,
        [pltpu.VMEM((rows, block_size), jnp.float32)],
    )(
        held, p_blocks, l_blocks, p_cols.transpose(0, 2, 1), l_cols.transpose(0, 2, 1), omegas[None], resist[None],
        branch_ends, part, sums,
    )
    early = swapped(early, "cell", 1)
    for move, piece in enumerate(pieces[:-1], 1):
        potential, flux = kernel_call(
            functools.partial(next_kernel, regions, move), (totals, totals), "vvvvvvv", NEXT
        )(table, piece, p_blocks, l_blocks, potential, flux, matrix)

    numbers_shape = jax.ShapeDtypeStruct((rows, block_size), jnp.int32)
    begun, numbers = kernel_call(
        functools.partial(main_kernel, regions),
        (jax.ShapeDtypeStruct((rows, share), jnp.float32), numbers_shape),
        "v" * (10 + regions),
        MAIN,
    )(*pieces, mine, table, p_blocks, l_blocks, potential, flux, early, matrix, other_matrix, held, factors)
    result = jax.ShapeDtypeStruct(charges.shape, jnp.float32)
    return kernel_call(
        functools.partial(last_kernel, regions), (result, result), "v" * (7 + regions), LAST
    )(*pieces, theirs, numbers, begun, early, other_matrix, held, outflow, factors)


def per_device(*args):
    row_blocks, regions = args[0].shape[:2]
    paired = lax.axis_size("cell") == 2 and lax.axis_size("col") == 2
    paired = paired and row_blocks % 2 == 0 and row_blocks * args[0].shape[2] <= 2 * args[4].shape[0]
    return (paired_step if paired else general_step)(*args)


def solution(mesh):
    placed = (
        P(("job", "blk", "cell"), None, None, None, None),
        P(("job", "blk", "cell"), None, None),
        P(("job", "blk", "cell"), None, None, None, None),
        P(("job", "blk", "cell"), None, None),
        P("col", None, ("job", "blk", "cell")),
        P("col", None, ("job", "blk", "cell")),
        P("col"),
        P(("job", "blk", "cell")),
        P(None, ("job", "blk", "cell")),
    )
    return jax.shard_map(
        per_device,
        mesh=mesh,
        in_specs=placed,
        out_specs=(P("col", None, ("job", "blk", "cell")), P("col", None, ("job", "blk", "cell"))),
        check_vma=False,
    )
```

```python
import functools

import jax
import jax.numpy as jnp
from jax import lax
from jax.experimental import pallas as pl
from jax.experimental.pallas import tpu as pltpu
from jax.sharding import PartitionSpec as P

NT = (((1,), (1,)), ((), ()))
NN = (((1,), (0,)), ((), ()))
VMEM = pl.BlockSpec(memory_space=pltpu.VMEM)
SMEM = pl.BlockSpec(memory_space=pltpu.SMEM)
ANY = pl.BlockSpec(memory_space=pl.ANY)
STACK = 5_000_000
JOIN = 10_000_000
SMALL = 1_000
NEXT = 3_000_000
MAIN = 1000000
LAST = 8_000_000


def halves(count):
    steps = []
    while count > 1:
        count //= 2
        steps.append(count)
    return steps


def swapped(array, axis, distance):
    return lax.ppermute(array, axis, [(i, i ^ distance) for i in range(lax.axis_size(axis))])


def block_kernel(offsets, cols_ref, place_ref, held_ref, slab_ref, out_ref):
    row_blocks, _, slots = slab_ref.shape[:3]
    own_region, own_cell = place_ref[0], place_ref[1]
    for row in range(row_blocks):
        total = jnp.zeros(out_ref.shape[1:], jnp.float32)
        for piece, offset in enumerate(offsets):
            region = own_region ^ offset
            for slot in range(slots):
                column = cols_ref[row, region, slot]
                side = lax.div(column, row_blocks) ^ own_cell
                block = held_ref[side, piece, lax.rem(column, row_blocks)]
                total += lax.dot_general(
                    block, slab_ref[row, region, slot], NT, preferred_element_type=jnp.float32
                )
        out_ref[row] = total.astype(out_ref.dtype)


def block_product(slab, cols, place, held, offsets, dtype):
    row_blocks, block_size = slab.shape[0], slab.shape[-1]
    rows = held.shape[-2]
    return pl.pallas_call(
        functools.partial(block_kernel, offsets),
        out_shape=jax.ShapeDtypeStruct((row_blocks, rows, block_size), dtype),
        in_specs=[SMEM, SMEM, VMEM, VMEM],
        out_specs=VMEM,
        compiler_params=pltpu.CompilerParams(vmem_limit_bytes=32 * 1024 * 1024),
        cost_estimate=pl.CostEstimate(
            flops=2 * rows * slab.size, bytes_accessed=2 * slab.size + 2 * held.size, transcendentals=0
        ),
    )(cols, place, held, slab)


def incidence_kernel(ends_ref, current_ref, matrix_ref, out_ref):
    blocks, _, block_size = out_ref.shape
    cells = ends_ref.shape[1]
    leaves, enters = ends_ref[0:1, :], ends_ref[1:2, :]
    current = current_ref[...]
    for block in range(blocks):
        panel = lax.broadcasted_iota(jnp.int32, (block_size, cells), 0) + block * block_size
        entry = (leaves == panel).astype(jnp.float32) - (enters == panel).astype(jnp.float32)
        entry = entry.astype(jnp.bfloat16)
        matrix_ref[block] = entry
        out_ref[block] = lax.dot_general(current, entry, NT, preferred_element_type=jnp.float32)


def incidence(ends, current, panels, block_size):
    cells = ends.shape[1]
    blocks = panels // block_size
    return pl.pallas_call(
        incidence_kernel,
        out_shape=(
            jax.ShapeDtypeStruct((blocks, block_size, cells), jnp.bfloat16),
            jax.ShapeDtypeStruct((blocks, current.shape[0], block_size), jnp.float32),
        ),
        in_specs=[VMEM, VMEM],
        out_specs=(VMEM, VMEM),
        compiler_params=pltpu.CompilerParams(vmem_limit_bytes=32 * 1024 * 1024),
        cost_estimate=pl.CostEstimate(
            flops=4 * panels * cells * current.shape[0], bytes_accessed=2 * panels * cells, transcendentals=0
        ),
    )(ends, current)


def drop_kernel(potential_ref, matrix_ref, base_ref, out_ref):
    total = base_ref[...]
    for block in range(matrix_ref.shape[0]):
        total += lax.dot_general(
            potential_ref[block], matrix_ref[block], NN, preferred_element_type=jnp.float32
        )
    out_ref[...] = total


def with_drop(potential, matrix, base):
    return pl.pallas_call(
        drop_kernel,
        out_shape=jax.ShapeDtypeStruct(base.shape, jnp.float32),
        in_specs=[VMEM, VMEM, VMEM],
        out_specs=VMEM,
        compiler_params=pltpu.CompilerParams(vmem_limit_bytes=32 * 1024 * 1024),
        cost_estimate=pl.CostEstimate(
            flops=2 * base.shape[0] * matrix.size, bytes_accessed=2 * matrix.size, transcendentals=0
        ),
    )(potential, matrix, base)


def turned(array):
    return jnp.stack([-array[:, 1], array[:, 0]], axis=1)


def general_step(p_blocks, p_cols, l_blocks, l_cols, charges, currents, omegas, resist, branch_ends):
    freq_count, _, share = charges.shape
    block_size = p_blocks.shape[-1]
    row_blocks = p_blocks.shape[0]
    rows = 2 * freq_count
    regions, cells = lax.axis_size("blk"), lax.axis_size("cell")
    region, cell = lax.axis_index("blk"), lax.axis_index("cell")
    place = jnp.stack([region, cell]).astype(jnp.int32)

    def blocked(array):
        return array.reshape(rows, row_blocks, block_size).transpose(1, 0, 2)

    def flat(array):
        return array.transpose(1, 0, 2).reshape(rows, share)

    held = jnp.stack([blocked(charges), blocked(turned(currents))])[:, None]
    offsets = [0]
    for step in halves(regions):
        held = jnp.concatenate([held, swapped(held, "blk", step)], axis=1)
        offsets = offsets + [o ^ step for o in offsets]

    local = ((branch_ends // share) ^ cell) * share + branch_ends % share
    matrix, outflow = incidence(local, currents.reshape(rows, share), cells * share, block_size)
    outflow = outflow.reshape(cells, row_blocks, rows, block_size)

    charge_all, current_all = held[0][None], held[1][None]
    for step in reversed(halves(cells)):
        charge_all = jnp.concatenate([charge_all, swapped(charge_all, "cell", step)], axis=0)
    potential = block_product(p_blocks, p_cols, place, charge_all, offsets, jnp.bfloat16)
    for step in reversed(halves(cells)):
        away = [o for o in range(cells) if o & step and not o & (step - 1)]
        kept = [o - step for o in away]
        sums = jnp.stack([outflow[o] for o in away]).astype(jnp.bfloat16)
        flat_current = current_all.reshape(-1, rows, block_size)
        message = jnp.concatenate([flat_current, sums.reshape(-1, rows, block_size)], axis=0)
        message = swapped(message, "cell", step)
        got = message[: flat_current.shape[0]].reshape(current_all.shape)
        more = message[flat_current.shape[0] :].reshape(sums.shape).astype(jnp.float32)
        current_all = jnp.concatenate([current_all, got], axis=0)
        for position, o in enumerate(kept):
            outflow = outflow.at[o].add(more[position])
    potential_all = potential[None]
    for step in reversed(halves(cells)):
        potential_all = jnp.concatenate([potential_all, swapped(potential_all, "cell", step)], axis=0)
    flux_turned = block_product(l_blocks, l_cols, place, current_all, offsets, jnp.float32)

    scale = jnp.repeat(omegas, 2)[:, None]
    base = resist * currents.reshape(rows, share).astype(jnp.float32) + scale * flat(flux_turned)
    cell_rows = with_drop(potential_all.reshape(-1, rows, block_size), matrix, base)
    panel_rows = flat(outflow[0]) + scale * turned(charges).reshape(rows, share).astype(jnp.float32)
    return (cell_rows.reshape(freq_count, 2, share), panel_rows.reshape(freq_count, 2, share))


def back(regions, move):
    own = lax.axis_index("blk")
    if move == 0:
        return own
    targets = region_moves(regions)[move - 1]
    return sum(jnp.where(own == target, source, 0) for source, target in enumerate(targets))


def region_moves(regions):
    if regions == 4:
        return [[2, 3, 0, 1], [3, 2, 1, 0], [1, 0, 3, 2]]
    return [[(place + shift) % regions for place in range(regions)] for shift in range(1, regions)]


def turned_rows(array):
    rows = array.shape[0]
    odd = lax.broadcasted_iota(jnp.int32, array.shape, 0) & 1
    return jnp.where(odd == 0, -pltpu.roll(array, rows - 1, 0), pltpu.roll(array, 1, 0))


def row_scale(omega_ref, rows):
    shape = (rows, omega_ref.shape[1])
    same = lax.broadcasted_iota(jnp.int32, shape, 0) >> 1 == lax.broadcasted_iota(jnp.int32, shape, 1)
    return jnp.sum(jnp.where(same, omega_ref[...], 0.0), axis=1, keepdims=True)


def lanes(blocks):
    return jnp.concatenate(blocks, axis=1)


def pair_dot(held_ref, positions, slabs):
    return lax.dot_general(
        lanes([held_ref[position] for position in positions]), lanes(slabs), NT, preferred_element_type=jnp.float32
    )


def region_terms(regions, move, table_ref, held_ref, p_ref, l_ref, row):
    region = back(regions, move)
    slots = range(p_ref.shape[2])
    return tuple(
        pair_dot(
            held_ref.at[kind],
            [table_ref[kind, move, row, slot, 0] for slot in slots],
            [slab_ref[row, region, slot] for slot in slots],
        )
        for kind, slab_ref in enumerate((p_ref, l_ref))
    )


def outflow_terms(side, chosen, ends_ref, current_ref, matrix_ref, store):
    block_size = matrix_ref.shape[1]
    row_blocks = ends_ref.shape[1] // block_size
    leaves, enters = ends_ref[0:1, :], ends_ref[1:2, :]
    current = lanes([current_ref[1, block] for block in range(row_blocks)])
    for block in chosen:
        base = ((lax.axis_index("cell") ^ side) * row_blocks + block) * block_size
        panel = lax.broadcasted_iota(jnp.int32, (block_size, ends_ref.shape[1]), 0) + base
        entry = (leaves == panel).astype(jnp.float32) - (enters == panel).astype(jnp.float32)
        entry = entry.astype(jnp.bfloat16)
        matrix_ref[block] = entry
        store(block, lax.dot_general(current, entry, NT, preferred_element_type=jnp.float32))


def outflow_kernel(message_ref, ends_ref, matrix_ref, outflow_ref):
    def store(block, sums):
        outflow_ref[block] = sums

    outflow_terms(0, range(matrix_ref.shape[0]), ends_ref, message_ref, matrix_ref, store)


def first_kernel(
    regions, held_ref, p_ref, l_ref, p_cols_ref, l_cols_ref, omega_ref, resist_ref, ends_ref, part_ref, sums_ref,
    factor_ref, table_ref, potential_ref, flux_ref, early_ref, matrix_ref, own_matrix_ref, outflow_ref, numbers_ref,
):
    row_blocks, rows, block_size = potential_ref.shape
    slots = p_ref.shape[2]
    cell = lax.axis_index("cell")
    shape = table_ref.shape[2:]
    lane = lax.broadcasted_iota(jnp.int32, shape, 2)
    numbers = jnp.zeros(shape, jnp.float32)
    for kind, cols_ref in enumerate((p_cols_ref, l_cols_ref)):
        columns = cols_ref[...].astype(jnp.float32)
        place = lax.broadcasted_iota(jnp.int32, columns.shape, 2)
        for move in range(regions):
            column = jnp.sum(jnp.where(place == back(regions, move), columns, 0.0), axis=2, keepdims=True)
            column = jnp.broadcast_to(column, shape)
            other = jnp.where(column < row_blocks, column + row_blocks, column - row_blocks)
            table_ref[kind, move] = jnp.where(cell == 0, column, other).astype(jnp.int32)
            if kind == 0:
                numbers = jnp.where(lane == move, jnp.where(cell == 0, other, column), numbers)
    numbers_ref[...] = jnp.zeros_like(numbers_ref)
    for row in range(row_blocks):
        numbers_ref[row * slots : (row + 1) * slots, :] = numbers[row]
    early_ref[2 * row_blocks] = numbers_ref[...].astype(jnp.bfloat16)

    def store(block, sums):
        early_ref[row_blocks + block] = sums.astype(jnp.bfloat16)

    def store_own(block, sums):
        outflow_ref[block] = sums

    done = part_ref.shape[0]
    own_matrix_ref[:done] = part_ref[...]
    outflow_ref[:done] = sums_ref[...]
    outflow_terms(0, range(done, row_blocks), ends_ref, held_ref, own_matrix_ref, store_own)
    outflow_terms(1, range(row_blocks), ends_ref, held_ref, matrix_ref, store)
    for row in range(row_blocks):
        potential, flux = region_terms(regions, 0, table_ref, held_ref, p_ref, l_ref, row)
        potential_ref[row], flux_ref[row] = potential, flux
        early_ref[row] = potential.astype(jnp.bfloat16)
    factor_ref[0] = jnp.broadcast_to(row_scale(omega_ref, rows), (rows, block_size))
    for row in range(row_blocks):
        columns = slice(row * block_size, (row + 1) * block_size)
        factor_ref[1 + row] = jnp.broadcast_to(resist_ref[:, columns], (rows, block_size))


def next_kernel(
    regions, move, table_ref, held_ref, p_ref, l_ref, p_in_ref, f_in_ref, matrix_ref, potential_ref, flux_ref
):
    del matrix_ref
    for row in range(potential_ref.shape[0]):
        potential, flux = region_terms(regions, move, table_ref, held_ref, p_ref, l_ref, row)
        potential_ref[row], flux_ref[row] = p_in_ref[row] + potential, f_in_ref[row] + flux


def stack_kernel(charge_ref, current_ref, out_ref):
    out_ref[0] = charge_ref[...]
    out_ref[1] = current_ref[...]


def send_kernel(regions, p_ref, after_ref, out_ref):
    del after_ref
    half = out_ref.shape[1]
    for move in range(1, regions):
        for row in range(half):
            out_ref[move - 1, row] = p_ref[lax.axis_index("col") * half + row, back(regions, move)]


def join_kernel(own_ref, other_ref, out_ref):
    blocks = own_ref.shape[1]
    for kind in range(own_ref.shape[0]):
        out_ref[kind, :blocks] = own_ref[kind]
        out_ref[kind, blocks:] = other_ref[kind]


def store_rows(out_ref, columns, array):
    for freq in range(out_ref.shape[0]):
        out_ref[freq, :, columns] = array[2 * freq : 2 * freq + 2]


def other_drop(part, slab_ref, numbers_ref, early_ref, piece_refs, matrix_ref):
    half, slots = slab_ref.shape[1:3]
    start = (lax.axis_index("col") ^ part) * half
    rows = []
    for position in range(half):
        row = start + position
        total = early_ref[row].astype(jnp.float32)
        for at, piece_ref in enumerate(piece_refs):
            total += pair_dot(
                piece_ref.at[0],
                [numbers_ref[row * slots + slot, at + 1] for slot in range(slots)],
                [slab_ref[at, position, slot] for slot in range(slots)],
            )
        rows.append(total.astype(jnp.bfloat16))
    matrix = matrix_ref[pl.ds(start, half)].reshape(half * matrix_ref.shape[1], -1)
    return lax.dot_general(lanes(rows), matrix, NN, preferred_element_type=jnp.float32)


def main_kernel(regions, *refs):
    piece_refs = refs[: regions - 1]
    (mine_ref, table_ref, p_ref, l_ref, p_in_ref, f_in_ref, early_ref, matrix_ref, other_matrix_ref, held_ref,
     factor_ref, out_ref, numbers_ref) = refs[regions - 1 :]
    row_blocks, _, block_size = p_in_ref.shape
    numbers_ref[...] = early_ref[2 * row_blocks].astype(jnp.float32).astype(jnp.int32)
    potentials, fluxes = [], []
    for row in range(row_blocks):
        potential, flux = region_terms(regions, regions - 1, table_ref, piece_refs[-1], p_ref, l_ref, row)
        potentials.append((p_in_ref[row] + potential).astype(jnp.bfloat16))
        fluxes.append(f_in_ref[row] + flux)
    drop = other_drop(0, mine_ref, numbers_ref, early_ref, piece_refs, other_matrix_ref)
    matrix = matrix_ref[...].reshape(row_blocks * block_size, -1)
    drop += lax.dot_general(lanes(potentials), matrix, NN, preferred_element_type=jnp.float32)
    for row in range(row_blocks):
        columns = slice(row * block_size, (row + 1) * block_size)
        current = held_ref[1, row].astype(jnp.float32)
        flux = factor_ref[0] * turned_rows(fluxes[row])
        out_ref[:, columns] = factor_ref[1 + row] * current + flux + drop[:, columns]


def last_kernel(regions, *refs):
    piece_refs = refs[: regions - 1]
    (theirs_ref, numbers_ref, begun_ref, early_ref, matrix_ref, held_ref, outflow_ref, factor_ref,
     cell_ref, panel_ref) = refs[regions - 1 :]
    row_blocks, _, block_size = outflow_ref.shape
    total = begun_ref[...] + other_drop(1, theirs_ref, numbers_ref, early_ref, piece_refs, matrix_ref)
    for row in range(row_blocks):
        columns = slice(row * block_size, (row + 1) * block_size)
        store_rows(cell_ref, columns, total[:, columns])
        outflow = outflow_ref[row] + early_ref[row_blocks + row].astype(jnp.float32)
        charge = factor_ref[0] * turned_rows(held_ref[0, row].astype(jnp.float32))
        store_rows(panel_ref, columns, outflow + charge)


def kernel_call(body, out_shape, memories, weight, scratch=()):
    many = isinstance(out_shape, tuple)
    return pl.pallas_call(
        body,
        out_shape=out_shape,
        in_specs=[{"v": VMEM, "a": ANY}[m] for m in memories],
        out_specs=tuple(VMEM for _ in out_shape) if many else VMEM,
        scratch_shapes=scratch,
        compiler_params=pltpu.CompilerParams(vmem_limit_bytes=16 * 1024 * 1024),
        cost_estimate=pl.CostEstimate(flops=weight * 1000, bytes_accessed=4_000_000, transcendentals=0),
    )


def paired_step(p_blocks, p_cols, l_blocks, l_cols, charges, currents, omegas, resist, branch_ends):
    freq_count, _, share = charges.shape
    block_size = p_blocks.shape[-1]
    row_blocks = p_blocks.shape[0]
    rows = 2 * freq_count
    regions = lax.axis_size("blk")

    def blocked(array):
        return array.reshape(rows, row_blocks, block_size).transpose(1, 0, 2)

    message = kernel_call(
        stack_kernel, jax.ShapeDtypeStruct((2, row_blocks, rows, block_size), jnp.bfloat16), "vv", STACK
    )(blocked(charges), blocked(currents))
    held = kernel_call(
        join_kernel, jax.ShapeDtypeStruct((2, 2 * row_blocks, rows, block_size), jnp.bfloat16), "vv", JOIN
    )(message, swapped(message, "cell", 1))

    totals = jax.ShapeDtypeStruct((row_blocks, rows, block_size), jnp.float32)
    matrix_shape = jax.ShapeDtypeStruct((row_blocks, block_size, share), jnp.bfloat16)
    done = row_blocks // 2
    part, sums = kernel_call(
        outflow_kernel,
        (
            jax.ShapeDtypeStruct((done, block_size, share), jnp.bfloat16),
            jax.ShapeDtypeStruct((done, rows, block_size), jnp.float32),
        ),
        "vv",
        SMALL,
    )(message, branch_ends)
    half_shape = jax.ShapeDtypeStruct((regions - 1, row_blocks // 2) + p_blocks.shape[2:], jnp.bfloat16)
    sent = kernel_call(functools.partial(send_kernel, regions), half_shape, "va", SMALL)(p_blocks, sums)
    mine = swapped(sent, "cell", 1)
    theirs = swapped(mine, "col", 1)

    pieces = [lax.ppermute(held, "blk", list(enumerate(targets))) for targets in region_moves(regions)]

    slots = p_cols.shape[2]
    factors, table, potential, flux, early, other_matrix, matrix, outflow = kernel_call(
        functools.partial(first_kernel, regions),
        (
            jax.ShapeDtypeStruct((1 + row_blocks, rows, block_size), jnp.float32),
            jax.ShapeDtypeStruct((2, regions, row_blocks, slots, block_size), jnp.int32),
            totals,
            totals,
            jax.ShapeDtypeStruct((2 * row_blocks + 1, rows, block_size), jnp.bfloat16),
            matrix_shape,
            matrix_shape,
            totals,
        ),
        "vvvvvvvvvv",
        SMALL,
        [pltpu.VMEM((rows, block_size), jnp.float32)],
    )(
        held, p_blocks, l_blocks, p_cols.transpose(0, 2, 1), l_cols.transpose(0, 2, 1), omegas[None], resist[None],
        branch_ends, part, sums,
    )
    early = swapped(early, "cell", 1)
    for move, piece in enumerate(pieces[:-1], 1):
        potential, flux = kernel_call(
            functools.partial(next_kernel, regions, move), (totals, totals), "vvvvvvv", NEXT
        )(table, piece, p_blocks, l_blocks, potential, flux, matrix)

    numbers_shape = jax.ShapeDtypeStruct((rows, block_size), jnp.int32)
    begun, numbers = kernel_call(
        functools.partial(main_kernel, regions),
        (jax.ShapeDtypeStruct((rows, share), jnp.float32), numbers_shape),
        "v" * (10 + regions),
        MAIN,
    )(*pieces, mine, table, p_blocks, l_blocks, potential, flux, early, matrix, other_matrix, held, factors)
    result = jax.ShapeDtypeStruct(charges.shape, jnp.float32)
    return kernel_call(
        functools.partial(last_kernel, regions), (result, result), "v" * (7 + regions), LAST
    )(*pieces, theirs, numbers, begun, early, other_matrix, held, outflow, factors)


def per_device(*args):
    row_blocks, regions = args[0].shape[:2]
    paired = lax.axis_size("cell") == 2 and lax.axis_size("col") == 2
    paired = paired and row_blocks % 2 == 0 and row_blocks * args[0].shape[2] <= 2 * args[4].shape[0]
    return (paired_step if paired else general_step)(*args)


def solution(mesh):
    placed = (
        P(("job", "blk", "cell"), None, None, None, None),
        P(("job", "blk", "cell"), None, None),
        P(("job", "blk", "cell"), None, None, None, None),
        P(("job", "blk", "cell"), None, None),
        P("col", None, ("job", "blk", "cell")),
        P("col", None, ("job", "blk", "cell")),
        P("col"),
        P(("job", "blk", "cell")),
        P(None, ("job", "blk", "cell")),
    )
    return jax.shard_map(
        per_device,
        mesh=mesh,
        in_specs=placed,
        out_specs=(P("col", None, ("job", "blk", "cell")), P("col", None, ("job", "blk", "cell"))),
        check_vma=False,
    )
```

```python
import functools

import jax
import jax.numpy as jnp
from jax import lax
from jax.experimental import pallas as pl
from jax.experimental.pallas import tpu as pltpu
from jax.sharding import PartitionSpec as P

NT = (((1,), (1,)), ((), ()))
NN = (((1,), (0,)), ((), ()))
VMEM = pl.BlockSpec(memory_space=pltpu.VMEM)
SMEM = pl.BlockSpec(memory_space=pltpu.SMEM)
ANY = pl.BlockSpec(memory_space=pl.ANY)
STACK = 5_000_000
JOIN = 10_000_000
SMALL = 1_000
NEXT = 3_000_000
MAIN = 1000000
LAST = 8_000_000


def halves(count):
    steps = []
    while count > 1:
        count //= 2
        steps.append(count)
    return steps


def swapped(array, axis, distance):
    return lax.ppermute(array, axis, [(i, i ^ distance) for i in range(lax.axis_size(axis))])


def block_kernel(offsets, cols_ref, place_ref, held_ref, slab_ref, out_ref):
    row_blocks, _, slots = slab_ref.shape[:3]
    own_region, own_cell = place_ref[0], place_ref[1]
    for row in range(row_blocks):
        total = jnp.zeros(out_ref.shape[1:], jnp.float32)
        for piece, offset in enumerate(offsets):
            region = own_region ^ offset
            for slot in range(slots):
                column = cols_ref[row, region, slot]
                side = lax.div(column, row_blocks) ^ own_cell
                block = held_ref[side, piece, lax.rem(column, row_blocks)]
                total += lax.dot_general(
                    block, slab_ref[row, region, slot], NT, preferred_element_type=jnp.float32
                )
        out_ref[row] = total.astype(out_ref.dtype)


def block_product(slab, cols, place, held, offsets, dtype):
    row_blocks, block_size = slab.shape[0], slab.shape[-1]
    rows = held.shape[-2]
    return pl.pallas_call(
        functools.partial(block_kernel, offsets),
        out_shape=jax.ShapeDtypeStruct((row_blocks, rows, block_size), dtype),
        in_specs=[SMEM, SMEM, VMEM, VMEM],
        out_specs=VMEM,
        compiler_params=pltpu.CompilerParams(vmem_limit_bytes=32 * 1024 * 1024),
        cost_estimate=pl.CostEstimate(
            flops=2 * rows * slab.size, bytes_accessed=2 * slab.size + 2 * held.size, transcendentals=0
        ),
    )(cols, place, held, slab)


def incidence_kernel(ends_ref, current_ref, matrix_ref, out_ref):
    blocks, _, block_size = out_ref.shape
    cells = ends_ref.shape[1]
    leaves, enters = ends_ref[0:1, :], ends_ref[1:2, :]
    current = current_ref[...]
    for block in range(blocks):
        panel = lax.broadcasted_iota(jnp.int32, (block_size, cells), 0) + block * block_size
        entry = (leaves == panel).astype(jnp.float32) - (enters == panel).astype(jnp.float32)
        entry = entry.astype(jnp.bfloat16)
        matrix_ref[block] = entry
        out_ref[block] = lax.dot_general(current, entry, NT, preferred_element_type=jnp.float32)


def incidence(ends, current, panels, block_size):
    cells = ends.shape[1]
    blocks = panels // block_size
    return pl.pallas_call(
        incidence_kernel,
        out_shape=(
            jax.ShapeDtypeStruct((blocks, block_size, cells), jnp.bfloat16),
            jax.ShapeDtypeStruct((blocks, current.shape[0], block_size), jnp.float32),
        ),
        in_specs=[VMEM, VMEM],
        out_specs=(VMEM, VMEM),
        compiler_params=pltpu.CompilerParams(vmem_limit_bytes=32 * 1024 * 1024),
        cost_estimate=pl.CostEstimate(
            flops=4 * panels * cells * current.shape[0], bytes_accessed=2 * panels * cells, transcendentals=0
        ),
    )(ends, current)


def drop_kernel(potential_ref, matrix_ref, base_ref, out_ref):
    total = base_ref[...]
    for block in range(matrix_ref.shape[0]):
        total += lax.dot_general(
            potential_ref[block], matrix_ref[block], NN, preferred_element_type=jnp.float32
        )
    out_ref[...] = total


def with_drop(potential, matrix, base):
    return pl.pallas_call(
        drop_kernel,
        out_shape=jax.ShapeDtypeStruct(base.shape, jnp.float32),
        in_specs=[VMEM, VMEM, VMEM],
        out_specs=VMEM,
        compiler_params=pltpu.CompilerParams(vmem_limit_bytes=32 * 1024 * 1024),
        cost_estimate=pl.CostEstimate(
            flops=2 * base.shape[0] * matrix.size, bytes_accessed=2 * matrix.size, transcendentals=0
        ),
    )(potential, matrix, base)


def turned(array):
    return jnp.stack([-array[:, 1], array[:, 0]], axis=1)


def general_step(p_blocks, p_cols, l_blocks, l_cols, charges, currents, omegas, resist, branch_ends):
    freq_count, _, share = charges.shape
    block_size = p_blocks.shape[-1]
    row_blocks = p_blocks.shape[0]
    rows = 2 * freq_count
    regions, cells = lax.axis_size("blk"), lax.axis_size("cell")
    region, cell = lax.axis_index("blk"), lax.axis_index("cell")
    place = jnp.stack([region, cell]).astype(jnp.int32)

    def blocked(array):
        return array.reshape(rows, row_blocks, block_size).transpose(1, 0, 2)

    def flat(array):
        return array.transpose(1, 0, 2).reshape(rows, share)

    held = jnp.stack([blocked(charges), blocked(turned(currents))])[:, None]
    offsets = [0]
    for step in halves(regions):
        held = jnp.concatenate([held, swapped(held, "blk", step)], axis=1)
        offsets = offsets + [o ^ step for o in offsets]

    local = ((branch_ends // share) ^ cell) * share + branch_ends % share
    matrix, outflow = incidence(local, currents.reshape(rows, share), cells * share, block_size)
    outflow = outflow.reshape(cells, row_blocks, rows, block_size)

    charge_all, current_all = held[0][None], held[1][None]
    for step in reversed(halves(cells)):
        charge_all = jnp.concatenate([charge_all, swapped(charge_all, "cell", step)], axis=0)
    potential = block_product(p_blocks, p_cols, place, charge_all, offsets, jnp.bfloat16)
    for step in reversed(halves(cells)):
        away = [o for o in range(cells) if o & step and not o & (step - 1)]
        kept = [o - step for o in away]
        sums = jnp.stack([outflow[o] for o in away]).astype(jnp.bfloat16)
        flat_current = current_all.reshape(-1, rows, block_size)
        message = jnp.concatenate([flat_current, sums.reshape(-1, rows, block_size)], axis=0)
        message = swapped(message, "cell", step)
        got = message[: flat_current.shape[0]].reshape(current_all.shape)
        more = message[flat_current.shape[0] :].reshape(sums.shape).astype(jnp.float32)
        current_all = jnp.concatenate([current_all, got], axis=0)
        for position, o in enumerate(kept):
            outflow = outflow.at[o].add(more[position])
    potential_all = potential[None]
    for step in reversed(halves(cells)):
        potential_all = jnp.concatenate([potential_all, swapped(potential_all, "cell", step)], axis=0)
    flux_turned = block_product(l_blocks, l_cols, place, current_all, offsets, jnp.float32)

    scale = jnp.repeat(omegas, 2)[:, None]
    base = resist * currents.reshape(rows, share).astype(jnp.float32) + scale * flat(flux_turned)
    cell_rows = with_drop(potential_all.reshape(-1, rows, block_size), matrix, base)
    panel_rows = flat(outflow[0]) + scale * turned(charges).reshape(rows, share).astype(jnp.float32)
    return (cell_rows.reshape(freq_count, 2, share), panel_rows.reshape(freq_count, 2, share))


def back(regions, move):
    own = lax.axis_index("blk")
    if move == 0:
        return own
    targets = region_moves(regions)[move - 1]
    return sum(jnp.where(own == target, source, 0) for source, target in enumerate(targets))


def region_moves(regions):
    if regions == 4:
        return [[2, 3, 0, 1], [3, 2, 1, 0], [1, 0, 3, 2]]
    return [[(place + shift) % regions for place in range(regions)] for shift in range(1, regions)]


def turned_rows(array):
    rows = array.shape[0]
    odd = lax.broadcasted_iota(jnp.int32, array.shape, 0) & 1
    return jnp.where(odd == 0, -pltpu.roll(array, rows - 1, 0), pltpu.roll(array, 1, 0))


def row_scale(omega_ref, rows):
    shape = (rows, omega_ref.shape[1])
    same = lax.broadcasted_iota(jnp.int32, shape, 0) >> 1 == lax.broadcasted_iota(jnp.int32, shape, 1)
    return jnp.sum(jnp.where(same, omega_ref[...], 0.0), axis=1, keepdims=True)


def lanes(blocks):
    return jnp.concatenate(blocks, axis=1)


def pair_dot(held_ref, positions, slabs):
    return lax.dot_general(
        lanes([held_ref[position] for position in positions]), lanes(slabs), NT, preferred_element_type=jnp.float32
    )


def region_terms(regions, move, table_ref, held_ref, p_ref, l_ref, row):
    region = back(regions, move)
    slots = range(p_ref.shape[2])
    return tuple(
        pair_dot(
            held_ref.at[kind],
            [table_ref[kind, move, row, slot, 0] for slot in slots],
            [slab_ref[row, region, slot] for slot in slots],
        )
        for kind, slab_ref in enumerate((p_ref, l_ref))
    )


def outflow_terms(side, chosen, ends_ref, current_ref, matrix_ref, store):
    block_size = matrix_ref.shape[1]
    row_blocks = ends_ref.shape[1] // block_size
    leaves, enters = ends_ref[0:1, :], ends_ref[1:2, :]
    current = lanes([current_ref[1, block] for block in range(row_blocks)])
    for block in chosen:
        base = ((lax.axis_index("cell") ^ side) * row_blocks + block) * block_size
        panel = lax.broadcasted_iota(jnp.int32, (block_size, ends_ref.shape[1]), 0) + base
        entry = (leaves == panel).astype(jnp.float32) - (enters == panel).astype(jnp.float32)
        entry = entry.astype(jnp.bfloat16)
        matrix_ref[block] = entry
        store(block, lax.dot_general(current, entry, NT, preferred_element_type=jnp.float32))


def outflow_kernel(message_ref, ends_ref, matrix_ref, outflow_ref):
    def store(block, sums):
        outflow_ref[block] = sums

    outflow_terms(0, range(matrix_ref.shape[0]), ends_ref, message_ref, matrix_ref, store)


def first_kernel(
    regions, held_ref, p_ref, l_ref, p_cols_ref, l_cols_ref, omega_ref, resist_ref, ends_ref, part_ref, sums_ref,
    factor_ref, table_ref, potential_ref, flux_ref, early_ref, matrix_ref, own_matrix_ref, outflow_ref, numbers_ref,
):
    row_blocks, rows, block_size = potential_ref.shape
    slots = p_ref.shape[2]
    cell = lax.axis_index("cell")
    shape = table_ref.shape[2:]
    lane = lax.broadcasted_iota(jnp.int32, shape, 2)
    numbers = jnp.zeros(shape, jnp.float32)
    for kind, cols_ref in enumerate((p_cols_ref, l_cols_ref)):
        columns = cols_ref[...].astype(jnp.float32)
        place = lax.broadcasted_iota(jnp.int32, columns.shape, 2)
        for move in range(regions):
            column = jnp.sum(jnp.where(place == back(regions, move), columns, 0.0), axis=2, keepdims=True)
            column = jnp.broadcast_to(column, shape)
            other = jnp.where(column < row_blocks, column + row_blocks, column - row_blocks)
            table_ref[kind, move] = jnp.where(cell == 0, column, other).astype(jnp.int32)
            if kind == 0:
                numbers = jnp.where(lane == move, jnp.where(cell == 0, other, column), numbers)
    numbers_ref[...] = jnp.zeros_like(numbers_ref)
    for row in range(row_blocks):
        numbers_ref[row * slots : (row + 1) * slots, :] = numbers[row]
    early_ref[2 * row_blocks] = numbers_ref[...].astype(jnp.bfloat16)

    def store(block, sums):
        early_ref[row_blocks + block] = sums.astype(jnp.bfloat16)

    def store_own(block, sums):
        outflow_ref[block] = sums

    done = part_ref.shape[0]
    own_matrix_ref[:done] = part_ref[...]
    outflow_ref[:done] = sums_ref[...]
    outflow_terms(0, range(done, row_blocks), ends_ref, held_ref, own_matrix_ref, store_own)
    outflow_terms(1, range(row_blocks), ends_ref, held_ref, matrix_ref, store)
    for row in range(row_blocks):
        potential, flux = region_terms(regions, 0, table_ref, held_ref, p_ref, l_ref, row)
        potential_ref[row], flux_ref[row] = potential, flux
        early_ref[row] = potential.astype(jnp.bfloat16)
    factor_ref[0] = jnp.broadcast_to(row_scale(omega_ref, rows), (rows, block_size))
    for row in range(row_blocks):
        columns = slice(row * block_size, (row + 1) * block_size)
        factor_ref[1 + row] = jnp.broadcast_to(resist_ref[:, columns], (rows, block_size))


def next_kernel(
    regions, move, table_ref, held_ref, p_ref, l_ref, p_in_ref, f_in_ref, matrix_ref, potential_ref, flux_ref
):
    del matrix_ref
    for row in range(potential_ref.shape[0]):
        potential, flux = region_terms(regions, move, table_ref, held_ref, p_ref, l_ref, row)
        potential_ref[row], flux_ref[row] = p_in_ref[row] + potential, f_in_ref[row] + flux


def stack_kernel(charge_ref, current_ref, out_ref):
    out_ref[0] = charge_ref[...]
    out_ref[1] = current_ref[...]


def send_kernel(regions, p_ref, after_ref, out_ref):
    del after_ref
    half = out_ref.shape[1]
    for move in range(1, regions):
        for row in range(half):
            out_ref[move - 1, row] = p_ref[lax.axis_index("col") * half + row, back(regions, move)]


def join_kernel(own_ref, other_ref, out_ref):
    blocks = own_ref.shape[1]
    for kind in range(own_ref.shape[0]):
        out_ref[kind, :blocks] = own_ref[kind]
        out_ref[kind, blocks:] = other_ref[kind]


def store_rows(out_ref, columns, array):
    for freq in range(out_ref.shape[0]):
        out_ref[freq, :, columns] = array[2 * freq : 2 * freq + 2]


def other_drop(part, slab_ref, numbers_ref, early_ref, piece_refs, matrix_ref):
    half, slots = slab_ref.shape[1:3]
    start = (lax.axis_index("col") ^ part) * half
    rows = []
    for position in range(half):
        row = start + position
        blocks, slabs = [], []
        for at, piece_ref in enumerate(piece_refs):
            for slot in range(slots):
                blocks.append(piece_ref[0, numbers_ref[row * slots + slot, at + 1]])
                slabs.append(slab_ref[at, position, slot])
        total = lax.dot_general(lanes(blocks), lanes(slabs), NT, preferred_element_type=jnp.float32)
        rows.append((early_ref[row].astype(jnp.float32) + total).astype(jnp.bfloat16))
    matrix = matrix_ref[pl.ds(start, half)].reshape(half * matrix_ref.shape[1], -1)
    return lax.dot_general(lanes(rows), matrix, NN, preferred_element_type=jnp.float32)


def main_kernel(regions, *refs):
    piece_refs = refs[: regions - 1]
    (mine_ref, table_ref, p_ref, l_ref, p_in_ref, f_in_ref, early_ref, matrix_ref, other_matrix_ref, held_ref,
     factor_ref, out_ref, numbers_ref) = refs[regions - 1 :]
    row_blocks, _, block_size = p_in_ref.shape
    numbers_ref[...] = early_ref[2 * row_blocks].astype(jnp.float32).astype(jnp.int32)
    potentials, fluxes = [], []
    for row in range(row_blocks):
        potential, flux = region_terms(regions, regions - 1, table_ref, piece_refs[-1], p_ref, l_ref, row)
        potentials.append((p_in_ref[row] + potential).astype(jnp.bfloat16))
        fluxes.append(f_in_ref[row] + flux)
    drop = other_drop(0, mine_ref, numbers_ref, early_ref, piece_refs, other_matrix_ref)
    matrix = matrix_ref[...].reshape(row_blocks * block_size, -1)
    drop += lax.dot_general(lanes(potentials), matrix, NN, preferred_element_type=jnp.float32)
    for row in range(row_blocks):
        columns = slice(row * block_size, (row + 1) * block_size)
        current = held_ref[1, row].astype(jnp.float32)
        flux = factor_ref[0] * turned_rows(fluxes[row])
        out_ref[:, columns] = factor_ref[1 + row] * current + flux + drop[:, columns]


def last_kernel(regions, *refs):
    piece_refs = refs[: regions - 1]
    (theirs_ref, numbers_ref, begun_ref, early_ref, matrix_ref, held_ref, outflow_ref, factor_ref,
     cell_ref, panel_ref) = refs[regions - 1 :]
    row_blocks, _, block_size = outflow_ref.shape
    total = begun_ref[...] + other_drop(1, theirs_ref, numbers_ref, early_ref, piece_refs, matrix_ref)
    for row in range(row_blocks):
        columns = slice(row * block_size, (row + 1) * block_size)
        store_rows(cell_ref, columns, total[:, columns])
        outflow = outflow_ref[row] + early_ref[row_blocks + row].astype(jnp.float32)
        charge = factor_ref[0] * turned_rows(held_ref[0, row].astype(jnp.float32))
        store_rows(panel_ref, columns, outflow + charge)


def kernel_call(body, out_shape, memories, weight, scratch=()):
    many = isinstance(out_shape, tuple)
    return pl.pallas_call(
        body,
        out_shape=out_shape,
        in_specs=[{"v": VMEM, "a": ANY}[m] for m in memories],
        out_specs=tuple(VMEM for _ in out_shape) if many else VMEM,
        scratch_shapes=scratch,
        compiler_params=pltpu.CompilerParams(vmem_limit_bytes=16 * 1024 * 1024),
        cost_estimate=pl.CostEstimate(flops=weight * 1000, bytes_accessed=4_000_000, transcendentals=0),
    )


def paired_step(p_blocks, p_cols, l_blocks, l_cols, charges, currents, omegas, resist, branch_ends):
    freq_count, _, share = charges.shape
    block_size = p_blocks.shape[-1]
    row_blocks = p_blocks.shape[0]
    rows = 2 * freq_count
    regions = lax.axis_size("blk")

    def blocked(array):
        return array.reshape(rows, row_blocks, block_size).transpose(1, 0, 2)

    message = kernel_call(
        stack_kernel, jax.ShapeDtypeStruct((2, row_blocks, rows, block_size), jnp.bfloat16), "vv", STACK
    )(blocked(charges), blocked(currents))
    held = kernel_call(
        join_kernel, jax.ShapeDtypeStruct((2, 2 * row_blocks, rows, block_size), jnp.bfloat16), "vv", JOIN
    )(message, swapped(message, "cell", 1))

    totals = jax.ShapeDtypeStruct((row_blocks, rows, block_size), jnp.float32)
    matrix_shape = jax.ShapeDtypeStruct((row_blocks, block_size, share), jnp.bfloat16)
    done = row_blocks - 1
    part, sums = kernel_call(
        outflow_kernel,
        (
            jax.ShapeDtypeStruct((done, block_size, share), jnp.bfloat16),
            jax.ShapeDtypeStruct((done, rows, block_size), jnp.float32),
        ),
        "vv",
        SMALL,
    )(message, branch_ends)
    half_shape = jax.ShapeDtypeStruct((regions - 1, row_blocks // 2) + p_blocks.shape[2:], jnp.bfloat16)
    sent = kernel_call(functools.partial(send_kernel, regions), half_shape, "va", SMALL)(p_blocks, sums)
    mine = swapped(sent, "cell", 1)
    theirs = swapped(mine, "col", 1)

    pieces = [lax.ppermute(held, "blk", list(enumerate(targets))) for targets in region_moves(regions)]

    slots = p_cols.shape[2]
    factors, table, potential, flux, early, other_matrix, matrix, outflow = kernel_call(
        functools.partial(first_kernel, regions),
        (
            jax.ShapeDtypeStruct((1 + row_blocks, rows, block_size), jnp.float32),
            jax.ShapeDtypeStruct((2, regions, row_blocks, slots, block_size), jnp.int32),
            totals,
            totals,
            jax.ShapeDtypeStruct((2 * row_blocks + 1, rows, block_size), jnp.bfloat16),
            matrix_shape,
            matrix_shape,
            totals,
        ),
        "vvvvvvvvvv",
        SMALL,
        [pltpu.VMEM((rows, block_size), jnp.float32)],
    )(
        held, p_blocks, l_blocks, p_cols.transpose(0, 2, 1), l_cols.transpose(0, 2, 1), omegas[None], resist[None],
        branch_ends, part, sums,
    )
    early = swapped(early, "cell", 1)
    for move, piece in enumerate(pieces[:-1], 1):
        potential, flux = kernel_call(
            functools.partial(next_kernel, regions, move), (totals, totals), "vvvvvvv", NEXT
        )(table, piece, p_blocks, l_blocks, potential, flux, matrix)

    numbers_shape = jax.ShapeDtypeStruct((rows, block_size), jnp.int32)
    begun, numbers = kernel_call(
        functools.partial(main_kernel, regions),
        (jax.ShapeDtypeStruct((rows, share), jnp.float32), numbers_shape),
        "v" * (10 + regions),
        MAIN,
    )(*pieces, mine, table, p_blocks, l_blocks, potential, flux, early, matrix, other_matrix, held, factors)
    result = jax.ShapeDtypeStruct(charges.shape, jnp.float32)
    return kernel_call(
        functools.partial(last_kernel, regions), (result, result), "v" * (7 + regions), LAST
    )(*pieces, theirs, numbers, begun, early, other_matrix, held, outflow, factors)


def per_device(*args):
    row_blocks, regions = args[0].shape[:2]
    paired = lax.axis_size("cell") == 2 and lax.axis_size("col") == 2
    paired = paired and row_blocks % 2 == 0 and row_blocks * args[0].shape[2] <= 2 * args[4].shape[0]
    return (paired_step if paired else general_step)(*args)


def solution(mesh):
    placed = (
        P(("job", "blk", "cell"), None, None, None, None),
        P(("job", "blk", "cell"), None, None),
        P(("job", "blk", "cell"), None, None, None, None),
        P(("job", "blk", "cell"), None, None),
        P("col", None, ("job", "blk", "cell")),
        P("col", None, ("job", "blk", "cell")),
        P("col"),
        P(("job", "blk", "cell")),
        P(None, ("job", "blk", "cell")),
    )
    return jax.shard_map(
        per_device,
        mesh=mesh,
        in_specs=placed,
        out_specs=(P("col", None, ("job", "blk", "cell")), P("col", None, ("job", "blk", "cell"))),
        check_vma=False,
    )
```
